128 devices in a mesh: rep: 4 (over z), fsdp: 8 (over x_lo, y), ctx: 4 (over x_hi, core).
Axes of the slice: x: 4 (x_hi: 2, x_lo: 2; x = x_hi * 2 + x_lo), y: 4, z: 4, core: 2. Of those that a mesh axis runs over, the one named last changes fastest.
Arguments:
- tokens: bfloat16 [32, 1024, 960], P(('rep', 'fsdp'), 'ctx'), may hold values from -6 to 6
- cotangent: bfloat16 [32, 1024, 960], P(('rep', 'fsdp'), 'ctx'), may hold values from -6 to 6
- query_weight: bfloat16 [960, 960], P('fsdp'), may hold values from -0.375 to 0.375
- keyval_weight: bfloat16 [2, 960, 320], P(None, 'fsdp'), may hold values from -0.1875 to 0.1875
- output_weight: bfloat16 [960, 960], P('fsdp'), may hold values from -0.5 to 0.5
- gateup_weight: bfloat16 [2, 960, 2560], P(None, 'fsdp'), may hold values from -0.1875 to 0.1875
- down_weight: bfloat16 [2560, 960], P('fsdp'), may hold values from -0.125 to 0.125
- norm_gains: bfloat16 [2, 960], P(None, 'fsdp'), may hold values from 0.5 to 1.5
- query_first: bfloat16 [960, 960], P('fsdp'), may hold values from -128 to 128
- keyval_first: bfloat16 [2, 960, 320], P(None, 'fsdp'), may hold values from -128 to 128
- output_first: bfloat16 [960, 960], P('fsdp'), may hold values from -48 to 48
- gateup_first: bfloat16 [2, 960, 2560], P(None, 'fsdp'), may hold values from -40 to 40
- down_first: bfloat16 [2560, 960], P('fsdp'), may hold values from -64 to 64
- gains_first: bfloat16 [2, 960], P(None, 'fsdp'), may hold values from -192 to 192
- query_second: bfloat16 [960, 960], P('fsdp'), may hold values from 1736 to 6880
- keyval_second: bfloat16 [2, 960, 320], P(None, 'fsdp'), may hold values from 1736 to 6880
- output_second: bfloat16 [960, 960], P('fsdp'), may hold values from 278 to 1112
- gateup_second: bfloat16 [2, 960, 2560], P(None, 'fsdp'), may hold values from 212 to 848
- down_second: bfloat16 [2560, 960], P('fsdp'), may hold values from 620 to 2480
- gains_second: bfloat16 [2, 960], P(None, 'fsdp'), may hold values from 3920 to 15680
Outputs:
- outputs: bfloat16 [32, 1024, 960], P(('rep', 'fsdp'), 'ctx')
- input_grad: float32 [32, 1024, 960], P(('rep', 'fsdp'), 'ctx')
- query_new: float32 [960, 960], P('fsdp')
- keyval_new: float32 [2, 960, 320], P(None, 'fsdp')
- output_new: float32 [960, 960], P('fsdp')
- gateup_new: float32 [2, 960, 2560], P(None, 'fsdp')
- down_new: float32 [2560, 960], P('fsdp')
- gains_new: float32 [2, 960], P(None, 'fsdp')
- query_first_new: float32 [960, 960], P('fsdp')
- keyval_first_new: float32 [2, 960, 320], P(None, 'fsdp')
- output_first_new: float32 [960, 960], P('fsdp')
- gateup_first_new: float32 [2, 960, 2560], P(None, 'fsdp')
- down_first_new: float32 [2560, 960], P('fsdp')
- gains_first_new: float32 [2, 960], P(None, 'fsdp')
- query_second_new: float32 [960, 960], P('fsdp')
- keyval_second_new: float32 [2, 960, 320], P(None, 'fsdp')
- output_second_new: float32 [960, 960], P('fsdp')
- gateup_second_new: float32 [2, 960, 2560], P(None, 'fsdp')
- down_second_new: float32 [2560, 960], P('fsdp')
- gains_second_new: float32 [2, 960], P(None, 'fsdp')
The draws below stay inside these ranges and needn't reach their ends.
All inputs are finite; a program needn't handle non-finite values.
Results may differ from the reference program's by a relative error of at most 0.035.
Values may be sent and summed in bfloat16 or wider, within the bound.
A program may use at most 192 MiB of HBM per device.

```python
import math
import jax
import jax.numpy as jnp
from jax import lax

D = 960
FF = 2560
QUERY_HEADS = 15
KEY_VALUE_HEADS = 5
HEAD_WIDTH = 64
TOK_DEV = 256
STEP = 10
QW = 960
KW = 320
SEQ = 1024
SEQS = 32
DEVICES = 128


def block_scale(key, extent, cuts, least, high):
    factor_of = 1.0
    for dim, parts in cuts:
        steps = jax.random.uniform(jax.random.fold_in(jax.random.fold_in(key, 6), dim), (parts,), jnp.float32, least / len(cuts), high / len(cuts))
        factor_of = factor_of * jnp.repeat(jnp.exp(steps), extent[dim] // parts).reshape((-1,) + (1,) * (len(extent) - 1 - dim))
    return factor_of


def gaussian(rng, extent, scale, limit, shards=(), kind=jnp.bfloat16):
    result = jax.random.normal(rng, extent, jnp.float32) * scale
    if len(shards) > 0:
        result = block_scale(rng, extent, shards, -0.22, 0.18) * result
    return jnp.clip(result, min=-limit, max=limit).astype(kind)


def setup_inputs(seed: int = 0) -> dict:
    seeds = jax.random.split(jax.random.key(seed), 21)
    tokens = gaussian(seeds[0], (SEQS, SEQ, D), 1.0, 6.0, ((0, 32), (1, 4)))
    cotangent = gaussian(seeds[1], (SEQS, SEQ, D), 1.0, 6.0, ((0, 32), (1, 4)))
    query_weight = gaussian(seeds[2], (D, QW), (D // 4) ** -0.5, 0.375, ((0, 8),))
    keyval_weight = gaussian(seeds[3], (2, D, KW), D ** -0.5, 0.1875, ((1, 8),))
    output_weight = gaussian(seeds[4], (QW, D), (QW // 8) ** -0.5, 0.5, ((0, 8),))
    gateup_weight = gaussian(seeds[5], (2, D, FF), D ** -0.5, 0.1875, ((1, 8),))
    down_weight = gaussian(seeds[6], (FF, D), FF ** -0.5, 0.125, ((0, 8),))
    norm_gains = jnp.clip(1.0 + 0.1 * jax.random.normal(seeds[7], (2, D), jnp.float32), 0.5, 1.5).astype(jnp.bfloat16)
    query_first = gaussian(seeds[8], (D, QW), (0.11 * (DEVICES * TOK_DEV) ** 0.5), 128.0, ((0, 8),))
    keyval_first = gaussian(seeds[9], (2, D, KW), (0.11 * (DEVICES * TOK_DEV) ** 0.5), 128.0, ((1, 8),))
    output_first = gaussian(seeds[10], (QW, D), (0.044 * (DEVICES * TOK_DEV) ** 0.5), 48.0, ((0, 8),))
    gateup_first = gaussian(seeds[11], (2, D, FF), (0.0385 * (DEVICES * TOK_DEV) ** 0.5), 40.0, ((1, 8),))
    down_first = gaussian(seeds[12], (FF, D), (0.066 * (DEVICES * TOK_DEV) ** 0.5), 64.0, ((0, 8),))
    gains_first = gaussian(seeds[13], (2, D), (0.165 * (DEVICES * TOK_DEV) ** 0.5), 192.0, ((1, 8),))
    query_second = jnp.clip(jnp.exp(math.log(6880.0) - 1.377035 * jax.random.uniform(seeds[14], (D, QW), jnp.float32) ** block_scale(seeds[14], (D, QW), ((0, 8),), -0.2, 0.2)), 1736.0, 6880.0).astype(jnp.bfloat16)
    keyval_second = jnp.clip(jnp.exp(math.log(6880.0) - 1.377035 * jax.random.uniform(seeds[15], (2, D, KW), jnp.float32) ** block_scale(seeds[15], (2, D, KW), ((1, 8),), -0.2, 0.2)), 1736.0, 6880.0).astype(jnp.bfloat16)
    output_second = jnp.clip(jnp.exp(math.log(1112.0) - 1.3862944 * jax.random.uniform(seeds[16], (QW, D), jnp.float32) ** block_scale(seeds[16], (QW, D), ((0, 8),), -0.2, 0.2)), 278.0, 1112.0).astype(jnp.bfloat16)
    gateup_second = jnp.clip(jnp.exp(math.log(848.0) - 1.3862944 * jax.random.uniform(seeds[17], (2, D, FF), jnp.float32) ** block_scale(seeds[17], (2, D, FF), ((1, 8),), -0.2, 0.2)), 212.0, 848.0).astype(jnp.bfloat16)
    down_second = jnp.clip(jnp.exp(math.log(2480.0) - 1.3862944 * jax.random.uniform(seeds[18], (FF, D), jnp.float32) ** block_scale(seeds[18], (FF, D), ((0, 8),), -0.2, 0.2)), 620.0, 2480.0).astype(jnp.bfloat16)
    gains_second = jnp.clip(jnp.exp(math.log(15680.0) - 1.3862944 * jax.random.uniform(seeds[19], (2, D), jnp.float32) ** block_scale(seeds[19], (2, D), ((1, 8),), -0.2, 0.2)), 3920.0, 15680.0).astype(jnp.bfloat16)
    return dict(tokens=tokens, cotangent=cotangent, query_weight=query_weight, keyval_weight=keyval_weight, output_weight=output_weight, gateup_weight=gateup_weight, down_weight=down_weight, norm_gains=norm_gains, query_first=query_first, keyval_first=keyval_first, output_first=output_first, gateup_first=gateup_first, down_first=down_first, gains_first=gains_first, query_second=query_second, keyval_second=keyval_second, output_second=output_second, gateup_second=gateup_second, down_second=down_second, gains_second=gains_second)


@jax.custom_vjp
def lower_precision(v):
    return lax.optimization_barrier(v.astype(jnp.bfloat16)).astype(jnp.float32)

@jax.custom_vjp
def low_back(v):
    return v

def low_keep(v):
    return (lower_precision(v), None)

def low_pass(kept, grad):
    return (grad,)

def back_keep(v):
    return (v, None)

def back_low(kept, grad):
    return (lower_precision(grad),)
lower_precision.defvjp(low_keep, low_pass)
low_back.defvjp(back_keep, back_low)
highest = lax.Precision.HIGHEST
norm_epsilon = 1e-05
rotary_base = 100000.0
beta_first = 0.9
beta_second = 0.95
adam_epsilon = 1e-08
matrix_rate = 0.06
matrix_decay = 0.1
gain_rate = 0.6

def product(left, right):
    return jnp.dot(left, right, precision=highest, preferred_element_type=jnp.float32)

def rms_norm(stream, gain_row):
    scale = lax.rsqrt(lax.optimization_barrier(jnp.mean(stream * stream, axis=-1, keepdims=True)) + norm_epsilon)
    return stream * scale * gain_row

def rotary_tables(positions, width):
    counter = jnp.arange(width // 2, dtype=jnp.float32)
    frequency = 1.0 / rotary_base ** (counter * (2.0 / width))
    angles = positions[:, None] * frequency[None, :]
    return (jnp.cos(angles), jnp.sin(angles))

def apply_rotary(field, cosine_table, sine_table):
    half_width = field.shape[-1] // 2
    former = field[..., :half_width]
    latter = field[..., half_width:]
    cos_rows = cosine_table[:, None, :]
    sin_rows = sine_table[:, None, :]
    return jnp.concatenate([former * cos_rows - latter * sin_rows, latter * cos_rows + former * sin_rows], axis=-1)

def sequence_forward(weights, stream):
    query_weight, keyval_weight, output_weight, gateup_weight, down_weight, norm_gains = weights
    sequence_length = stream.shape[0]
    heads_per_group = QUERY_HEADS // KEY_VALUE_HEADS
    positions = jnp.arange(sequence_length, dtype=jnp.float32)
    cosine_table, sine_table = rotary_tables(positions, HEAD_WIDTH)
    normed_one = lower_precision(rms_norm(stream, norm_gains[0]))
    query_linear = low_back(product(normed_one, query_weight))
    key_linear = low_back(product(normed_one, keyval_weight[0]))
    values_lower = low_back(lower_precision(product(normed_one, keyval_weight[1])))
    query_rotated = lower_precision(apply_rotary(query_linear.reshape(sequence_length, QUERY_HEADS, HEAD_WIDTH), cosine_table, sine_table)).reshape(sequence_length, KEY_VALUE_HEADS, heads_per_group, HEAD_WIDTH)
    key_rotated = lower_precision(apply_rotary(key_linear.reshape(sequence_length, KEY_VALUE_HEADS, HEAD_WIDTH), cosine_table, sine_table))
    value_head_rows = values_lower.reshape(sequence_length, KEY_VALUE_HEADS, HEAD_WIDTH)
    scores = low_back(jnp.einsum('qhgd,khd->hgqk', query_rotated, key_rotated, precision=highest) * HEAD_WIDTH ** (-0.5))
    ordinal = jnp.arange(sequence_length)
    allowed = ordinal[None, :] <= ordinal[:, None]
    probs = jax.nn.softmax(jnp.where(allowed, scores, -1e+30), axis=-1)
    attended = jnp.einsum('hgqk,khd->qhgd', lower_precision(probs), value_head_rows, precision=highest)
    attended = low_back(lower_precision(attended.reshape(sequence_length, QUERY_HEADS * HEAD_WIDTH)))
    middle = stream + low_back(product(attended, output_weight))
    normed_two = lower_precision(rms_norm(middle, norm_gains[1]))
    gate = low_back(product(normed_two, gateup_weight[0]))
    upward = low_back(product(normed_two, gateup_weight[1]))
    hidden = lower_precision(jax.nn.silu(gate) * upward)
    return middle + product(hidden, down_weight)

def forward(weights, stream):
    checked = jax.checkpoint(lambda sequence: sequence_forward(weights, sequence))
    return lax.map(checked, stream)

def adamw_update(weight, gradient, first, second, rate, decay):
    weight = weight.astype(jnp.float32)
    first_new = beta_first * first.astype(jnp.float32) + (1.0 - beta_first) * gradient
    second_new = beta_second * second.astype(jnp.float32) + (1.0 - beta_second) * gradient * gradient
    first_hat = first_new / (1.0 - beta_first ** STEP)
    second_hat = second_new / (1.0 - beta_second ** STEP)
    weight_new = weight - rate * (first_hat / (jnp.sqrt(second_hat) + adam_epsilon) + decay * weight)
    return (weight_new, first_new, second_new)

def reference(tokens, cotangent, query_weight, keyval_weight, output_weight, gateup_weight, down_weight, norm_gains, query_first, keyval_first, output_first, gateup_first, down_first, gains_first, query_second, keyval_second, output_second, gateup_second, down_second, gains_second):
    initials = (query_weight, keyval_weight, output_weight, gateup_weight, down_weight, norm_gains)
    weights = tuple((weight.astype(jnp.float32) for weight in initials))
    stream = tokens.astype(jnp.float32)
    incoming = cotangent.astype(jnp.float32)
    outputs, pullback = jax.vjp(forward, weights, stream)
    weight_grads, input_grad = pullback(incoming)
    firsts = (query_first, keyval_first, output_first, gateup_first, down_first, gains_first)
    seconds = (query_second, keyval_second, output_second, gateup_second, down_second, gains_second)
    rates = (matrix_rate, matrix_rate, matrix_rate, matrix_rate, matrix_rate, gain_rate)
    decays = (matrix_decay, matrix_decay, matrix_decay, matrix_decay, matrix_decay, 0.0)
    updated = [adamw_update(weights[slot], weight_grads[slot], firsts[slot], seconds[slot], rates[slot], decays[slot]) for slot in range(6)]
    return (outputs.astype(jnp.bfloat16), input_grad, updated[0][0], updated[1][0], updated[2][0], updated[3][0], updated[4][0], updated[5][0], updated[0][1], updated[1][1], updated[2][1], updated[3][1], updated[4][1], updated[5][1], updated[0][2], updated[1][2], updated[2][2], updated[3][2], updated[4][2], updated[5][2])
```

```python
import functools

import jax
import jax.numpy as jnp
from jax import lax
from jax.experimental import pallas as pl
from jax.experimental.pallas import tpu as pltpu
from jax.sharding import PartitionSpec as P

QUERY_HEADS = 15
KEY_VALUE_HEADS = 5
GROUP = QUERY_HEADS // KEY_VALUE_HEADS
HEAD_WIDTH = 64
HALF = HEAD_WIDTH // 2
STEP = 10
TOK = 256
D = 960
KW = 320
FF = 2560
FH = FF // 2
ROWS = 120
PAD = 128
BF = jnp.bfloat16
F32 = jnp.float32
MESH = pl.DeviceIdType.MESH

norm_epsilon = 1e-05
rotary_base = 100000.0
beta_first = 0.9
beta_second = 0.95
adam_epsilon = 1e-08
matrix_rate = 0.06
matrix_decay = 0.1
gain_rate = 0.6
score_scale = HEAD_WIDTH ** (-0.5)

ANY = pl.BlockSpec(memory_space=pl.ANY)
VM = pl.BlockSpec(memory_space=pltpu.VMEM)


def place():
    f = lax.axis_index("fsdp")
    q = lax.axis_index("ctx")
    z = lax.axis_index("rep")
    return (q // 2) * 2 + f // 4, f % 4, z, q % 2


def at(x, y, z, core):
    x, y, z = lax.rem(x, 4), lax.rem(y, 4), lax.rem(z, 4)
    return {"rep": z, "fsdp": lax.rem(x, 2) * 4 + y, "ctx": (x // 2) * 2 + core}


def greet(devices):
    barrier = pltpu.get_barrier_semaphore()
    for device in devices:
        pl.semaphore_signal(barrier, inc=1, device_id=device, device_id_type=MESH)
    pl.semaphore_wait(barrier, len(devices))


def remote(src, dst, send, recv, device):
    return pltpu.make_async_remote_copy(
        src_ref=src, dst_ref=dst, send_sem=send, recv_sem=recv, device_id=device, device_id_type=MESH
    )


def params(number, vmem=56):
    return pltpu.CompilerParams(
        collective_id=number, has_side_effects=True, vmem_limit_bytes=vmem * 2**20
    )


def gather_kernel(
    qo, kv, gu, dn, dy, qo_all, kv_all, gu_all, dn_all, dy_all, send_y, send_x, send_s, recv, recv_s, local
):
    x, y, z, c = place()
    xl = lax.rem(x, 2)
    f = 4 * xl + y
    sibling = at(x, y, z, 1 - c)
    lanes = pl.ds(pl.multiple_of(c * FH, 128), FH)
    greet([at(x, y + j, z, c) for j in (1, 2, 3)] + [at(x + j, y, z, c) for j in (1, 3)] + [sibling])
    holds = c == xl

    own = (qo.at[c], kv.at[c], gu.at[:, :, lanes], dn)

    def slot(item, g):
        if item == 0:
            return qo_all.at[c, g]
        if item == 1:
            return kv_all.at[c, g]
        if item == 2:
            return gu_all.at[:, g]
        return dn_all.at[lax.rem(g, 4)]

    def wait_slot(item, g):
        remote(slot(item, g), slot(item, g), send_s.at[0, 0], recv.at[item, g], sibling).wait_recv()

    def send_row(item, j):
        return remote(own[item], slot(item, f), send_y.at[item, j - 1], recv.at[item, f], at(x, y + j, z, c))

    def send_side(item, j):
        g = 4 * xl + lax.rem(y + j, 4)
        step = 3 if item == 2 else 1
        return remote(
            own[item] if j == 0 else slot(item, g),
            slot(item, g),
            send_x.at[item, j],
            recv.at[item, g],
            at(x + step, y, z, c),
        )

    def send_sib(item, k):
        g = 4 * xl + lax.rem(y + k + 1, 4) if k < 3 else 4 * (1 - xl) + lax.rem(y + k - 3, 4)
        return remote(slot(item, g), slot(item, g), send_s.at[item, k], recv_s.at[item, g], sibling)

    def other(k):
        return 4 * (1 - xl) + lax.rem(y + k, 4)

    order = (1, 3, 2)
    for item in (0, 1):
        for j in order:
            send_row(item, j).start()
        send_side(item, 0).start()
    exchange = remote(dy, dy_all.at[1], send_s.at[2, 0], recv_s.at[2, 0], sibling)
    exchange.start()
    for item in (2, 3):

        def begin(item=item):
            for j in order:
                send_row(item, j).start()
            send_side(item, 0).start()

        if item == 3:
            pl.when(holds)(begin)
        else:
            begin()
    copies = [
        pltpu.make_async_copy(qo, qo_all.at[:, f], local.at[0]),
        pltpu.make_async_copy(kv, kv_all.at[:, f], local.at[1]),
        pltpu.make_async_copy(own[2], gu_all.at[:, f], local.at[2]),
        pltpu.make_async_copy(dy, dy_all.at[0], local.at[4]),
    ]
    for copy in copies:
        copy.start()
    own_down = pltpu.make_async_copy(dn, dn_all.at[y], local.at[3])
    pl.when(holds)(own_down.start)

    for j in order:
        g = 4 * xl + lax.rem(y + j, 4)
        for item in (0, 1):
            wait_slot(item, g)
            send_side(item, j).start()
            send_sib(item, j - 1).start()
    for k in (0, 1, 3, 2):
        for item in (0, 1):
            wait_slot(item, other(k))
            send_sib(item, k + 3).start()
    for j in order:
        g = 4 * xl + lax.rem(y + j, 4)
        wait_slot(2, g)
        send_side(2, j).start()

        @pl.when(holds)
        def _():
            wait_slot(3, g)
            send_side(3, j).start()

    for k in (0, 1, 3, 2):
        wait_slot(2, other(k))
        pl.when(jnp.logical_not(holds))(functools.partial(wait_slot, 3, other(k)))

    for copy in copies:
        copy.wait()
    exchange.wait()
    for item in (0, 1):
        for k in range(7):
            g = 4 * xl + lax.rem(y + k + 1, 4) if k < 3 else other(k - 3)
            arriving = (qo_all, kv_all)[item].at[1 - c, g]
            remote(arriving, arriving, send_s.at[0, 0], recv_s.at[item, g], sibling).wait_recv()
            send_sib(item, k).wait_send()
    for item in (0, 1, 2):
        for j in order:
            send_row(item, j).wait_send()
        for j in range(4):
            send_side(item, j).wait_send()

    @pl.when(holds)
    def _():
        own_down.wait()
        for j in order:
            send_row(3, j).wait_send()
        for j in range(4):
            send_side(3, j).wait_send()


def gather_weights(qo, kv, gu, dn, dy):
    sem = pltpu.SemaphoreType.DMA
    return pl.pallas_call(
        gather_kernel,
        name="gather_weights",
        out_shape=(
            jax.ShapeDtypeStruct((2, 8, ROWS, D), BF),
            jax.ShapeDtypeStruct((2, 8, ROWS, KW), BF),
            jax.ShapeDtypeStruct((2, 8, ROWS, FH), BF),
            jax.ShapeDtypeStruct((4, KW, D), BF),
            jax.ShapeDtypeStruct((2, TOK, D), BF),
        ),
        in_specs=[ANY] * 5,
        out_specs=(ANY,) * 5,
        scratch_shapes=[sem((4, 3)), sem((4, 4)), sem((3, 7)), sem((4, 8)), sem((3, 8)), sem((5,))],
        compiler_params=params(0),
    )(qo, kv, gu, dn, dy)


def swap_kernel(count, *refs):
    ins, outs = refs[:count], refs[count : 2 * count]
    send, recv = refs[2 * count :]
    x, y, z, c = place()
    sibling = at(x, y, z, 1 - c)
    greet([sibling])
    copies = [
        remote(ins[i], outs[i], send.at[i], recv.at[i], sibling) for i in range(count)
    ]
    for copy in copies:
        copy.start()
    for copy in copies:
        copy.wait()


def swap(number, *arrays):
    count = len(arrays)
    return pl.pallas_call(
        functools.partial(swap_kernel, count),
        name="swap_%d" % number,
        out_shape=tuple(jax.ShapeDtypeStruct(a.shape, a.dtype) for a in arrays),
        in_specs=[ANY] * count,
        out_specs=(ANY,) * count,
        scratch_shapes=[pltpu.SemaphoreType.DMA((count,)), pltpu.SemaphoreType.DMA((count,))],
        compiler_params=params(number),
    )(*arrays)


def dot(a, b, ca, cb):
    return lax.dot_general(a, b, (((ca,), (cb,)), ((), ())), preferred_element_type=F32)


def attend_kernel(q, kv, cos, sin, q_low, att, lse, kv_out, keys, send, recv):
    x, y, z, c = place()
    me = 2 * (x // 2) + c
    sib_slot, far_slot, diag_slot = me + 1 - 2 * c, lax.rem(me + 2, 4), lax.rem(me + 2, 4) + 1 - 2 * c
    sibling, far = at(x, y, z, 1 - c), at(x + 2, y, z, c)
    greet([sibling, far])
    co, si = cos[...], sin[...]
    for h in range(KEY_VALUE_HEADS):
        a, b = kv[64 * h : 64 * h + 32, :], kv[64 * h + 32 : 64 * h + 64, :]
        keys[me, 64 * h : 64 * h + 32, :] = (a * co - b * si).astype(BF)
        keys[me, 64 * h + 32 : 64 * h + 64, :] = (b * co + a * si).astype(BF)
    keys[me, KW:, :] = kv[KW:, :].astype(BF)
    to_far = remote(keys.at[me], keys.at[me], send.at[0], recv.at[0], far)
    to_sib = remote(keys.at[me], keys.at[me], send.at[1], recv.at[1], sibling)
    to_far.start()
    to_sib.start()
    for h in range(QUERY_HEADS):
        a, b = q[64 * h : 64 * h + 32, :], q[64 * h + 32 : 64 * h + 64, :]
        q_low[64 * h : 64 * h + 32, :] = ((a * co - b * si).astype(BF) * score_scale).astype(BF)
        q_low[64 * h + 32 : 64 * h + 64, :] = ((b * co + a * si).astype(BF) * score_scale).astype(BF)
    remote(keys.at[far_slot], keys.at[far_slot], send.at[0], recv.at[0], far).wait_recv()
    on = remote(keys.at[far_slot], keys.at[far_slot], send.at[2], recv.at[2], sibling)
    on.start()
    remote(keys.at[sib_slot], keys.at[sib_slot], send.at[1], recv.at[1], sibling).wait_recv()
    remote(keys.at[diag_slot], keys.at[diag_slot], send.at[2], recv.at[2], sibling).wait_recv()
    gap = lax.broadcasted_iota(jnp.int32, (TOK, TOK), 0) - lax.broadcasted_iota(jnp.int32, (TOK, TOK), 1)

    def head(h, carry):
        rows = pl.ds(pl.multiple_of(h * 64, 64), 64)
        g = h // GROUP
        krows = pl.ds(pl.multiple_of(g * 64, 64), 64)
        vrows = pl.ds(pl.multiple_of(KW + g * 64, 64), 64)
        qh = q_low[rows, :]
        s = []
        for j in range(4):
            part = dot(keys[j, krows, :], qh, 0, 0)
            s.append(jnp.where(gap <= 256 * (me - j), part, -1e30))
        top = jnp.max(jnp.maximum(jnp.maximum(s[0], s[1]), jnp.maximum(s[2], s[3])), axis=0, keepdims=True)
        e = [jnp.exp(part - top) for part in s]
        total = jnp.sum(e[0] + e[1] + (e[2] + e[3]), axis=0, keepdims=True)
        acc = dot(keys[0, vrows, :], e[0].astype(BF), 1, 0)
        for j in range(1, 4):
            acc += dot(keys[j, vrows, :], e[j].astype(BF), 1, 0)
        att[rows, :] = (acc / total).astype(BF)
        lse[pl.ds(h, 1), 0, :] = top + jnp.log(total)
        return carry

    lax.fori_loop(0, QUERY_HEADS, head, 0)
    kv_out[...] = keys[...]
    to_far.wait_send()
    to_sib.wait_send()
    on.wait_send()


def attend(q, kv, cos, sin):
    sem = pltpu.SemaphoreType.DMA
    return pl.pallas_call(
        attend_kernel,
        name="attend",
        out_shape=(
            jax.ShapeDtypeStruct((D, TOK), BF),
            jax.ShapeDtypeStruct((D, TOK), BF),
            jax.ShapeDtypeStruct((16, 1, TOK), F32),
            jax.ShapeDtypeStruct((4, 2 * KW, TOK), BF),
        ),
        in_specs=[VM] * 4,
        out_specs=(VM,) * 4,
        scratch_shapes=[pltpu.VMEM((4, 2 * KW, TOK), BF), sem((3,)), sem((3,))],
        compiler_params=params(1),
    )(q, kv, cos, sin)


def attend_back_kernel(
    q_low, keys, lse, att, grad, cos, sin, q_back, kv_back, mine, got, far_got, acc, send, recv
):
    x, y, z, c = place()
    me = 2 * (x // 2) + c
    far_slot = lax.rem(me + 2, 4)
    sib_slot = me + 1 - 2 * c
    diag_slot = far_slot + 1 - 2 * c
    sibling, far = at(x, y, z, 1 - c), at(x + 2, y, z, c)
    greet([sibling, far])
    co, si = cos[...], sin[...]
    gap = lax.broadcasted_iota(jnp.int32, (TOK, TOK), 0) - lax.broadcasted_iota(jnp.int32, (TOK, TOK), 1)

    def group(g, carry):
        krows = pl.ds(pl.multiple_of(g * 64, 64), 64)
        vrows = pl.ds(pl.multiple_of(KW + g * 64, 64), 64)

        def head(t, inner):
            h = g * GROUP + t
            rows = pl.ds(pl.multiple_of(h * 64, 64), 64)
            qh, gh = q_low[rows, :], grad[rows, :]
            row_dot = jnp.sum(gh.astype(F32) * att[rows, :].astype(F32), axis=0, keepdims=True)
            level = lse[pl.ds(h, 1), 0, :]
            dq = jnp.zeros((64, TOK), F32)
            for j in range(4):
                s = dot(keys[j, krows, :], qh, 0, 0)
                s = jnp.where(gap <= 256 * (me - j), s, -1e30)
                p = jnp.exp(s - level)
                dp = dot(keys[j, vrows, :], gh, 0, 0)
                ds = (p * (dp - row_dot)).astype(BF)
                pb = p.astype(BF)
                dq += dot(keys[j, krows, :], ds, 1, 0)
                dk = dot(qh, ds, 1, 1)
                dv = dot(gh, pb, 1, 1)
                first = t == 0
                acc[j, 0] = jnp.where(first, dk, acc[j, 0] + dk)
                acc[j, 1] = jnp.where(first, dv, acc[j, 1] + dv)
            dq = dq * score_scale
            a, b = dq[:32], dq[32:]
            q_back[pl.ds(pl.multiple_of(h * 64, 32), 32), :] = (a * co + b * si).astype(BF)
            q_back[pl.ds(pl.multiple_of(h * 64 + 32, 32), 32), :] = (b * co - a * si).astype(BF)
            return inner

        lax.fori_loop(0, GROUP, head, 0)
        for j in range(4):
            mine[j, krows, :] = acc[j, 0].astype(BF)
            mine[j, vrows, :] = acc[j, 1].astype(BF)
        return carry

    acc[...] = jnp.zeros_like(acc)
    lax.fori_loop(0, KEY_VALUE_HEADS, group, 0)
    to_sib_far = remote(mine.at[diag_slot], got.at[1], send.at[0], recv.at[0], sibling)
    to_sib = remote(mine.at[sib_slot], got.at[0], send.at[1], recv.at[1], sibling)
    to_sib_far.start()
    to_sib.start()
    to_sib_far.wait_recv()
    got[1] = (mine[far_slot].astype(F32) + got[1].astype(F32)).astype(BF)
    to_far = remote(got.at[1], far_got, send.at[2], recv.at[2], far)
    to_far.start()
    to_sib.wait_recv()
    near = mine[me].astype(F32) + got[0].astype(F32)
    to_far.wait_recv()
    total = near + far_got[...].astype(F32)
    for h in range(KEY_VALUE_HEADS):
        a, b = total[64 * h : 64 * h + 32, :], total[64 * h + 32 : 64 * h + 64, :]
        kv_back[64 * h : 64 * h + 32, :] = (a * co + b * si).astype(BF)
        kv_back[64 * h + 32 : 64 * h + 64, :] = (b * co - a * si).astype(BF)
    kv_back[KW:, :] = total[KW:, :].astype(BF)
    to_sib_far.wait_send()
    to_sib.wait_send()
    to_far.wait_send()


def attend_back(q_low, keys, lse, att, grad, cos, sin):
    sem = pltpu.SemaphoreType.DMA
    return pl.pallas_call(
        attend_back_kernel,
        name="attend_back",
        out_shape=(
            jax.ShapeDtypeStruct((D, TOK), BF),
            jax.ShapeDtypeStruct((2 * KW, TOK), BF),
        ),
        in_specs=[VM] * 7,
        out_specs=(VM,) * 2,
        scratch_shapes=[
            pltpu.VMEM((4, 2 * KW, TOK), BF),
            pltpu.VMEM((2, 2 * KW, TOK), BF),
            pltpu.VMEM((2 * KW, TOK), BF),
            pltpu.VMEM((4, 2, 64, TOK), F32),
            sem((3,)),
            sem((3,)),
        ],
        compiler_params=params(2),
    )(q_low, keys, lse, att, grad, cos, sin)


def add_up(out, own, got):
    out[...] = (
        own[...].astype(F32) + got[0].astype(F32) + (got[1].astype(F32) + got[2].astype(F32))
    ).astype(BF)


def reduce_kernel(
    a, b, cc, d,
    a_sum, b_sum, c_sum, d_sum,
    a1, a1r, a2, a2r, a3, a3r,
    b1, b1r, b2, b2r, b3, b3r,
    d1, d1r, d2, d2r, d3, d3r,
    c1, c1r, c2, c2r, c3, c3r,
    send1, recv1, send2, recv2, send3, recv3, send4, recv4, send5, recv5, local,
):
    x, y, z, c = place()
    xl = lax.rem(x, 2)
    holds = c == xl
    sibling = at(x, y, z, 1 - c)
    along_x = [at(x + j, y, z, c) for j in (1, 2, 3)]
    along_y = [at(x, y + j, z, c) for j in (1, 2, 3)]
    along_z = [at(x, y, z + j, c) for j in (1, 2, 3)]
    greet(along_x + along_y + along_z + [sibling])
    offsets = (1, 3, 2)
    A, B, C, DN = 0, 1, 2, 3

    def quarter(index):
        index = lax.rem(index, 4)
        return index // 2, pl.ds(pl.multiple_of(640 * lax.rem(index, 2), 128), 640)

    def rows(index, size):
        return pl.ds(pl.multiple_of(lax.rem(index, 4) * size, 16), size)

    def first(item, j):
        to = lax.rem(y + j, 4)
        if item == C:
            m, lanes = quarter(z + j)
            return remote(cc.at[m, :, :, :, lanes], c1r.at[j - 1], send1.at[C, j - 1], recv1.at[C, j - 1], along_z[j - 1])
        src, dst = {
            A: (a.at[:, to], a1r), B: (b.at[:, to], b1r), DN: (d.at[to], d1r)
        }[item]
        return remote(src, dst.at[j - 1], send1.at[item, j - 1], recv1.at[item, j - 1], along_y[j - 1])

    for j in offsets:
        for item in (C, DN, A, B):
            first(item, j).start()
    m, lanes = quarter(z)
    copies = [
        pltpu.make_async_copy(a.at[:, y], a1, local.at[0]),
        pltpu.make_async_copy(b.at[:, y], b1, local.at[1]),
        pltpu.make_async_copy(cc.at[m, :, :, :, lanes], c1, local.at[2]),
        pltpu.make_async_copy(d.at[y], d1, local.at[3]),
    ]
    for copy in copies:
        copy.start()
    for copy in copies:
        copy.wait()

    def second(item, j):
        if item == C:
            return remote(c1.at[:, lax.rem(y + j, 4)], c2r.at[j - 1], send2.at[C, j - 1], recv2.at[C, j - 1], along_y[j - 1])
        if item == DN:
            return remote(d1, d2r.at[j - 1], send2.at[DN, j - 1], recv2.at[DN, j - 1], along_x[j - 1])
        src, dst = ((a1, a2r), (b1, b2r))[item]
        side = xl if j == 2 else 1 - xl
        return remote(src.at[side], dst.at[j - 1], send2.at[item, j - 1], recv2.at[item, j - 1], along_x[j - 1])

    for j in (1, 2, 3):
        first(DN, j).wait_recv()
    add_up(d1, d1, d1r)
    pl.when(holds)(lambda: second(DN, 2).start())

    @pl.when(jnp.logical_not(holds))
    def _():
        second(DN, 1).start()
        second(DN, 3).start()

    for item, own, got in ((A, a1, a1r), (B, b1, b1r)):
        for j in (1, 2, 3):
            first(item, j).wait_recv()
        add_up(own, own, got)
        for j in offsets:
            second(item, j).start()
    for j in (1, 2, 3):
        first(C, j).wait_recv()

    @pl.loop(0, 2)
    def _(i):
        for k in range(4):
            c1[i, k] = (
                c1[i, k].astype(F32)
                + c1r[0, i, k].astype(F32)
                + (c1r[1, i, k].astype(F32) + c1r[2, i, k].astype(F32))
            ).astype(BF)

    for j in offsets:
        second(C, j).start()

    def third(item, j):
        if item == C:
            side = xl if j == 2 else 1 - xl
            return remote(c2.at[side], c3r.at[j - 1], send3.at[C, j - 1], recv3.at[C, j - 1], along_x[j - 1])
        src, dst, size = {A: (a2, a3r, 32), B: (b2, b3r, 32), DN: (d2, d3r, 80)}[item]
        return remote(
            src.at[rows(z + j, size)], dst.at[j - 1], send3.at[item, j - 1], recv3.at[item, j - 1], along_z[j - 1]
        )

    @pl.when(holds)
    def _():
        for j in (1, 2, 3):
            second(DN, j).wait_recv()
        add_up(d2, d1, d2r)
        for j in offsets:
            third(DN, j).start()

    for item, out, own, got in ((A, a2, a1, a2r), (B, b2, b1, b2r)):
        for j in (1, 2, 3):
            second(item, j).wait_recv()
        add_up(out, own.at[xl], got)
        for j in offsets:
            third(item, j).start()
    for j in (1, 2, 3):
        second(C, j).wait_recv()
    for i in range(2):
        c2[i] = (
            c1[i, y].astype(F32)
            + c2r[0, i].astype(F32)
            + (c2r[1, i].astype(F32) + c2r[2, i].astype(F32))
        ).astype(BF)
    for j in offsets:
        third(C, j).start()

    def summed(item, index):
        if item == C:
            m, _ = quarter(index)
            start = FH * c + 640 * lax.rem(index, 2)
            return c_sum.at[m, :, pl.ds(pl.multiple_of(start, 128), 640)]
        if item == DN:
            return d_sum.at[rows(index, 80)]
        return (a_sum, b_sum)[item].at[c, rows(index, 32)]

    part = {A: a3, B: b3, C: c3, DN: d3}

    def spread(item, j):
        return remote(
            part[item], summed(item, z), send4.at[item, j - 1], recv4.at[item, j - 1], along_z[j - 1]
        )

    def keep(item):
        return pltpu.make_async_copy(part[item], summed(item, z), local.at[item])

    def landed(item, j):
        ref = summed(item, lax.rem(z + 4 - j, 4))
        remote(ref, ref, send4.at[item, j - 1], recv4.at[item, j - 1], sibling).wait_recv()

    @pl.when(holds)
    def _():
        for j in (1, 2, 3):
            third(DN, j).wait_recv()
        add_up(d3, d2.at[rows(z, 80)], d3r)
        for j in offsets:
            spread(DN, j).start()
        keep(DN).start()

    for item, out, own, got in ((A, a3, a2, a3r), (B, b3, b2, b3r)):
        for j in (1, 2, 3):
            third(item, j).wait_recv()
        add_up(out, own.at[rows(z, 32)], got)
        for j in offsets:
            spread(item, j).start()
        keep(item).start()
    for j in (1, 2, 3):
        third(C, j).wait_recv()
    add_up(c3, c2.at[xl], c3r)
    for j in offsets:
        spread(C, j).start()
    keep(C).start()

    def whole(item, core):
        if item == C:
            return c_sum.at[:, :, pl.ds(pl.multiple_of(FH * core, 128), FH)]
        if item == DN:
            return d_sum
        return (a_sum, b_sum)[item].at[core]

    def across(item):
        return remote(whole(item, c), whole(item, c), send5.at[item], recv5.at[item], sibling)

    def arrive(item):
        ref = whole(item, 1 - c)
        remote(ref, ref, send5.at[item], recv5.at[item], sibling).wait_recv()

    @pl.when(holds)
    def _():
        keep(DN).wait()
        for j in (1, 2, 3):
            landed(DN, j)
        across(DN).start()

    for item in (A, B, C):
        keep(item).wait()
        for j in (1, 2, 3):
            landed(item, j)
        across(item).start()
    for item in (A, B, C):
        arrive(item)
    pl.when(jnp.logical_not(holds))(lambda: arrive(DN))

    for item in (A, B, C):
        for j in (1, 2, 3):
            first(item, j).wait_send()
            second(item, j).wait_send()
            third(item, j).wait_send()
            spread(item, j).wait_send()
        across(item).wait_send()
    for j in (1, 2, 3):
        first(DN, j).wait_send()

    @pl.when(holds)
    def _():
        second(DN, 2).wait_send()
        for j in (1, 2, 3):
            third(DN, j).wait_send()
            spread(DN, j).wait_send()
        across(DN).wait_send()

    @pl.when(jnp.logical_not(holds))
    def _():
        second(DN, 1).wait_send()
        second(DN, 3).wait_send()


def reduce_gradients(a, b, c, d):
    sem = pltpu.SemaphoreType.DMA
    vm = lambda *shape: pltpu.VMEM(shape, BF)

    def planes(width):
        return [
            vm(2, PAD, width), vm(3, 2, PAD, width), vm(PAD, width), vm(3, PAD, width),
            vm(32, width), vm(3, 32, width),
        ]

    return pl.pallas_call(
        reduce_kernel,
        name="reduce_gradients",
        out_shape=(
            jax.ShapeDtypeStruct((2, PAD, D), BF),
            jax.ShapeDtypeStruct((2, PAD, KW), BF),
            jax.ShapeDtypeStruct((2, ROWS, FF), BF),
            jax.ShapeDtypeStruct((KW, D), BF),
        ),
        in_specs=[ANY] * 4,
        out_specs=(ANY,) * 4,
        scratch_shapes=planes(D)
        + planes(KW)
        + [vm(KW, D), vm(3, KW, D), vm(KW, D), vm(3, KW, D), vm(80, D), vm(3, 80, D)]
        + [
            vm(2, 4, ROWS, 640), vm(3, 2, 4, ROWS, 640), vm(2, ROWS, 640), vm(3, 2, ROWS, 640),
            vm(ROWS, 640), vm(3, ROWS, 640),
        ]
        + [sem((4, 3))] * 8
        + [sem((4,))] * 3,
        compiler_params=params(3),
    )(
        a.reshape(2, 4, PAD, D),
        b.reshape(2, 4, PAD, KW),
        c.reshape(2, 2, 4, ROWS, FH),
        d.reshape(4, KW, D),
    )


def matmul(left, right):
    return jnp.dot(left, right, preferred_element_type=F32)


def rms_scale(stream):
    return lax.rsqrt(jnp.mean(stream * stream, axis=-1, keepdims=True) + norm_epsilon)


def norm_backward(stream, gain_row, incoming):
    scale = rms_scale(stream)
    normal = stream * scale
    gain_grad = jnp.sum(incoming * normal, axis=0)
    scaled = incoming * gain_row
    stream_grad = scale * (scaled - normal * jnp.mean(scaled * normal, axis=-1, keepdims=True))
    return (stream_grad, gain_grad)


def adamw_update(weight, gradient, first, second, rate, decay):
    weight = weight.astype(F32)
    first_new = beta_first * first.astype(F32) + (1.0 - beta_first) * gradient
    second_new = beta_second * second.astype(F32) + (1.0 - beta_second) * gradient * gradient
    first_hat = first_new / (1.0 - beta_first**STEP)
    second_hat = second_new / (1.0 - beta_second**STEP)
    weight_new = weight - rate * (
        first_hat / (jnp.sqrt(second_hat) + adam_epsilon) + decay * weight
    )
    return (weight_new, first_new, second_new)


def body(
    tokens,
    cotangent,
    query_weight,
    keyval_weight,
    output_weight,
    gateup_weight,
    down_weight,
    norm_gains,
    query_first,
    keyval_first,
    output_first,
    gateup_first,
    down_first,
    gains_first,
    query_second,
    keyval_second,
    output_second,
    gateup_second,
    down_second,
    gains_second,
):
    ctx = lax.axis_index("ctx")
    core = lax.rem(ctx, 2)
    gains = lax.all_gather(norm_gains, "fsdp", axis=1, tiled=True).astype(F32)
    qo_all, kv_all, gu_all, dn_all, dy_all = gather_weights(
        jnp.stack([query_weight, output_weight]), keyval_weight, gateup_weight, down_weight, cotangent[0]
    )
    query_full, output_full = qo_all[0].reshape(D, D), qo_all[1].reshape(D, D)
    key_full, value_full = kv_all[0].reshape(D, KW), kv_all[1].reshape(D, KW)
    gate_full, up_full = gu_all[0].reshape(D, FH), gu_all[1].reshape(D, FH)
    down_full = dn_all.reshape(FH, D)
    both_dy = dy_all.reshape(2 * TOK, D)

    stream = tokens[0].astype(F32)
    positions = (ctx * TOK + jnp.arange(TOK, dtype=jnp.int32)).astype(F32)
    counter = jnp.arange(HALF, dtype=F32)
    frequency = 1.0 / rotary_base ** (counter * (2.0 / HEAD_WIDTH))
    angles = frequency[:, None] * positions[None, :]
    cosine, sine = jnp.cos(angles), jnp.sin(angles)

    normed_one = (stream * rms_scale(stream) * gains[0]).astype(BF)
    turn = lambda w, n: lax.dot_general(w, n, (((0,), (1,)), ((), ())), preferred_element_type=F32)
    query_t = turn(query_full, normed_one)
    keyval_t = jnp.concatenate([turn(key_full, normed_one), turn(value_full, normed_one)])
    query_low, attended_t, level, keys = attend(query_t, keyval_t, cosine, sine)
    attended = attended_t.T
    middle = stream + matmul(attended, output_full)
    normed_two = (middle * rms_scale(middle) * gains[1]).astype(BF)
    (normed_other,) = swap(4, normed_two)
    both_two = jnp.concatenate([normed_two, normed_other])
    gate = matmul(both_two, gate_full)
    upward = matmul(both_two, up_full)
    sigmoid_gate = jax.nn.sigmoid(gate)
    hidden = (gate * sigmoid_gate * upward).astype(BF)
    down_part = matmul(hidden, down_full)
    hidden_grad = matmul(both_dy, down_full.T)
    gate_grad = (hidden_grad * upward * sigmoid_gate * (1.0 + gate * (1.0 - sigmoid_gate))).astype(BF)
    up_grad = (hidden_grad * gate * sigmoid_gate).astype(BF)
    two_part = matmul(gate_grad, gate_full.T) + matmul(up_grad, up_full.T)
    down_other, two_other = swap(5, down_part[TOK:], two_part[TOK:])
    result = middle + down_part[:TOK] + down_other
    normed_two_grad = two_part[:TOK] + two_other
    grad_down = matmul(hidden.T, both_dy).astype(BF)
    grad_gateup = jnp.stack(
        [matmul(both_two.T, gate_grad).astype(BF), matmul(both_two.T, up_grad).astype(BF)]
    )

    incoming = cotangent[0].astype(F32)
    middle_norm_grad, gain_two_grad = norm_backward(middle, gains[1], normed_two_grad)
    middle_grad = incoming + middle_norm_grad
    middle_low = middle_grad.astype(BF)
    attended_grad_t = lax.dot_general(
        output_full, middle_low, (((1,), (1,)), ((), ())), preferred_element_type=F32
    ).astype(BF)
    query_back_t, keyval_back_t = attend_back(
        query_low, keys, level, attended_t, attended_grad_t, cosine, sine
    )
    query_back = query_back_t.T
    key_back, value_back = keyval_back_t[:KW].T, keyval_back_t[KW:].T

    zero = core == 0
    left_out, left_in = jnp.where(zero, attended, normed_one), jnp.where(zero, normed_one, attended)
    right_out, right_in = jnp.where(zero, middle_low, query_back), jnp.where(zero, query_back, middle_low)
    narrow_out, narrow_in = jnp.where(zero, value_back, key_back), jnp.where(zero, key_back, value_back)
    left_got, right_got, narrow_got, one_got = swap(6, left_out, right_out, narrow_out, normed_one)

    def padded(rows):
        return jnp.pad(rows.reshape(2 * TOK, 8, ROWS), ((0, 0), (0, 0), (0, PAD - ROWS))).reshape(2 * TOK, 8 * PAD)

    grad_wide = matmul(
        padded(jnp.concatenate([left_in, left_got])).T, jnp.concatenate([right_in, right_got])
    ).astype(BF)
    grad_narrow = matmul(
        padded(jnp.concatenate([normed_one, one_got])).T, jnp.concatenate([narrow_in, narrow_got])
    ).astype(BF)

    normed_one_grad = (
        matmul(query_back, query_full.T) + matmul(key_back, key_full.T) + matmul(value_back, value_full.T)
    )
    stream_norm_grad, gain_one_grad = norm_backward(stream, gains[0], normed_one_grad)
    input_grad = middle_grad + stream_norm_grad
    grad_gains = jnp.stack([gain_one_grad, gain_two_grad]).reshape(2, 8, ROWS).transpose(1, 0, 2).astype(BF)
    grad_wide = grad_wide.reshape(8, PAD, D).at[:, ROWS : ROWS + 2, :ROWS].set(grad_gains)

    wide, narrow, gateup, down = reduce_gradients(grad_wide, grad_narrow, grad_gateup, grad_down)
    gains_sum = wide[0, ROWS : ROWS + 2, :ROWS].astype(F32) + wide[1, ROWS : ROWS + 2, :ROWS].astype(F32)
    summed = (
        wide[0, :ROWS].astype(F32),
        narrow[:, :ROWS].astype(F32),
        wide[1, :ROWS].astype(F32),
        gateup.astype(F32),
        down.astype(F32),
        gains_sum,
    )
    shards = (query_weight, keyval_weight, output_weight, gateup_weight, down_weight, norm_gains)
    firsts = (query_first, keyval_first, output_first, gateup_first, down_first, gains_first)
    seconds = (query_second, keyval_second, output_second, gateup_second, down_second, gains_second)
    rates = (matrix_rate,) * 5 + (gain_rate,)
    decays = (matrix_decay,) * 5 + (0.0,)
    updated = [
        adamw_update(shards[i], summed[i], firsts[i], seconds[i], rates[i], decays[i])
        for i in range(6)
    ]
    return (
        result.astype(BF)[None],
        input_grad[None],
        *[updated[i][0] for i in range(6)],
        *[updated[i][1] for i in range(6)],
        *[updated[i][2] for i in range(6)],
    )


def solution(mesh):
    row, mid = P("fsdp", None), P(None, "fsdp", None)
    weights = (row, mid, row, mid, row, P(None, "fsdp"))
    stream = P(("rep", "fsdp"), "ctx", None)
    return jax.shard_map(
        body,
        mesh=mesh,
        in_specs=(stream, stream) + weights * 3,
        out_specs=(stream, stream) + weights * 3,
        check_vma=False,
    )
```

```python
import functools

import jax
import jax.numpy as jnp
from jax import lax
from jax.experimental import pallas as pl
from jax.experimental.pallas import tpu as pltpu
from jax.sharding import PartitionSpec as P

QUERY_HEADS = 15
KEY_VALUE_HEADS = 5
GROUP = QUERY_HEADS // KEY_VALUE_HEADS
HEAD_WIDTH = 64
HALF = HEAD_WIDTH // 2
STEP = 10
TOK = 256
D = 960
KW = 320
FF = 2560
FH = FF // 2
ROWS = 120
PAD = 128
BF = jnp.bfloat16
F32 = jnp.float32
MESH = pl.DeviceIdType.MESH

norm_epsilon = 1e-05
rotary_base = 100000.0
beta_first = 0.9
beta_second = 0.95
adam_epsilon = 1e-08
matrix_rate = 0.06
matrix_decay = 0.1
gain_rate = 0.6
score_scale = HEAD_WIDTH ** (-0.5)

ANY = pl.BlockSpec(memory_space=pl.ANY)
VM = pl.BlockSpec(memory_space=pltpu.VMEM)


def place():
    f = lax.axis_index("fsdp")
    q = lax.axis_index("ctx")
    z = lax.axis_index("rep")
    return (q // 2) * 2 + f // 4, f % 4, z, q % 2


def at(x, y, z, core):
    x, y, z = lax.rem(x, 4), lax.rem(y, 4), lax.rem(z, 4)
    return {"rep": z, "fsdp": lax.rem(x, 2) * 4 + y, "ctx": (x // 2) * 2 + core}


def greet(devices):
    barrier = pltpu.get_barrier_semaphore()
    for device in devices:
        pl.semaphore_signal(barrier, inc=1, device_id=device, device_id_type=MESH)
    pl.semaphore_wait(barrier, len(devices))


def remote(src, dst, send, recv, device):
    return pltpu.make_async_remote_copy(
        src_ref=src, dst_ref=dst, send_sem=send, recv_sem=recv, device_id=device, device_id_type=MESH
    )


def params(number, vmem=56):
    return pltpu.CompilerParams(
        collective_id=number, has_side_effects=True, vmem_limit_bytes=vmem * 2**20
    )


ORDER = (1, 3, 2)
SIDE = (1, 3, 3, 1)


def gather_kernel(
    qo, kv, gain, dy, qo_all, kv_all, gain_all, dy_all, send_y, send_x, send_s, recv, recv_s, local
):
    x, y, z, c = place()
    xl = lax.rem(x, 2)
    f = 4 * xl + y
    sibling = at(x, y, z, 1 - c)
    greet([at(x, y + j, z, c) for j in (1, 2, 3)] + [at(x + j, y, z, c) for j in (1, 3)] + [sibling])
    own = (qo.at[c], kv.at[c], gain)

    def slot(item, g, core):
        if item == 2:
            return gain_all.at[g]
        return (qo_all, kv_all)[item].at[core, g]

    def wait_slot(item, g):
        ref = slot(item, g, c)
        remote(ref, ref, send_s.at[0, 0], recv.at[item, g], sibling).wait_recv()

    def send_row(item, j):
        return remote(own[item], slot(item, f, c), send_y.at[item, j - 1], recv.at[item, f], at(x, y + j, z, c))

    def send_side(item, j):
        g = 4 * xl + lax.rem(y + j, 4)
        return remote(
            own[item] if j == 0 else slot(item, g, c),
            slot(item, g, c),
            send_x.at[item, j],
            recv.at[item, g],
            at(x + SIDE[j], y, z, c),
        )

    def column(k):
        return 4 * xl + lax.rem(y + k + 1, 4) if k < 3 else 4 * (1 - xl) + lax.rem(y + k - 3, 4)

    def send_sib(item, k):
        ref = slot(item, column(k), c)
        return remote(ref, ref, send_s.at[item, k], recv_s.at[item, column(k)], sibling)

    items = (2, 0, 1)
    for item in items:
        send_side(item, 0).start()
        for j in ORDER:
            send_row(item, j).start()
    exchange = remote(dy, dy_all.at[1], send_s.at[2, 0], recv_s.at[2, 0], sibling)
    exchange.start()
    copies = [
        pltpu.make_async_copy(qo, qo_all.at[:, f], local.at[0]),
        pltpu.make_async_copy(kv, kv_all.at[:, f], local.at[1]),
        pltpu.make_async_copy(gain, gain_all.at[f], local.at[2]),
        pltpu.make_async_copy(dy, dy_all.at[0], local.at[3]),
    ]
    for copy in copies:
        copy.start()
    for item in items:
        for j in (1, 3):
            wait_slot(item, 4 * xl + lax.rem(y + j, 4))
            send_side(item, j).start()
            if item < 2:
                send_sib(item, j - 1).start()
    for item in (0, 1):
        wait_slot(item, column(3))
        send_sib(item, 3).start()
    for item in items:
        wait_slot(item, column(1))
        send_side(item, 2).start()
        if item < 2:
            send_sib(item, 1).start()
    for k in (4, 6, 5):
        for item in (0, 1):
            wait_slot(item, column(k))
            send_sib(item, k).start()
    for k in (3, 4, 6, 5):
        wait_slot(2, column(k))
    for copy in copies:
        copy.wait()
    exchange.wait()
    for item in (0, 1):
        for k in range(7):
            ref = slot(item, column(k), 1 - c)
            remote(ref, ref, send_s.at[0, 0], recv_s.at[item, column(k)], sibling).wait_recv()
            send_sib(item, k).wait_send()
    for item in items:
        for j in ORDER:
            send_row(item, j).wait_send()
        for j in range(4):
            send_side(item, j).wait_send()


def gather_weights(qo, kv, gain, dy):
    sem = pltpu.SemaphoreType.DMA
    return pl.pallas_call(
        gather_kernel,
        name="gather_weights",
        out_shape=(
            jax.ShapeDtypeStruct((2, 8, ROWS, D), BF),
            jax.ShapeDtypeStruct((2, 8, ROWS, KW), BF),
            jax.ShapeDtypeStruct((8, 8, 128), F32),
            jax.ShapeDtypeStruct((2, D, TOK), BF),
        ),
        in_specs=[ANY] * 4,
        out_specs=(ANY,) * 4,
        scratch_shapes=[sem((3, 3)), sem((3, 4)), sem((3, 7)), sem((3, 8)), sem((3, 8)), sem((4,))],
        compiler_params=params(0),
    )(qo, kv, gain, dy)


def swap_kernel(count, *refs):
    ins, outs = refs[:count], refs[count : 2 * count]
    send, recv = refs[2 * count :]
    x, y, z, c = place()
    sibling = at(x, y, z, 1 - c)
    greet([sibling])
    copies = [
        remote(ins[i], outs[i], send.at[i], recv.at[i], sibling) for i in range(count)
    ]
    for copy in copies:
        copy.start()
    for copy in copies:
        copy.wait()


def swap(number, *arrays):
    count = len(arrays)
    return pl.pallas_call(
        functools.partial(swap_kernel, count),
        name="swap_%d" % number,
        out_shape=tuple(jax.ShapeDtypeStruct(a.shape, a.dtype) for a in arrays),
        in_specs=[ANY] * count,
        out_specs=(ANY,) * count,
        scratch_shapes=[pltpu.SemaphoreType.DMA((count,)), pltpu.SemaphoreType.DMA((count,))],
        compiler_params=params(number),
    )(*arrays)


def dot(a, b, ca, cb):
    return lax.dot_general(a, b, (((ca,), (cb,)), ((), ())), preferred_element_type=F32)


def forward_kernel(
    stream, wq, wk, wv, wo, gains, cos, sin, gu, dn,
    q_low, att, lse, kv_out, one, mid, two_all, gu_all, dn_all,
    keys, wide, two, send, recv, send_y, send_x, recv_w, local,
):
    x, y, z, c = place()
    xl = lax.rem(x, 2)
    f = 4 * xl + y
    holds = c == xl
    me = 2 * (x // 2) + c
    sib_slot, far_slot, diag_slot = me + 1 - 2 * c, lax.rem(me + 2, 4), lax.rem(me + 2, 4) + 1 - 2 * c
    sibling, far = at(x, y, z, 1 - c), at(x + 2, y, z, c)
    greet([at(x, y + j, z, c) for j in (1, 2, 3)] + [at(x + j, y, z, c) for j in (1, 2, 3)] + [sibling])

    lanes = pl.ds(pl.multiple_of(c * FH, 128), FH)
    own = (gu.at[0, :, lanes], gu.at[1, :, lanes], dn.at[0:160], dn.at[160:320])

    def slot(item, g):
        if item < 2:
            return gu_all.at[item, g]
        return dn_all.at[lax.rem(g, 4), 160 * (item - 2) : 160 * (item - 1)]

    def wait_slot(item, g):
        remote(slot(item, g), slot(item, g), send_x.at[0, 0], recv_w.at[item, g], sibling).wait_recv()

    def send_row(item, j):
        return remote(own[item], slot(item, f), send_y.at[item, j - 1], recv_w.at[item, f], at(x, y + j, z, c))

    def send_side(item, j):
        g = 4 * xl + lax.rem(y + j, 4)
        return remote(
            own[item] if j == 0 else slot(item, g),
            slot(item, g),
            send_x.at[item, j],
            recv_w.at[item, g],
            at(x + (1, 3, 1, 3)[item], y, z, c),
        )

    def pass_on(items, offsets):
        for item in items:
            for j in offsets:
                wait_slot(item, 4 * xl + lax.rem(y + j, 4))
                send_side(item, j).start()

    def pass_down(offsets):
        pl.when(holds)(lambda: pass_on((2, 3), offsets))

    for j in ORDER:
        for item in (0, 1):
            send_row(item, j).start()

        @pl.when(holds)
        def _():
            for item in (2, 3):
                send_row(item, j).start()

    own_copies = [pltpu.make_async_copy(gu.at[:, :, lanes], gu_all.at[:, f], local.at[0])]
    own_copies[0].start()
    own_down = pltpu.make_async_copy(dn, dn_all.at[y], local.at[1])
    pl.when(holds)(own_down.start)

    co, si = cos[...], sin[...]
    scale = lax.rsqrt(jnp.sum(stream[...].astype(F32) ** 2, axis=0, keepdims=True) / D + norm_epsilon)
    one[...] = (stream[...].astype(F32) * scale * gains[0]).astype(BF)
    wide[:KW, :] = dot(wk[...], one[...], 0, 0)
    wide[KW : 2 * KW, :] = dot(wv[...], one[...], 0, 0)
    for h in range(KEY_VALUE_HEADS):
        a, b = wide[64 * h : 64 * h + 32, :], wide[64 * h + 32 : 64 * h + 64, :]
        keys[me, 64 * h : 64 * h + 32, :] = (a * co - b * si).astype(BF)
        keys[me, 64 * h + 32 : 64 * h + 64, :] = (b * co + a * si).astype(BF)
    keys[me, KW:, :] = wide[KW : 2 * KW, :].astype(BF)
    to_far = remote(keys.at[me], keys.at[me], send.at[0], recv.at[0], far)
    to_sib = remote(keys.at[me], keys.at[me], send.at[1], recv.at[1], sibling)
    to_far.start()
    to_sib.start()
    for item in (0, 1):
        send_side(item, 0).start()

    @pl.when(holds)
    def _():
        for item in (2, 3):
            send_side(item, 0).start()

    for start in range(0, D, 256):
        stop = min(start + 256, D)
        wide[start:stop, :] = dot(wq[:, start:stop], one[...], 0, 0)
    for h in range(QUERY_HEADS):
        a, b = wide[64 * h : 64 * h + 32, :], wide[64 * h + 32 : 64 * h + 64, :]
        q_low[64 * h : 64 * h + 32, :] = ((a * co - b * si).astype(BF) * score_scale).astype(BF)
        q_low[64 * h + 32 : 64 * h + 64, :] = ((b * co + a * si).astype(BF) * score_scale).astype(BF)
    pass_on((0,), (1, 3))
    remote(keys.at[far_slot], keys.at[far_slot], send.at[0], recv.at[0], far).wait_recv()
    on = remote(keys.at[far_slot], keys.at[far_slot], send.at[2], recv.at[2], sibling)
    on.start()
    remote(keys.at[sib_slot], keys.at[sib_slot], send.at[1], recv.at[1], sibling).wait_recv()
    remote(keys.at[diag_slot], keys.at[diag_slot], send.at[2], recv.at[2], sibling).wait_recv()
    gap = lax.broadcasted_iota(jnp.int32, (TOK, TOK), 0) - lax.broadcasted_iota(jnp.int32, (TOK, TOK), 1)

    def head(h, carry):
        rows = pl.ds(pl.multiple_of(h * 64, 64), 64)
        g = h // GROUP
        krows = pl.ds(pl.multiple_of(g * 64, 64), 64)
        vrows = pl.ds(pl.multiple_of(KW + g * 64, 64), 64)
        qh = q_low[rows, :]
        s = []
        for j in range(4):
            part = dot(keys[j, krows, :], qh, 0, 0)
            s.append(jnp.where(gap <= 256 * (me - j), part, -1e30))
        top = jnp.max(jnp.maximum(jnp.maximum(s[0], s[1]), jnp.maximum(s[2], s[3])), axis=0, keepdims=True)
        e = [jnp.exp(part - top) for part in s]
        total = jnp.sum(e[0] + e[1] + (e[2] + e[3]), axis=0, keepdims=True)
        acc = dot(keys[0, vrows, :], e[0].astype(BF), 1, 0)
        for j in range(1, 4):
            acc += dot(keys[j, vrows, :], e[j].astype(BF), 1, 0)
        att[rows, :] = (acc / total).astype(BF)
        lse[pl.ds(h, 1), 0, :] = top + jnp.log(total)
        pl.when(h == 1)(lambda: pass_on((1,), (1, 3)))
        pl.when(h == 5)(lambda: pass_down((1, 3)))
        pl.when(h == 9)(lambda: pass_on((0,), (2,)))
        pl.when(h == 13)(lambda: pass_on((1,), (2,)))
        return carry

    lax.fori_loop(0, QUERY_HEADS, head, 0)
    kv_out[...] = keys[...]

    square = jnp.zeros((1, TOK), F32)
    for start in range(0, D, 256):
        stop = min(start + 256, D)
        part = stream[start:stop, :].astype(F32) + dot(wo[:, start:stop], att[...], 0, 0)
        mid[start:stop, :] = part
        square += jnp.sum(part * part, axis=0, keepdims=True)
    scale = lax.rsqrt(square / D + norm_epsilon)
    two[...] = (mid[...] * scale * gains[1]).astype(BF)
    keep = pltpu.make_async_copy(two, two_all.at[0], local.at[2])
    keep.start()
    trade = remote(two, two_all.at[1], send.at[3], recv.at[3], sibling)
    trade.start()
    pass_down((2,))

    for k in range(4):
        g = 4 * (1 - xl) + lax.rem(y + k, 4)
        for item in (0, 1):
            wait_slot(item, g)

        @pl.when(jnp.logical_not(holds))
        def _():
            for item in (2, 3):
                wait_slot(item, g)

    own_copies[0].wait()
    keep.wait()
    trade.wait()
    to_far.wait_send()
    to_sib.wait_send()
    on.wait_send()

    def sent(items):
        for item in items:
            for j in ORDER:
                send_row(item, j).wait_send()
            for j in range(4):
                send_side(item, j).wait_send()

    sent((0, 1))

    @pl.when(holds)
    def _():
        own_down.wait()
        sent((2, 3))


def forward(stream, wq, wk, wv, wo, gains, cos, sin, gu, dn):
    sem = pltpu.SemaphoreType.DMA
    return pl.pallas_call(
        forward_kernel,
        name="forward",
        out_shape=(
            jax.ShapeDtypeStruct((D, TOK), BF),
            jax.ShapeDtypeStruct((D, TOK), BF),
            jax.ShapeDtypeStruct((16, 1, TOK), F32),
            jax.ShapeDtypeStruct((4, 2 * KW, TOK), BF),
            jax.ShapeDtypeStruct((D, TOK), BF),
            jax.ShapeDtypeStruct((D, TOK), F32),
            jax.ShapeDtypeStruct((2, D, TOK), BF),
            jax.ShapeDtypeStruct((2, 8, ROWS, FH), BF),
            jax.ShapeDtypeStruct((4, KW, D), BF),
        ),
        in_specs=[VM] * 8 + [ANY] * 2,
        out_specs=(VM,) * 6 + (ANY,) * 3,
        scratch_shapes=[
            pltpu.VMEM((4, 2 * KW, TOK), BF),
            pltpu.VMEM((D, TOK), F32),
            pltpu.VMEM((D, TOK), BF),
            sem((4,)),
            sem((4,)),
            sem((4, 3)),
            sem((4, 4)),
            sem((4, 8)),
            sem((3,)),
        ],
        compiler_params=params(1),
    )(stream, wq, wk, wv, wo, gains, cos, sin, gu, dn)


def summed(own, got, count=3):
    total = own.astype(F32)
    for i in range(count):
        total += got[i].astype(F32)
    return total.astype(BF)


def ring(x, y, z, c):
    along_x = [at(x + j, y, z, c) for j in (1, 2, 3)]
    along_y = [at(x, y + j, z, c) for j in (1, 2, 3)]
    along_z = [at(x, y, z + j, c) for j in (1, 2, 3)]
    return along_x, along_y, along_z


def quarter(index, size):
    return pl.ds(pl.multiple_of(lax.rem(index, 4) * size, 16), size)


def planes(value, extra):
    return [
        jnp.concatenate([value[ROWS * f : ROWS * (f + 1)], extra[f]], axis=0).astype(BF)
        for f in range(8)
    ]


def columns(total):
    return [(start, min(start + 256, total)) for start in range(0, total, 256)]


def backward_kernel(
    q_low, keys, lse, att, grad, cos, sin, two, gate_grad, up_grad, hidden, dy,
    q_back, kv_back, c0_out, c1_out, d_out,
    mine, got, far_got, acc, c0, c0r, c1, c1r, c1s, c1t, d, dr, ds_, dt,
    send, recv, send_z, recv_z, send_x, recv_x, send_t, recv_t, send_y, recv_y, send_d, recv_d,
):
    x, y, z, c = place()
    xl = lax.rem(x, 2)
    holds = c == xl
    me = 2 * (x // 2) + c
    far_slot = lax.rem(me + 2, 4)
    sib_slot = me + 1 - 2 * c
    diag_slot = far_slot + 1 - 2 * c
    sibling, far = at(x, y, z, 1 - c), at(x + 2, y, z, c)
    along_x, along_y, along_z = ring(x, y, z, c)
    greet(along_x + along_y + along_z + [sibling])
    co, si = cos[...], sin[...]
    nothing = [jnp.zeros((8, 256), F32)] * 8

    def c0_z(j):
        return remote(c0.at[:, :, quarter(z + j, 32)], c0r.at[j - 1], send_z.at[j - 1], recv_z.at[j - 1], along_z[j - 1])

    def c1_x(i):
        return remote(
            c1.at[1 - xl, :, :, 640 * i : 640 * (i + 1)], c1r.at[i], send_x.at[i], recv_x.at[i], along_x[2 * i]
        )

    def c1_z(j):
        return remote(c1s.at[:, quarter(z + j, 32)], c1t.at[j - 1], send_t.at[j - 1], recv_t.at[j - 1], along_z[j - 1])

    def d_y(j):
        return remote(d.at[lax.rem(y + j, 4)], dr.at[j - 1], send_y.at[j - 1], recv_y.at[j - 1], along_y[j - 1])

    def d_x(j):
        return remote(ds_, dt.at[j - 1], send_d.at[j - 1], recv_d.at[j - 1], along_x[j - 1])

    for start, stop in columns(FH):
        part = planes(dot(two[...], gate_grad[start:stop, :], 1, 1), nothing)
        for f in range(8):
            c0[f // 4, f % 4, :, start:stop] = part[f]
    for j in ORDER:
        c0_z(j).start()
    for start, stop in columns(D):
        part = dot(hidden[...], dy[start:stop, :], 1, 1).astype(BF)
        for k in range(4):
            d[k, :, start:stop] = part[KW * k : KW * (k + 1)]
    for j in ORDER:
        d_y(j).start()
    for start, stop in columns(FH):
        part = planes(dot(two[...], up_grad[start:stop, :], 1, 1), nothing)
        for f in range(8):
            c1[f // 4, f % 4, :, start:stop] = part[f]
    for i in (0, 1):
        c1_x(i).start()

    def step_c1():
        for i in (0, 1):
            c1_x(i).wait_recv()
        for k in range(4):
            for i in (0, 1):
                lanes = slice(640 * i, 640 * (i + 1))
                c1s[k, :, lanes] = (c1[xl, k, :, lanes].astype(F32) + c1r[i, k].astype(F32)).astype(BF)
        for j in ORDER:
            c1_z(j).start()

    def step_d():
        for j in (1, 2, 3):
            d_y(j).wait_recv()
        ds_[...] = summed(d[y], dr)
        pl.when(holds)(lambda: d_x(2).start())

        @pl.when(jnp.logical_not(holds))
        def _():
            d_x(1).start()
            d_x(3).start()

    gap = lax.broadcasted_iota(jnp.int32, (TOK, TOK), 0) - lax.broadcasted_iota(jnp.int32, (TOK, TOK), 1)

    def group(g, carry):
        krows = pl.ds(pl.multiple_of(g * 64, 64), 64)
        vrows = pl.ds(pl.multiple_of(KW + g * 64, 64), 64)

        def head(t, inner):
            h = g * GROUP + t
            rows = pl.ds(pl.multiple_of(h * 64, 64), 64)
            qh, gh = q_low[rows, :], grad[rows, :]
            row_dot = jnp.sum(gh.astype(F32) * att[rows, :].astype(F32), axis=0, keepdims=True)
            level = lse[pl.ds(h, 1), 0, :]
            dq = jnp.zeros((64, TOK), F32)
            for j in range(4):
                s = dot(keys[j, krows, :], qh, 0, 0)
                s = jnp.where(gap <= 256 * (me - j), s, -1e30)
                p = jnp.exp(s - level)
                dp = dot(keys[j, vrows, :], gh, 0, 0)
                ds = (p * (dp - row_dot)).astype(BF)
                pb = p.astype(BF)
                dq += dot(keys[j, krows, :], ds, 1, 0)
                dk = dot(qh, ds, 1, 1)
                dv = dot(gh, pb, 1, 1)
                first = t == 0
                acc[j, 0] = jnp.where(first, dk, acc[j, 0] + dk)
                acc[j, 1] = jnp.where(first, dv, acc[j, 1] + dv)
            dq = dq * score_scale
            a, b = dq[:32], dq[32:]
            q_back[pl.ds(pl.multiple_of(h * 64, 32), 32), :] = (a * co + b * si).astype(BF)
            q_back[pl.ds(pl.multiple_of(h * 64 + 32, 32), 32), :] = (b * co - a * si).astype(BF)
            return inner

        lax.fori_loop(0, GROUP, head, 0)
        for j in range(4):
            mine[j, krows, :] = acc[j, 0].astype(BF)
            mine[j, vrows, :] = acc[j, 1].astype(BF)
        pl.when(g == 1)(step_c1)
        pl.when(g == 3)(step_d)
        return carry

    acc[...] = jnp.zeros_like(acc)
    lax.fori_loop(0, KEY_VALUE_HEADS, group, 0)
    to_sib_far = remote(mine.at[diag_slot], got.at[1], send.at[0], recv.at[0], sibling)
    to_sib = remote(mine.at[sib_slot], got.at[0], send.at[1], recv.at[1], sibling)
    to_sib_far.start()
    to_sib.start()
    to_sib_far.wait_recv()
    got[1] = (mine[far_slot].astype(F32) + got[1].astype(F32)).astype(BF)
    to_far = remote(got.at[1], far_got, send.at[2], recv.at[2], far)
    to_far.start()
    to_sib.wait_recv()

    @pl.when(holds)
    def _():
        for j in (1, 2, 3):
            d_x(j).wait_recv()
        d_out[...] = summed(ds_[...], dt)

    @pl.when(jnp.logical_not(holds))
    def _():
        d_out[...] = jnp.zeros_like(d_out)

    near = mine[me].astype(F32) + got[0].astype(F32)
    to_far.wait_recv()
    total = near + far_got[...].astype(F32)
    for h in range(KEY_VALUE_HEADS):
        a, b = total[64 * h : 64 * h + 32, :], total[64 * h + 32 : 64 * h + 64, :]
        kv_back[64 * h : 64 * h + 32, :] = (a * co + b * si).astype(BF)
        kv_back[64 * h + 32 : 64 * h + 64, :] = (b * co - a * si).astype(BF)
    kv_back[KW:, :] = total[KW:, :].astype(BF)
    for j in (1, 2, 3):
        c0_z(j).wait_recv()
    for i in (0, 1):
        for k in range(4):
            c0_out[i, k] = summed(c0[i, k, quarter(z, 32)], [c0r[j, i, k] for j in range(3)])
    for j in (1, 2, 3):
        c1_z(j).wait_recv()
    for k in range(4):
        c1_out[k] = summed(c1s[k, quarter(z, 32)], [c1t[j, k] for j in range(3)])

    to_sib_far.wait_send()
    to_sib.wait_send()
    to_far.wait_send()
    for j in (1, 2, 3):
        c0_z(j).wait_send()
        c1_z(j).wait_send()
        d_y(j).wait_send()
    for i in (0, 1):
        c1_x(i).wait_send()
    pl.when(holds)(lambda: d_x(2).wait_send())

    @pl.when(jnp.logical_not(holds))
    def _():
        d_x(1).wait_send()
        d_x(3).wait_send()


def backward(*args):
    sem = pltpu.SemaphoreType.DMA
    vm = lambda *shape: pltpu.VMEM(shape, BF)
    return pl.pallas_call(
        backward_kernel,
        name="backward",
        out_shape=(
            jax.ShapeDtypeStruct((D, TOK), BF),
            jax.ShapeDtypeStruct((2 * KW, TOK), BF),
            jax.ShapeDtypeStruct((2, 4, 32, FH), BF),
            jax.ShapeDtypeStruct((4, 32, FH), BF),
            jax.ShapeDtypeStruct((KW, D), BF),
        ),
        in_specs=[VM] * 12,
        out_specs=(VM,) * 5,
        scratch_shapes=[
            vm(4, 2 * KW, TOK), vm(2, 2 * KW, TOK), vm(2 * KW, TOK), pltpu.VMEM((4, 2, 64, TOK), F32),
            vm(2, 4, PAD, FH), vm(3, 2, 4, 32, FH),
            vm(2, 4, PAD, FH), vm(2, 4, PAD, 640), vm(4, PAD, FH), vm(3, 4, 32, FH),
            vm(4, KW, D), vm(3, KW, D), vm(KW, D), vm(3, KW, D),
        ]
        + [sem((3,))] * 4
        + [sem((2,))] * 2
        + [sem((3,))] * 6,
        compiler_params=params(2),
    )(*args)


WIDE, NARROW = 512, D - 512


def finish_kernel(
    one, att, mid, q_back, kv_back, gain, c0, c1, dd,
    lo_sum, hi_sum, kv_sum, c0_sum, c1_sum, d_sum,
    left, right, thin, both, lo, hi, kv,
    lo1, lo1r, lo2, lo2r, lo3, lo3r,
    kv1, kv1r, kv2, kv2r, kv3, kv3r,
    hi1, hi1r, hi2, hi2r, hi3, hi3r,
    c02r, c02, c03r, c03,
    c1r, c1s, c1t, c1u,
    dr, ds_,
    send, recv, send_s, recv_s, send_g, recv_g, send_o, recv_o, local,
):
    x, y, z, c = place()
    xl = lax.rem(x, 2)
    holds = c == xl
    sibling = at(x, y, z, 1 - c)
    along_x, along_y, along_z = ring(x, y, z, c)
    greet(along_x + along_y + along_z + [sibling])
    LO, HI, KV, C0, C1, DN = range(6)

    def trade(i, src, dst):
        return remote(src, dst, send_s.at[i], recv_s.at[i], sibling)

    far = slice(TOK, 2 * TOK)

    def trades(core):
        return [
            trade(0, att if core == 0 else one, left.at[:, far]),
            trade(1, mid if core == 0 else q_back, right.at[:, far]),
            trade(2, kv_back.at[KW:] if core == 0 else kv_back.at[:KW], thin.at[:, far]),
            trade(3, one, both.at[:, far]),
        ]

    def move(item, phase, j, src, dst, along):
        return remote(src, dst.at[j - 1], send.at[item, phase, j - 1], recv.at[item, phase, j - 1], along[j - 1])

    def y1(item, j):
        src, dst = {LO: (lo, lo1r), KV: (kv, kv1r)}[item]
        return move(item, 0, j, src.at[:, lax.rem(y + j, 4)], dst, along_y)

    def x2(item, j):
        src, dst = {LO: (lo1, lo2r), KV: (kv1, kv2r)}[item]
        return move(item, 1, j, src.at[xl if j == 2 else 1 - xl], dst, along_x)

    def z3(item, j):
        if item == DN:
            return move(item, 2, j, dd.at[quarter(z + j, 80)], dr, along_z)
        src, dst = {LO: (lo2, lo3r), KV: (kv2, kv3r)}[item]
        return move(item, 2, j, src.at[quarter(z + j, 32)], dst, along_z)

    def z1(j):
        return move(HI, 0, j, hi.at[:, :, quarter(z + j, 32)], hi1r, along_z)

    def y2(item, j):
        src, dst = {HI: (hi1, hi2r), C0: (c0, c02r)}[item]
        return move(item, 1, j, src.at[:, lax.rem(y + j, 4)], dst, along_y)

    def x3(item, j):
        src, dst = {HI: (hi2, hi3r), C0: (c02, c03r)}[item]
        return move(item, 2, j, src.at[xl if j == 2 else 1 - xl], dst, along_x)

    def y_up(j):
        return move(C1, 0, j, c1.at[lax.rem(y + j, 4)], c1r, along_y)

    def x_up():
        return remote(c1s, c1t, send.at[C1, 1, 0], recv.at[C1, 1, 0], along_x[1])

    for core in (0, 1):

        @pl.when(c == core)
        def _(core=core):
            for copy in trades(core):
                copy.start()

    for j in ORDER:
        y2(C0, j).start()
        y_up(j).start()

    @pl.when(holds)
    def _():
        for j in ORDER:
            z3(DN, j).start()

    near = slice(0, TOK)

    @pl.when(c == 0)
    def _():
        left[:, near] = one[...]
        right[:, near] = q_back[...]
        thin[:, near] = kv_back[:KW, :]

    @pl.when(c == 1)
    def _():
        left[:, near] = att[...]
        right[:, near] = mid[...]
        thin[:, near] = kv_back[KW:, :]

    both[:, near] = one[...]
    trade(3, one, both.at[:, far]).wait_recv()
    trade(2, kv_back.at[:KW], thin.at[:, far]).wait_recv()
    nothing = [jnp.zeros((8, KW), F32)] * 8
    part = planes(dot(both[...], thin[...], 1, 1), nothing)
    for f in range(8):
        kv[f // 4, f % 4] = part[f]
    for j in ORDER:
        y1(KV, j).start()
    trade(0, one, left.at[:, far]).wait_recv()
    trade(1, one, right.at[:, far]).wait_recv()
    for start, stop in ((256, 512), (0, 256), (512, 768), (768, D)):
        size = stop - start
        extra = [gain[f] if start == 0 else jnp.zeros((8, size), F32) for f in range(8)]
        part = planes(dot(left[...], right[start:stop, :], 1, 1), extra)
        for f in range(8):
            if start < WIDE:
                lo[f // 4, f % 4, :, start:stop] = part[f]
            else:
                hi[f // 4, f % 4, :, start - WIDE : stop - WIDE] = part[f]
        if start == 0:
            for j in ORDER:
                y1(LO, j).start()
    for j in ORDER:
        z1(j).start()

    def arrived(make, *key):
        for j in (1, 2, 3):
            make(*key, j).wait_recv()

    arrived(y2, C0)
    for i in range(2):
        c02[i] = summed(c0[i, y], [c02r[j, i] for j in range(3)])
    for j in ORDER:
        x3(C0, j).start()
    arrived(y_up)
    c1s[...] = summed(c1[y], c1r)
    x_up().start()

    part_of = {LO: lo3, HI: hi3, KV: kv3, C0: c03, C1: c1u, DN: ds_}

    def place_of(item, index, core):
        if item == DN:
            return d_sum.at[quarter(index, 80)]
        if item in (C0, C1):
            lanes = pl.ds(pl.multiple_of(FH * core, 128), FH)
            return (c0_sum if item == C0 else c1_sum).at[quarter(index, 32), lanes]
        return {LO: lo_sum, HI: hi_sum, KV: kv_sum}[item].at[core, quarter(index, 32)]

    def spread(item, j):
        return remote(
            part_of[item], place_of(item, z, c), send_g.at[item, j - 1], recv_g.at[item, j - 1], along_z[j - 1]
        )

    def keep(item):
        return pltpu.make_async_copy(part_of[item], place_of(item, z, c), local.at[item])

    def across(item, k):
        index = lax.rem(z + 4 - k, 4)
        src = part_of[item] if k == 0 else place_of(item, index, c)
        return remote(src, place_of(item, index, c), send_o.at[item, k], recv_o.at[item, k], sibling)

    def publish(item):
        keep(item).start()
        for j in ORDER:
            spread(item, j).start()
        across(item, 0).start()

    def landed(item, j):
        ref = place_of(item, lax.rem(z + 4 - j, 4), c)
        remote(ref, ref, send_g.at[item, j - 1], recv_g.at[item, j - 1], sibling).wait_recv()

    def collect(item):
        for j in ORDER:
            landed(item, j)
            across(item, j).start()

    def arrive(item):
        for k in range(4):
            ref = place_of(item, lax.rem(z + 4 - k, 4), 1 - c)
            remote(ref, ref, send_o.at[item, k], recv_o.at[item, k], sibling).wait_recv()

    @pl.when(holds)
    def _():
        arrived(z3, DN)
        ds_[...] = summed(dd[quarter(z, 80)], dr)
        publish(DN)

    x_up().wait_recv()
    c1u[...] = (c1s[...].astype(F32) + c1t[...].astype(F32)).astype(BF)
    publish(C1)
    arrived(x3, C0)
    c03[...] = summed(c02[xl], c03r)
    publish(C0)

    arrived(y1, KV)
    for i in range(2):
        kv1[i] = summed(kv[i, y], [kv1r[j, i] for j in range(3)])
    for j in ORDER:
        x2(KV, j).start()
    arrived(y1, LO)
    for i in range(2):
        lo1[i] = summed(lo[i, y], [lo1r[j, i] for j in range(3)])
    for j in ORDER:
        x2(LO, j).start()
    arrived(z1)
    for i in range(2):
        for k in range(4):
            hi1[i, k] = summed(hi[i, k, quarter(z, 32)], [hi1r[j, i, k] for j in range(3)])
    for j in ORDER:
        y2(HI, j).start()
    arrived(x2, KV)
    kv2[...] = summed(kv1[xl], kv2r)
    for j in ORDER:
        z3(KV, j).start()
    arrived(x2, LO)
    lo2[...] = summed(lo1[xl], lo2r)
    for j in ORDER:
        z3(LO, j).start()
    arrived(y2, HI)
    for i in range(2):
        hi2[i] = summed(hi1[i, y], [hi2r[j, i] for j in range(3)])
    for j in ORDER:
        x3(HI, j).start()
    arrived(z3, KV)
    kv3[...] = summed(kv2[quarter(z, 32)], kv3r)
    publish(KV)
    arrived(z3, LO)
    lo3[...] = summed(lo2[quarter(z, 32)], lo3r)
    publish(LO)
    arrived(x3, HI)
    hi3[...] = summed(hi2[xl], hi3r)
    publish(HI)

    pl.when(holds)(lambda: collect(DN))
    for item in (C1, C0, KV, LO, HI):
        collect(item)
    pl.when(jnp.logical_not(holds))(lambda: arrive(DN))
    for item in (C1, C0, KV, LO, HI):
        arrive(item)

    for core in (0, 1):

        @pl.when(c == core)
        def _(core=core):
            for copy in trades(core):
                copy.wait_send()

    def settled(item):
        keep(item).wait()
        for j in (1, 2, 3):
            spread(item, j).wait_send()
        for k in range(4):
            across(item, k).wait_send()

    for j in (1, 2, 3):
        for make, key in (
            (y1, LO), (x2, LO), (z3, LO), (y1, KV), (x2, KV), (z3, KV), (y2, HI), (x3, HI), (y2, C0), (x3, C0),
        ):
            make(key, j).wait_send()
        z1(j).wait_send()
        y_up(j).wait_send()
    x_up().wait_send()
    for item in (LO, HI, KV, C0, C1):
        settled(item)

    @pl.when(holds)
    def _():
        for j in (1, 2, 3):
            z3(DN, j).wait_send()
        settled(DN)


def finish(*args):
    sem = pltpu.SemaphoreType.DMA
    vm = lambda *shape: pltpu.VMEM(shape, BF)

    def yxz(width):
        return [
            vm(2, PAD, width), vm(3, 2, PAD, width), vm(PAD, width), vm(3, PAD, width),
            vm(32, width), vm(3, 32, width),
        ]

    return pl.pallas_call(
        finish_kernel,
        name="finish",
        out_shape=(
            jax.ShapeDtypeStruct((2, PAD, WIDE), BF),
            jax.ShapeDtypeStruct((2, PAD, NARROW), BF),
            jax.ShapeDtypeStruct((2, PAD, KW), BF),
            jax.ShapeDtypeStruct((PAD, FF), BF),
            jax.ShapeDtypeStruct((PAD, FF), BF),
            jax.ShapeDtypeStruct((KW, D), BF),
        ),
        in_specs=[VM] * 9,
        out_specs=(ANY,) * 6,
        scratch_shapes=[
            vm(D, 2 * TOK), vm(D, 2 * TOK), vm(KW, 2 * TOK), vm(D, 2 * TOK),
            vm(2, 4, PAD, WIDE), vm(2, 4, PAD, NARROW), vm(2, 4, PAD, KW),
        ]
        + yxz(WIDE)
        + yxz(KW)
        + [
            vm(2, 4, 32, NARROW), vm(3, 2, 4, 32, NARROW), vm(2, 32, NARROW), vm(3, 2, 32, NARROW),
            vm(32, NARROW), vm(3, 32, NARROW),
        ]
        + [vm(3, 2, 32, FH), vm(2, 32, FH), vm(3, 32, FH), vm(32, FH)]
        + [vm(3, 32, FH), vm(32, FH), vm(32, FH), vm(32, FH)]
        + [vm(3, 80, D), vm(80, D)]
        + [sem((6, 3, 3)), sem((6, 3, 3)), sem((4,)), sem((4,)), sem((6, 3)), sem((6, 3)), sem((6, 4)), sem((6, 4)), sem((6,))],
        compiler_params=params(3),
    )(*args)


def norm_backward(stream, gain, incoming):
    scale = lax.rsqrt(jnp.mean(stream * stream, axis=0, keepdims=True) + norm_epsilon)
    normal = stream * scale
    gain_grad = jnp.sum(incoming * normal, axis=1)
    scaled = incoming * gain
    stream_grad = scale * (scaled - normal * jnp.mean(scaled * normal, axis=0, keepdims=True))
    return (stream_grad, gain_grad)


def adamw_update(weight, gradient, first, second, rate, decay):
    weight = weight.astype(F32)
    first_new = beta_first * first.astype(F32) + (1.0 - beta_first) * gradient
    second_new = beta_second * second.astype(F32) + (1.0 - beta_second) * gradient * gradient
    first_hat = first_new / (1.0 - beta_first**STEP)
    second_hat = second_new / (1.0 - beta_second**STEP)
    weight_new = weight - rate * (
        first_hat / (jnp.sqrt(second_hat) + adam_epsilon) + decay * weight
    )
    return (weight_new, first_new, second_new)


def body(
    tokens,
    cotangent,
    query_weight,
    keyval_weight,
    output_weight,
    gateup_weight,
    down_weight,
    norm_gains,
    query_first,
    keyval_first,
    output_first,
    gateup_first,
    down_first,
    gains_first,
    query_second,
    keyval_second,
    output_second,
    gateup_second,
    down_second,
    gains_second,
):
    ctx = lax.axis_index("ctx")
    core = lax.rem(ctx, 2)
    stream_t, dy_t = tokens[0].T, cotangent[0].T
    gain_tile = jnp.pad(norm_gains.astype(F32), ((0, 6), (0, 8)))
    qo_all, kv_all, gain_all, dy_all = gather_weights(
        jnp.stack([query_weight, output_weight]), keyval_weight, gain_tile, dy_t
    )
    gains = gain_all[:, :2, :ROWS].transpose(1, 0, 2).reshape(2, D, 1)
    query_full, output_full = qo_all[0].reshape(D, D), qo_all[1].reshape(D, D)
    key_full, value_full = kv_all[0].reshape(D, KW), kv_all[1].reshape(D, KW)

    positions = (ctx * TOK + jnp.arange(TOK, dtype=jnp.int32)).astype(F32)
    counter = jnp.arange(HALF, dtype=F32)
    frequency = 1.0 / rotary_base ** (counter * (2.0 / HEAD_WIDTH))
    angles = frequency[:, None] * positions[None, :]
    cosine, sine = jnp.cos(angles), jnp.sin(angles)

    query_low, attended_t, level, keys, one_t, middle_t, two_all, gu_all, dn_all = forward(
        stream_t, query_full, key_full, value_full, output_full, gains, cosine, sine, gateup_weight, down_weight
    )
    gate_full, up_full = gu_all[0].reshape(D, FH), gu_all[1].reshape(D, FH)
    down_full = dn_all.reshape(FH, D)
    both_dy = jnp.concatenate([dy_all[0], dy_all[1]], axis=1)
    both_two = jnp.concatenate([two_all[0], two_all[1]], axis=1)

    def dg(a, b, ca, cb):
        return lax.dot_general(a, b, (((ca,), (cb,)), ((), ())), preferred_element_type=F32)

    gate = dg(gate_full, both_two, 0, 0)
    upward = dg(up_full, both_two, 0, 0)
    sigmoid_gate = jax.nn.sigmoid(gate)
    hidden = (gate * sigmoid_gate * upward).astype(BF)
    down_part = dg(down_full, hidden, 0, 0)
    hidden_grad = dg(down_full, both_dy, 1, 0)
    gate_grad = (hidden_grad * upward * sigmoid_gate * (1.0 + gate * (1.0 - sigmoid_gate))).astype(BF)
    up_grad = (hidden_grad * gate * sigmoid_gate).astype(BF)
    two_part = dg(gate_full, gate_grad, 1, 0) + dg(up_full, up_grad, 1, 0)
    down_other, two_other = swap(5, down_part[:, TOK:], two_part[:, TOK:])
    result_t = (middle_t + down_part[:, :TOK] + down_other).astype(BF)
    two_grad = two_part[:, :TOK] + two_other
    incoming = dy_t.astype(F32)
    middle_norm_grad, gain_two_grad = norm_backward(middle_t, gains[1], two_grad)
    middle_grad = incoming + middle_norm_grad
    middle_low = middle_grad.astype(BF)
    attended_grad_t = dg(output_full, middle_low, 1, 0).astype(BF)
    query_back, keyval_back, gate_part, up_part, down_sum = backward(
        query_low, keys, level, attended_t, attended_grad_t, cosine, sine,
        both_two, gate_grad, up_grad, hidden, both_dy,
    )
    key_back, value_back = keyval_back[:KW], keyval_back[KW:]

    one_grad = dg(query_full, query_back, 1, 0) + dg(key_full, key_back, 1, 0) + dg(value_full, value_back, 1, 0)
    stream_norm_grad, gain_one_grad = norm_backward(stream_t.astype(F32), gains[0], one_grad)
    input_grad = middle_grad + stream_norm_grad
    grad_gains = jnp.stack([gain_one_grad, gain_two_grad]).reshape(2, 8, ROWS).transpose(1, 0, 2)
    gain_rows = jnp.pad(grad_gains, ((0, 0), (0, 6), (0, 256 - ROWS)))
    low, high, narrow, gate_sum, up_sum, down = finish(
        one_t, attended_t, middle_low, query_back, keyval_back, gain_rows, gate_part, up_part, down_sum
    )
    wide = jnp.concatenate([low, high], axis=2)
    gains_sum = low[0, ROWS : ROWS + 2, :ROWS].astype(F32) + low[1, ROWS : ROWS + 2, :ROWS].astype(F32)
    summed_rows = (
        wide[0, :ROWS].astype(F32),
        narrow[:, :ROWS].astype(F32),
        wide[1, :ROWS].astype(F32),
        jnp.stack([gate_sum[:ROWS], up_sum[:ROWS]]).astype(F32),
        down.astype(F32),
        gains_sum,
    )
    shards = (query_weight, keyval_weight, output_weight, gateup_weight, down_weight, norm_gains)
    firsts = (query_first, keyval_first, output_first, gateup_first, down_first, gains_first)
    seconds = (query_second, keyval_second, output_second, gateup_second, down_second, gains_second)
    rates = (matrix_rate,) * 5 + (gain_rate,)
    decays = (matrix_decay,) * 5 + (0.0,)
    updated = [
        adamw_update(shards[i], summed_rows[i], firsts[i], seconds[i], rates[i], decays[i])
        for i in range(6)
    ]
    return (
        result_t.T[None],
        input_grad.T[None],
        *[updated[i][0] for i in range(6)],
        *[updated[i][1] for i in range(6)],
        *[updated[i][2] for i in range(6)],
    )


def solution(mesh):
    row, mid = P("fsdp", None), P(None, "fsdp", None)
    weights = (row, mid, row, mid, row, P(None, "fsdp"))
    stream = P(("rep", "fsdp"), "ctx", None)
    return jax.shard_map(
        body,
        mesh=mesh,
        in_specs=(stream, stream) + weights * 3,
        out_specs=(stream, stream) + weights * 3,
        check_vma=False,
    )
```

```python
import functools

import jax
import jax.numpy as jnp
from jax import lax
from jax.experimental import pallas as pl
from jax.experimental.pallas import tpu as pltpu
from jax.sharding import PartitionSpec as P

QUERY_HEADS = 15
KEY_VALUE_HEADS = 5
GROUP = QUERY_HEADS // KEY_VALUE_HEADS
HEAD_WIDTH = 64
HALF = HEAD_WIDTH // 2
STEP = 10
TOK = 256
D = 960
KW = 320
FF = 2560
FH = FF // 2
ROWS = 120
PAD = 128
BF = jnp.bfloat16
F32 = jnp.float32
MESH = pl.DeviceIdType.MESH

norm_epsilon = 1e-05
rotary_base = 100000.0
beta_first = 0.9
beta_second = 0.95
adam_epsilon = 1e-08
matrix_rate = 0.06
matrix_decay = 0.1
gain_rate = 0.6
score_scale = HEAD_WIDTH ** (-0.5)

ANY = pl.BlockSpec(memory_space=pl.ANY)
VM = pl.BlockSpec(memory_space=pltpu.VMEM)


def place():
    f = lax.axis_index("fsdp")
    q = lax.axis_index("ctx")
    z = lax.axis_index("rep")
    return (q // 2) * 2 + f // 4, f % 4, z, q % 2


def at(x, y, z, core):
    x, y, z = lax.rem(x, 4), lax.rem(y, 4), lax.rem(z, 4)
    return {"rep": z, "fsdp": lax.rem(x, 2) * 4 + y, "ctx": (x // 2) * 2 + core}


def greet(devices):
    barrier = pltpu.get_barrier_semaphore()
    for device in devices:
        pl.semaphore_signal(barrier, inc=1, device_id=device, device_id_type=MESH)
    pl.semaphore_wait(barrier, len(devices))


def remote(src, dst, send, recv, device):
    return pltpu.make_async_remote_copy(
        src_ref=src, dst_ref=dst, send_sem=send, recv_sem=recv, device_id=device, device_id_type=MESH
    )


def params(number, vmem=56):
    return pltpu.CompilerParams(
        collective_id=number, has_side_effects=True, vmem_limit_bytes=vmem * 2**20
    )


def columns(total):
    return [(start, min(start + 256, total)) for start in range(0, total, 256)]


ORDER = (1, 3, 2)
SIDE = (1, 3, 3, 1)


def dot(a, b, ca, cb):
    return lax.dot_general(a, b, (((ca,), (cb,)), ((), ())), preferred_element_type=F32)


def forward_kernel(
    stream, cos, sin, qo, kv, gain, dy, gu, dn,
    q_low, att, lse, kv_out, one, mid, two_all, dy_all, gains_out, q_all, o_all, k_all, v_all, gate_all, up_all, dn_all,
    keys, wide, ones, two, qo_land, kv_land, gain_land,
    send, recv, send_y, send_x, recv_w, send_ay, send_ax, send_as, recv_a, recv_as, local,
):
    x, y, z, c = place()
    xl = lax.rem(x, 2)
    f = 4 * xl + y
    holds = c == xl
    me = 2 * (x // 2) + c
    sib_slot, far_slot, diag_slot = me + 1 - 2 * c, lax.rem(me + 2, 4), lax.rem(me + 2, 4) + 1 - 2 * c
    sibling, far = at(x, y, z, 1 - c), at(x + 2, y, z, c)
    greet([at(x, y + j, z, c) for j in (1, 2, 3)] + [at(x + j, y, z, c) for j in (1, 2, 3)] + [sibling])

    def column(k):
        return 4 * xl + lax.rem(y + k + 1, 4) if k < 3 else 4 * (1 - xl) + lax.rem(y + k - 3, 4)

    own_a = (qo.at[c], kv.at[c], gain)

    def slot_a(item, g, core):
        if item == 2:
            return gain_land.at[g]
        return (qo_land, kv_land)[item].at[core, g]

    def wait_a(item, k):
        ref = slot_a(item, column(k), c)
        remote(ref, ref, send_as.at[0, 0], recv_a.at[item, column(k)], sibling).wait_recv()

    def row_a(item, j):
        return remote(own_a[item], slot_a(item, f, c), send_ay.at[item, j - 1], recv_a.at[item, f], at(x, y + j, z, c))

    def side_a(item, j):
        g = 4 * xl + lax.rem(y + j, 4)
        return remote(
            own_a[item] if j == 0 else slot_a(item, g, c),
            slot_a(item, g, c),
            send_ax.at[item, j],
            recv_a.at[item, g],
            at(x + SIDE[j], y, z, c),
        )

    def sib_a(item, k):
        ref = slot_a(item, column(k), c)
        return remote(ref, ref, send_as.at[item, k], recv_as.at[item, column(k)], sibling)

    def take(item, k):
        wait_a(item, k)
        if k < 3:
            side_a(item, k + 1).start()
        if item < 2:
            sib_a(item, k).start()

    def taken(item):
        for k in range(7):
            ref = slot_a(item, column(k), 1 - c)
            remote(ref, ref, send_as.at[0, 0], recv_as.at[item, column(k)], sibling).wait_recv()

    lanes = pl.ds(pl.multiple_of(c * FH, 128), FH)
    own = (gu.at[0, :, lanes], gu.at[1, :, lanes], dn.at[0:160], dn.at[160:320])

    def slot(item, g):
        if item < 2:
            return (gate_all, up_all)[item].at[g]
        return dn_all.at[lax.rem(g, 4), 160 * (item - 2) : 160 * (item - 1)]

    def wait_slot(item, g):
        remote(slot(item, g), slot(item, g), send_x.at[0, 0], recv_w.at[item, g], sibling).wait_recv()

    def send_row(item, j):
        return remote(own[item], slot(item, f), send_y.at[item, j - 1], recv_w.at[item, f], at(x, y + j, z, c))

    def send_side(item, j):
        g = 4 * xl + lax.rem(y + j, 4)
        return remote(
            own[item] if j == 0 else slot(item, g),
            slot(item, g),
            send_x.at[item, j],
            recv_w.at[item, g],
            at(x + (1, 3, 1, 3)[item], y, z, c),
        )

    def pass_on(items, offsets):
        for item in items:
            for j in offsets:
                wait_slot(item, 4 * xl + lax.rem(y + j, 4))
                send_side(item, j).start()

    def pass_down(offsets):
        pl.when(holds)(lambda: pass_on((2, 3), offsets))

    for item in (2, 1, 0):
        side_a(item, 0).start()
        for j in ORDER:
            row_a(item, j).start()
    copies = [
        pltpu.make_async_copy(gain, gain_land.at[f], local.at[0]),
        pltpu.make_async_copy(kv, kv_land.at[:, f], local.at[1]),
        pltpu.make_async_copy(qo, qo_land.at[:, f], local.at[2]),
        pltpu.make_async_copy(own[0], gate_all.at[f], local.at[3]),
        pltpu.make_async_copy(own[1], up_all.at[f], local.at[8]),
        pltpu.make_async_copy(dy, dy_all.at[0], local.at[4]),
    ]
    for copy in copies:
        copy.start()
    own_down = pltpu.make_async_copy(dn, dn_all.at[y], local.at[5])
    pl.when(holds)(own_down.start)

    co, si = cos[...], sin[...]
    wide[...] = stream[...].astype(F32)
    scale = lax.rsqrt(jnp.sum(wide[...] ** 2, axis=0, keepdims=True) / D + norm_epsilon)

    for k in (0, 2):
        take(2, k)
        take(1, k)
    take(1, 3)
    wait_a(2, 3)
    for k in (0, 2):
        take(0, k)
    for j in ORDER:
        for item in (0, 1):
            send_row(item, j).start()

        @pl.when(holds)
        def _():
            for item in (2, 3):
                send_row(item, j).start()

    take(2, 1)
    take(1, 1)
    take(0, 3)
    for k in (4, 6, 5):
        wait_a(2, k)
        take(1, k)
    take(0, 1)

    for copy in copies[:3]:
        copy.wait()
    for g in range(8):
        tile = gain_land[g].T
        gains_out[0, ROWS * g : ROWS * (g + 1), :] = tile[:ROWS, 0:1]
        gains_out[1, ROWS * g : ROWS * (g + 1), :] = tile[:ROWS, 1:2]
    ones[...] = wide[...] * scale * gains_out[0]
    one[...] = ones[...].astype(BF)
    taken(1)

    def block(ref, g):
        return ref[ROWS * g : ROWS * (g + 1), :].astype(BF)

    def project(land, which, cols, source):
        total = dot(land[which, 0, :, cols], block(source, 0), 0, 0)
        for g in range(1, 8):
            total += dot(land[which, g, :, cols], block(source, g), 0, 0)
        return total

    key = project(kv_land, 0, slice(0, KW), ones)
    for h in range(KEY_VALUE_HEADS):
        a, b = key[64 * h : 64 * h + 32, :], key[64 * h + 32 : 64 * h + 64, :]
        keys[me, 64 * h : 64 * h + 32, :] = (a * co - b * si).astype(BF)
        keys[me, 64 * h + 32 : 64 * h + 64, :] = (b * co + a * si).astype(BF)
    keys[me, KW:, :] = project(kv_land, 1, slice(0, KW), ones).astype(BF)
    to_far = remote(keys.at[me], keys.at[me], send.at[0], recv.at[0], far)
    to_sib = remote(keys.at[me], keys.at[me], send.at[1], recv.at[1], sibling)
    to_far.start()
    to_sib.start()
    for k in (4, 6, 5):
        take(0, k)
    for item in (0, 1):
        send_side(item, 0).start()

    @pl.when(holds)
    def _():
        for item in (2, 3):
            send_side(item, 0).start()

    taken(0)
    exchange = remote(dy, dy_all.at[1], send.at[4], recv.at[4], sibling)
    exchange.start()
    keep_a = [
        pltpu.make_async_copy(qo_land.at[0], q_all, local.at[0]),
        pltpu.make_async_copy(qo_land.at[1], o_all, local.at[1]),
        pltpu.make_async_copy(kv_land.at[0], k_all, local.at[2]),
        pltpu.make_async_copy(kv_land.at[1], v_all, local.at[6]),
    ]
    for copy in keep_a:
        copy.start()
    for start, stop in columns(D):
        query = project(qo_land, 0, slice(start, stop), ones)
        for h in range(0, stop - start, 64):
            a, b = query[h : h + 32, :], query[h + 32 : h + 64, :]
            rows = start + h
            q_low[rows : rows + 32, :] = ((a * co - b * si).astype(BF) * score_scale).astype(BF)
            q_low[rows + 32 : rows + 64, :] = ((b * co + a * si).astype(BF) * score_scale).astype(BF)
    pass_on((0,), (1, 3))
    remote(keys.at[far_slot], keys.at[far_slot], send.at[0], recv.at[0], far).wait_recv()
    on = remote(keys.at[far_slot], keys.at[far_slot], send.at[2], recv.at[2], sibling)
    on.start()
    remote(keys.at[sib_slot], keys.at[sib_slot], send.at[1], recv.at[1], sibling).wait_recv()
    remote(keys.at[diag_slot], keys.at[diag_slot], send.at[2], recv.at[2], sibling).wait_recv()
    gap = lax.broadcasted_iota(jnp.int32, (TOK, TOK), 0) - lax.broadcasted_iota(jnp.int32, (TOK, TOK), 1)

    def head(h, carry):
        rows = pl.ds(pl.multiple_of(h * 64, 64), 64)
        g = h // GROUP
        krows = pl.ds(pl.multiple_of(g * 64, 64), 64)
        vrows = pl.ds(pl.multiple_of(KW + g * 64, 64), 64)
        qh = q_low[rows, :]
        s = []
        for j in range(4):
            part = dot(keys[j, krows, :], qh, 0, 0)
            s.append(jnp.where(gap <= 256 * (me - j), part, -1e30))
        top = jnp.max(jnp.maximum(jnp.maximum(s[0], s[1]), jnp.maximum(s[2], s[3])), axis=0, keepdims=True)
        e = [jnp.exp(part - top) for part in s]
        total = jnp.sum(e[0] + e[1] + (e[2] + e[3]), axis=0, keepdims=True)
        acc = dot(keys[0, vrows, :], e[0].astype(BF), 1, 0)
        for j in range(1, 4):
            acc += dot(keys[j, vrows, :], e[j].astype(BF), 1, 0)
        ones[rows, :] = acc / total
        lse[pl.ds(h, 1), 0, :] = top + jnp.log(total)
        pl.when(h == 1)(lambda: pass_on((1,), (1, 3)))
        pl.when(h == 4)(lambda: pass_down((1, 3)))
        pl.when(h == 9)(lambda: pass_on((0,), (2,)))
        pl.when(h == 13)(lambda: pass_on((1,), (2,)))
        return carry

    lax.fori_loop(0, QUERY_HEADS, head, 0)
    kv_out[...] = keys[...]
    att[...] = ones[...].astype(BF)

    square = jnp.zeros((1, TOK), F32)
    for start, stop in columns(D):
        part = wide[start:stop, :] + project(qo_land, 1, slice(start, stop), ones)
        mid[start:stop, :] = part
        square += jnp.sum(part * part, axis=0, keepdims=True)
    scale = lax.rsqrt(square / D + norm_epsilon)
    two[...] = (mid[...] * scale * gains_out[1]).astype(BF)
    keep = pltpu.make_async_copy(two, two_all.at[0], local.at[7])
    keep.start()
    trade = remote(two, two_all.at[1], send.at[3], recv.at[3], sibling)
    trade.start()
    pass_down((2,))

    for k in range(4):
        g = 4 * (1 - xl) + lax.rem(y + k, 4)
        for item in (0, 1):
            wait_slot(item, g)

        @pl.when(jnp.logical_not(holds))
        def _():
            for item in (2, 3):
                wait_slot(item, g)

    for copy in copies[3:] + keep_a + [keep]:
        copy.wait()
    trade.wait()
    exchange.wait()
    to_far.wait_send()
    to_sib.wait_send()
    on.wait_send()
    for item in (0, 1, 2):
        for j in ORDER:
            row_a(item, j).wait_send()
        for j in range(4):
            side_a(item, j).wait_send()
        if item < 2:
            for k in range(7):
                sib_a(item, k).wait_send()

    def sent(items):
        for item in items:
            for j in ORDER:
                send_row(item, j).wait_send()
            for j in range(4):
                send_side(item, j).wait_send()

    sent((0, 1))

    @pl.when(holds)
    def _():
        own_down.wait()
        sent((2, 3))


def forward(*args):
    sem = pltpu.SemaphoreType.DMA
    low = lambda *shape: jax.ShapeDtypeStruct(shape, BF)
    return pl.pallas_call(
        forward_kernel,
        name="forward",
        out_shape=(
            low(D, TOK),
            low(D, TOK),
            jax.ShapeDtypeStruct((16, 1, TOK), F32),
            low(4, 2 * KW, TOK),
            low(D, TOK),
            jax.ShapeDtypeStruct((D, TOK), F32),
            low(2, D, TOK),
            low(2, D, TOK),
            jax.ShapeDtypeStruct((2, D, 1), F32),
            low(8, ROWS, D),
            low(8, ROWS, D),
            low(8, ROWS, KW),
            low(8, ROWS, KW),
            low(8, ROWS, FH),
            low(8, ROWS, FH),
            low(4, KW, D),
        ),
        in_specs=[VM] * 3 + [ANY] * 6,
        out_specs=(VM,) * 6 + (ANY,) * 2 + (VM,) + (ANY,) * 7,
        scratch_shapes=[
            pltpu.VMEM((4, 2 * KW, TOK), BF),
            pltpu.VMEM((D, TOK), F32),
            pltpu.VMEM((D, TOK), F32),
            pltpu.VMEM((D, TOK), BF),
            pltpu.VMEM((2, 8, ROWS, D), BF),
            pltpu.VMEM((2, 8, ROWS, KW), BF),
            pltpu.VMEM((8, 8, 128), F32),
            sem((5,)),
            sem((5,)),
            sem((4, 3)),
            sem((4, 4)),
            sem((4, 8)),
            sem((3, 3)),
            sem((3, 4)),
            sem((2, 7)),
            sem((3, 8)),
            sem((2, 8)),
            sem((9,)),
        ],
        compiler_params=params(1),
    )(*args)


def summed(own, got, count=3):
    total = own.astype(F32)
    for i in range(count):
        total += got[i].astype(F32)
    return total.astype(BF)


def ring(x, y, z, c):
    along_x = [at(x + j, y, z, c) for j in (1, 2, 3)]
    along_y = [at(x, y + j, z, c) for j in (1, 2, 3)]
    along_z = [at(x, y, z + j, c) for j in (1, 2, 3)]
    return along_x, along_y, along_z


def quarter(index, size):
    return pl.ds(pl.multiple_of(lax.rem(index, 4) * size, 16), size)


def planes(value, extra):
    return [
        jnp.concatenate([value[ROWS * f : ROWS * (f + 1)], extra[f]], axis=0).astype(BF)
        for f in range(8)
    ]


def backward_kernel(
    q_low, keys, lse, att, cos, sin, two_all, dy_all, mid, gains, wg, wu, wd, wo,
    q_back, kv_back, c0_out, c1_out, d_out, result, mid_grad, mid_low, gain_grad,
    two, dy, gate_grad, up_grad, hidden, grad, down_part, down_got, two_part, two_got, send_s, recv_s,
    mine, got, far_got, acc, c0, c0r, c1, c1r, c1s, c1t, d, dr, ds_, dt,
    send, recv, send_z, recv_z, send_x, recv_x, send_t, recv_t, send_y, recv_y, send_d, recv_d,
):
    x, y, z, c = place()
    xl = lax.rem(x, 2)
    holds = c == xl
    me = 2 * (x // 2) + c
    far_slot = lax.rem(me + 2, 4)
    sib_slot = me + 1 - 2 * c
    diag_slot = far_slot + 1 - 2 * c
    sibling, far = at(x, y, z, 1 - c), at(x + 2, y, z, c)
    along_x, along_y, along_z = ring(x, y, z, c)
    greet(along_x + along_y + along_z + [sibling])
    co, si = cos[...], sin[...]
    nothing = [jnp.zeros((8, 256), F32)] * 8

    def c0_z(j):
        return remote(c0.at[:, :, quarter(z + j, 32)], c0r.at[j - 1], send_z.at[j - 1], recv_z.at[j - 1], along_z[j - 1])

    def c1_x(i):
        return remote(
            c1.at[1 - xl, :, :, 640 * i : 640 * (i + 1)], c1r.at[i], send_x.at[i], recv_x.at[i], along_x[2 * i]
        )

    def c1_z(j):
        return remote(c1s.at[:, quarter(z + j, 32)], c1t.at[j - 1], send_t.at[j - 1], recv_t.at[j - 1], along_z[j - 1])

    def d_y(j):
        return remote(d.at[lax.rem(y + j, 4)], dr.at[j - 1], send_y.at[j - 1], recv_y.at[j - 1], along_y[j - 1])

    def d_x(j):
        return remote(ds_, dt.at[j - 1], send_d.at[j - 1], recv_d.at[j - 1], along_x[j - 1])

    for i in (0, 1):
        two[:, TOK * i : TOK * (i + 1)] = two_all[i]
        dy[:, TOK * i : TOK * (i + 1)] = dy_all[i]
    for start, stop in columns(FH):
        gate = dot(wg[:, start:stop], two[...], 0, 0)
        up = dot(wu[:, start:stop], two[...], 0, 0)
        back = dot(wd[start:stop, :], dy[...], 1, 0)
        sigmoid = jax.nn.sigmoid(gate)
        silu = gate * sigmoid
        hidden[start:stop, :] = (silu * up).astype(BF)
        gate_grad[start:stop, :] = (back * up * sigmoid * (1.0 + gate * (1.0 - sigmoid))).astype(BF)
        up_grad[start:stop, :] = (back * silu).astype(BF)

    for start, stop in columns(FH):
        part = planes(dot(two[...], gate_grad[start:stop, :], 1, 1), nothing)
        for f in range(8):
            c0[f // 4, f % 4, :, start:stop] = part[f]
    for j in ORDER:
        c0_z(j).start()
    for start, stop in columns(D):
        part = dot(hidden[...], dy[start:stop, :], 1, 1).astype(BF)
        for k in range(4):
            d[k, :, start:stop] = part[KW * k : KW * (k + 1)]
    for j in ORDER:
        d_y(j).start()
    for start, stop in columns(FH):
        part = planes(dot(two[...], up_grad[start:stop, :], 1, 1), nothing)
        for f in range(8):
            c1[f // 4, f % 4, :, start:stop] = part[f]
    for i in (0, 1):
        c1_x(i).start()

    far_half = pl.ds(TOK, TOK)
    for start, stop in columns(D):
        two_part[start:stop, :] = dot(wg[start:stop, :], gate_grad[...], 1, 0) + dot(wu[start:stop, :], up_grad[...], 1, 0)
    trade_two = remote(two_part.at[:, far_half], two_got, send_s.at[0], recv_s.at[0], sibling)
    trade_two.start()
    for start, stop in columns(D):
        down_part[start:stop, :] = dot(wd[:, start:stop], hidden[...], 0, 0)
    trade_down = remote(down_part.at[:, far_half], down_got, send_s.at[1], recv_s.at[1], sibling)
    trade_down.start()
    middle = mid[...]
    scale = lax.rsqrt(jnp.sum(middle * middle, axis=0, keepdims=True) / D + norm_epsilon)
    trade_two.wait_recv()
    normal = middle * scale
    incoming = two_part[:, :TOK] + two_got[...]
    gain_grad[...] = jnp.sum(incoming * normal, axis=1, keepdims=True)
    scaled = incoming * gains[1]
    level_two = jnp.sum(scaled * normal, axis=0, keepdims=True) / D
    mid_grad[...] = dy_all[0].astype(F32) + scale * (scaled - normal * level_two)
    mid_low[...] = mid_grad[...].astype(BF)
    for start, stop in columns(D):
        grad[start:stop, :] = dot(wo[start:stop, :], mid_low[...], 1, 0).astype(BF)
    trade_down.wait_recv()
    result[...] = (middle + down_part[:, :TOK] + down_got[...]).astype(BF)

    def step_c1():
        for i in (0, 1):
            c1_x(i).wait_recv()
        for k in range(4):
            for i in (0, 1):
                lanes = slice(640 * i, 640 * (i + 1))
                c1s[k, :, lanes] = (c1[xl, k, :, lanes].astype(F32) + c1r[i, k].astype(F32)).astype(BF)
        for j in ORDER:
            c1_z(j).start()

    def step_d():
        for j in (1, 2, 3):
            d_y(j).wait_recv()
        ds_[...] = summed(d[y], dr)
        pl.when(holds)(lambda: d_x(2).start())

        @pl.when(jnp.logical_not(holds))
        def _():
            d_x(1).start()
            d_x(3).start()

    gap = lax.broadcasted_iota(jnp.int32, (TOK, TOK), 0) - lax.broadcasted_iota(jnp.int32, (TOK, TOK), 1)

    def group(g, carry):
        krows = pl.ds(pl.multiple_of(g * 64, 64), 64)
        vrows = pl.ds(pl.multiple_of(KW + g * 64, 64), 64)

        def head(t, inner):
            h = g * GROUP + t
            rows = pl.ds(pl.multiple_of(h * 64, 64), 64)
            qh, gh = q_low[rows, :], grad[rows, :]
            row_dot = jnp.sum(gh.astype(F32) * att[rows, :].astype(F32), axis=0, keepdims=True)
            level = lse[pl.ds(h, 1), 0, :]
            dq = jnp.zeros((64, TOK), F32)
            for j in range(4):
                s = dot(keys[j, krows, :], qh, 0, 0)
                s = jnp.where(gap <= 256 * (me - j), s, -1e30)
                p = jnp.exp(s - level)
                dp = dot(keys[j, vrows, :], gh, 0, 0)
                ds = (p * (dp - row_dot)).astype(BF)
                pb = p.astype(BF)
                dq += dot(keys[j, krows, :], ds, 1, 0)
                dk = dot(qh, ds, 1, 1)
                dv = dot(gh, pb, 1, 1)
                first = t == 0
                acc[j, 0] = jnp.where(first, dk, acc[j, 0] + dk)
                acc[j, 1] = jnp.where(first, dv, acc[j, 1] + dv)
            dq = dq * score_scale
            a, b = dq[:32], dq[32:]
            q_back[pl.ds(pl.multiple_of(h * 64, 32), 32), :] = (a * co + b * si).astype(BF)
            q_back[pl.ds(pl.multiple_of(h * 64 + 32, 32), 32), :] = (b * co - a * si).astype(BF)
            return inner

        lax.fori_loop(0, GROUP, head, 0)
        for j in range(4):
            mine[j, krows, :] = acc[j, 0].astype(BF)
            mine[j, vrows, :] = acc[j, 1].astype(BF)
        pl.when(g == 1)(step_c1)
        pl.when(g == 3)(step_d)
        return carry

    acc[...] = jnp.zeros_like(acc)
    lax.fori_loop(0, KEY_VALUE_HEADS, group, 0)
    to_sib_far = remote(mine.at[diag_slot], got.at[1], send.at[0], recv.at[0], sibling)
    to_sib = remote(mine.at[sib_slot], got.at[0], send.at[1], recv.at[1], sibling)
    to_sib_far.start()
    to_sib.start()
    to_sib_far.wait_recv()
    got[1] = (mine[far_slot].astype(F32) + got[1].astype(F32)).astype(BF)
    to_far = remote(got.at[1], far_got, send.at[2], recv.at[2], far)
    to_far.start()
    to_sib.wait_recv()

    @pl.when(holds)
    def _():
        for j in (1, 2, 3):
            d_x(j).wait_recv()
        d_out[...] = summed(ds_[...], dt)

    @pl.when(jnp.logical_not(holds))
    def _():
        d_out[...] = jnp.zeros_like(d_out)

    near = mine[me].astype(F32) + got[0].astype(F32)
    to_far.wait_recv()
    total = near + far_got[...].astype(F32)
    for h in range(KEY_VALUE_HEADS):
        a, b = total[64 * h : 64 * h + 32, :], total[64 * h + 32 : 64 * h + 64, :]
        kv_back[64 * h : 64 * h + 32, :] = (a * co + b * si).astype(BF)
        kv_back[64 * h + 32 : 64 * h + 64, :] = (b * co - a * si).astype(BF)
    kv_back[KW:, :] = total[KW:, :].astype(BF)
    for j in (1, 2, 3):
        c0_z(j).wait_recv()
    for i in (0, 1):
        for k in range(4):
            c0_out[i, k] = summed(c0[i, k, quarter(z, 32)], [c0r[j, i, k] for j in range(3)])
    for j in (1, 2, 3):
        c1_z(j).wait_recv()
    for k in range(4):
        c1_out[k] = summed(c1s[k, quarter(z, 32)], [c1t[j, k] for j in range(3)])

    trade_two.wait_send()
    trade_down.wait_send()
    to_sib_far.wait_send()
    to_sib.wait_send()
    to_far.wait_send()
    for j in (1, 2, 3):
        c0_z(j).wait_send()
        c1_z(j).wait_send()
        d_y(j).wait_send()
    for i in (0, 1):
        c1_x(i).wait_send()
    pl.when(holds)(lambda: d_x(2).wait_send())

    @pl.when(jnp.logical_not(holds))
    def _():
        d_x(1).wait_send()
        d_x(3).wait_send()


def backward(*args):
    sem = pltpu.SemaphoreType.DMA
    vm = lambda *shape: pltpu.VMEM(shape, BF)
    return pl.pallas_call(
        backward_kernel,
        name="backward",
        out_shape=(
            jax.ShapeDtypeStruct((D, TOK), BF),
            jax.ShapeDtypeStruct((2 * KW, TOK), BF),
            jax.ShapeDtypeStruct((2, 4, 32, FH), BF),
            jax.ShapeDtypeStruct((4, 32, FH), BF),
            jax.ShapeDtypeStruct((KW, D), BF),
            jax.ShapeDtypeStruct((D, TOK), BF),
            jax.ShapeDtypeStruct((D, TOK), F32),
            jax.ShapeDtypeStruct((D, TOK), BF),
            jax.ShapeDtypeStruct((D, 1), F32),
        ),
        in_specs=[VM] * 14,
        out_specs=(VM,) * 9,
        scratch_shapes=[
            vm(D, 2 * TOK), vm(D, 2 * TOK), vm(FH, 2 * TOK), vm(FH, 2 * TOK), vm(FH, 2 * TOK), vm(D, TOK),
            pltpu.VMEM((D, 2 * TOK), F32), pltpu.VMEM((D, TOK), F32),
            pltpu.VMEM((D, 2 * TOK), F32), pltpu.VMEM((D, TOK), F32),
            sem((2,)), sem((2,)),
            vm(4, 2 * KW, TOK), vm(2, 2 * KW, TOK), vm(2 * KW, TOK), pltpu.VMEM((4, 2, 64, TOK), F32),
            vm(2, 4, PAD, FH), vm(3, 2, 4, 32, FH),
            vm(2, 4, PAD, FH), vm(2, 4, PAD, 640), vm(4, PAD, FH), vm(3, 4, 32, FH),
            vm(4, KW, D), vm(3, KW, D), vm(KW, D), vm(3, KW, D),
        ]
        + [sem((3,))] * 4
        + [sem((2,))] * 2
        + [sem((3,))] * 6,
        compiler_params=params(2),
    )(*args)


WIDE, NARROW = 512, D - 512


def finish_kernel(
    one, att, mid, q_back, kv_back, c0, c1, dd, stream, mid_grad, gains, gain_two, wq, wk, wv,
    lo_sum, hi_sum, kv_sum, c0_sum, c1_sum, d_sum, in_grad,
    gain_cols,
    left, right, thin, both, lo, hi, kv,
    lo1, lo1r, lo2, lo2r, lo3, lo3r,
    kv1, kv1r, kv2, kv2r, kv3, kv3r,
    hi1, hi1r, hi2, hi2r, hi3, hi3r,
    c02r, c02, c03r, c03,
    c1r, c1s, c1t, c1u,
    dr, ds_,
    send, recv, send_s, recv_s, send_g, recv_g, send_o, recv_o, local,
):
    x, y, z, c = place()
    xl = lax.rem(x, 2)
    holds = c == xl
    sibling = at(x, y, z, 1 - c)
    along_x, along_y, along_z = ring(x, y, z, c)
    greet(along_x + along_y + along_z + [sibling])
    LO, HI, KV, C0, C1, DN = range(6)

    def trade(i, src, dst):
        return remote(src, dst, send_s.at[i], recv_s.at[i], sibling)

    far = slice(TOK, 2 * TOK)

    def trades(core):
        return [
            trade(0, att if core == 0 else one, left.at[:, far]),
            trade(1, mid if core == 0 else q_back, right.at[:, far]),
            trade(2, kv_back.at[KW:] if core == 0 else kv_back.at[:KW], thin.at[:, far]),
            trade(3, one, both.at[:, far]),
        ]

    def move(item, phase, j, src, dst, along):
        return remote(src, dst.at[j - 1], send.at[item, phase, j - 1], recv.at[item, phase, j - 1], along[j - 1])

    def y1(item, j):
        src, dst = {LO: (lo, lo1r), KV: (kv, kv1r)}[item]
        return move(item, 0, j, src.at[:, lax.rem(y + j, 4)], dst, along_y)

    def x2(item, j):
        src, dst = {LO: (lo1, lo2r), KV: (kv1, kv2r)}[item]
        return move(item, 1, j, src.at[xl if j == 2 else 1 - xl], dst, along_x)

    def z3(item, j):
        if item == DN:
            return move(item, 2, j, dd.at[quarter(z + j, 80)], dr, along_z)
        src, dst = {LO: (lo2, lo3r), KV: (kv2, kv3r)}[item]
        return move(item, 2, j, src.at[quarter(z + j, 32)], dst, along_z)

    def z1(j):
        return move(HI, 0, j, hi.at[:, :, quarter(z + j, 32)], hi1r, along_z)

    def y2(item, j):
        src, dst = {HI: (hi1, hi2r), C0: (c0, c02r)}[item]
        return move(item, 1, j, src.at[:, lax.rem(y + j, 4)], dst, along_y)

    def x3(item, j):
        src, dst = {HI: (hi2, hi3r), C0: (c02, c03r)}[item]
        return move(item, 2, j, src.at[xl if j == 2 else 1 - xl], dst, along_x)

    def y_up(j):
        return move(C1, 0, j, c1.at[lax.rem(y + j, 4)], c1r, along_y)

    def x_up():
        return remote(c1s, c1t, send.at[C1, 1, 0], recv.at[C1, 1, 0], along_x[1])

    for core in (0, 1):

        @pl.when(c == core)
        def _(core=core):
            for copy in trades(core):
                copy.start()

    for j in ORDER:
        y2(C0, j).start()
        y_up(j).start()

    @pl.when(holds)
    def _():
        for j in ORDER:
            z3(DN, j).start()

    near = slice(0, TOK)

    @pl.when(c == 0)
    def _():
        left[:, near] = one[...]
        right[:, near] = q_back[...]
        thin[:, near] = kv_back[:KW, :]

    @pl.when(c == 1)
    def _():
        left[:, near] = att[...]
        right[:, near] = mid[...]
        thin[:, near] = kv_back[KW:, :]

    both[:, near] = one[...]

    source = stream[...].astype(F32)
    scale = lax.rsqrt(jnp.sum(source * source, axis=0, keepdims=True) / D + norm_epsilon)
    normal = source * scale
    for start, stop in columns(D):
        in_grad[start:stop, :] = (
            dot(wq[start:stop, :], q_back[...], 1, 0)
            + dot(wk[start:stop, :], kv_back[:KW, :], 1, 0)
            + dot(wv[start:stop, :], kv_back[KW:, :], 1, 0)
        )
    incoming = in_grad[...]
    gain_cols[...] = jnp.sum(incoming * normal, axis=1, keepdims=True)
    scaled = incoming * gains[0]
    level = jnp.sum(scaled * normal, axis=0, keepdims=True) / D
    in_grad[...] = mid_grad[...] + scale * (scaled - normal * level)
    lane = lax.broadcasted_iota(jnp.int32, (PAD, 128), 1)
    gain = []
    for f in range(8):
        rows_f = slice(ROWS * f, ROWS * (f + 1))
        zeros = jnp.zeros((PAD - ROWS, 128), F32)
        first_col = jnp.concatenate([jnp.broadcast_to(gain_cols[rows_f, :], (ROWS, 128)), zeros], axis=0)
        second_col = jnp.concatenate([jnp.broadcast_to(gain_two[rows_f, :], (ROWS, 128)), zeros], axis=0)
        tile = jnp.where(lane == 0, first_col, jnp.where(lane == 1, second_col, 0.0)).T
        gain.append(jnp.concatenate([tile[:8], jnp.zeros((8, 128), F32)], axis=1))

    trade(3, one, both.at[:, far]).wait_recv()
    trade(2, kv_back.at[:KW], thin.at[:, far]).wait_recv()
    nothing = [jnp.zeros((8, KW), F32)] * 8
    part = planes(dot(both[...], thin[...], 1, 1), nothing)
    for f in range(8):
        kv[f // 4, f % 4] = part[f]
    for j in ORDER:
        y1(KV, j).start()
    trade(0, one, left.at[:, far]).wait_recv()
    trade(1, one, right.at[:, far]).wait_recv()
    for start, stop in ((256, 512), (0, 256), (512, 768), (768, D)):
        size = stop - start
        extra = [gain[f] if start == 0 else jnp.zeros((8, size), F32) for f in range(8)]
        part = planes(dot(left[...], right[start:stop, :], 1, 1), extra)
        for f in range(8):
            if start < WIDE:
                lo[f // 4, f % 4, :, start:stop] = part[f]
            else:
                hi[f // 4, f % 4, :, start - WIDE : stop - WIDE] = part[f]
        if start == 0:
            for j in ORDER:
                y1(LO, j).start()
    for j in ORDER:
        z1(j).start()

    def arrived(make, *key):
        for j in (1, 2, 3):
            make(*key, j).wait_recv()

    arrived(y2, C0)
    for i in range(2):
        c02[i] = summed(c0[i, y], [c02r[j, i] for j in range(3)])
    for j in ORDER:
        x3(C0, j).start()
    arrived(y_up)
    c1s[...] = summed(c1[y], c1r)
    x_up().start()

    part_of = {LO: lo3, HI: hi3, KV: kv3, C0: c03, C1: c1u, DN: ds_}

    def place_of(item, index, core):
        if item == DN:
            return d_sum.at[quarter(index, 80)]
        if item in (C0, C1):
            lanes = pl.ds(pl.multiple_of(FH * core, 128), FH)
            return (c0_sum if item == C0 else c1_sum).at[quarter(index, 32), lanes]
        return {LO: lo_sum, HI: hi_sum, KV: kv_sum}[item].at[core, quarter(index, 32)]

    def spread(item, j):
        return remote(
            part_of[item], place_of(item, z, c), send_g.at[item, j - 1], recv_g.at[item, j - 1], along_z[j - 1]
        )

    def keep(item):
        return pltpu.make_async_copy(part_of[item], place_of(item, z, c), local.at[item])

    def across(item, k):
        index = lax.rem(z + 4 - k, 4)
        src = part_of[item] if k == 0 else place_of(item, index, c)
        return remote(src, place_of(item, index, c), send_o.at[item, k], recv_o.at[item, k], sibling)

    def publish(item):
        keep(item).start()
        for j in ORDER:
            spread(item, j).start()
        across(item, 0).start()

    def landed(item, j):
        ref = place_of(item, lax.rem(z + 4 - j, 4), c)
        remote(ref, ref, send_g.at[item, j - 1], recv_g.at[item, j - 1], sibling).wait_recv()

    def collect(item):
        for j in ORDER:
            landed(item, j)
            across(item, j).start()

    def arrive(item):
        for k in range(4):
            ref = place_of(item, lax.rem(z + 4 - k, 4), 1 - c)
            remote(ref, ref, send_o.at[item, k], recv_o.at[item, k], sibling).wait_recv()

    @pl.when(holds)
    def _():
        arrived(z3, DN)
        ds_[...] = summed(dd[quarter(z, 80)], dr)
        publish(DN)

    x_up().wait_recv()
    c1u[...] = (c1s[...].astype(F32) + c1t[...].astype(F32)).astype(BF)
    publish(C1)
    arrived(x3, C0)
    c03[...] = summed(c02[xl], c03r)
    publish(C0)

    arrived(y1, KV)
    for i in range(2):
        kv1[i] = summed(kv[i, y], [kv1r[j, i] for j in range(3)])
    for j in ORDER:
        x2(KV, j).start()
    arrived(y1, LO)
    for i in range(2):
        lo1[i] = summed(lo[i, y], [lo1r[j, i] for j in range(3)])
    for j in ORDER:
        x2(LO, j).start()
    arrived(z1)
    for i in range(2):
        for k in range(4):
            hi1[i, k] = summed(hi[i, k, quarter(z, 32)], [hi1r[j, i, k] for j in range(3)])
    for j in ORDER:
        y2(HI, j).start()
    arrived(x2, KV)
    kv2[...] = summed(kv1[xl], kv2r)
    for j in ORDER:
        z3(KV, j).start()
    arrived(x2, LO)
    lo2[...] = summed(lo1[xl], lo2r)
    for j in ORDER:
        z3(LO, j).start()
    arrived(y2, HI)
    for i in range(2):
        hi2[i] = summed(hi1[i, y], [hi2r[j, i] for j in range(3)])
    for j in ORDER:
        x3(HI, j).start()
    arrived(z3, KV)
    kv3[...] = summed(kv2[quarter(z, 32)], kv3r)
    publish(KV)
    arrived(z3, LO)
    lo3[...] = summed(lo2[quarter(z, 32)], lo3r)
    publish(LO)
    arrived(x3, HI)
    hi3[...] = summed(hi2[xl], hi3r)
    publish(HI)

    pl.when(holds)(lambda: collect(DN))
    for item in (C1, C0, KV, LO, HI):
        collect(item)
    pl.when(jnp.logical_not(holds))(lambda: arrive(DN))
    for item in (C1, C0, KV, LO, HI):
        arrive(item)

    for core in (0, 1):

        @pl.when(c == core)
        def _(core=core):
            for copy in trades(core):
                copy.wait_send()

    def settled(item):
        keep(item).wait()
        for j in (1, 2, 3):
            spread(item, j).wait_send()
        for k in range(4):
            across(item, k).wait_send()

    for j in (1, 2, 3):
        for make, key in (
            (y1, LO), (x2, LO), (z3, LO), (y1, KV), (x2, KV), (z3, KV), (y2, HI), (x3, HI), (y2, C0), (x3, C0),
        ):
            make(key, j).wait_send()
        z1(j).wait_send()
        y_up(j).wait_send()
    x_up().wait_send()
    for item in (LO, HI, KV, C0, C1):
        settled(item)

    @pl.when(holds)
    def _():
        for j in (1, 2, 3):
            z3(DN, j).wait_send()
        settled(DN)


def finish(*args):
    sem = pltpu.SemaphoreType.DMA
    vm = lambda *shape: pltpu.VMEM(shape, BF)

    def yxz(width):
        return [
            vm(2, PAD, width), vm(3, 2, PAD, width), vm(PAD, width), vm(3, PAD, width),
            vm(32, width), vm(3, 32, width),
        ]

    return pl.pallas_call(
        finish_kernel,
        name="finish",
        out_shape=(
            jax.ShapeDtypeStruct((2, PAD, WIDE), BF),
            jax.ShapeDtypeStruct((2, PAD, NARROW), BF),
            jax.ShapeDtypeStruct((2, PAD, KW), BF),
            jax.ShapeDtypeStruct((PAD, FF), BF),
            jax.ShapeDtypeStruct((PAD, FF), BF),
            jax.ShapeDtypeStruct((KW, D), BF),
            jax.ShapeDtypeStruct((D, TOK), F32),
        ),
        in_specs=[VM] * 15,
        out_specs=(ANY,) * 6 + (VM,),
        scratch_shapes=[
            pltpu.VMEM((D, 1), F32),
            vm(D, 2 * TOK), vm(D, 2 * TOK), vm(KW, 2 * TOK), vm(D, 2 * TOK),
            vm(2, 4, PAD, WIDE), vm(2, 4, PAD, NARROW), vm(2, 4, PAD, KW),
        ]
        + yxz(WIDE)
        + yxz(KW)
        + [
            vm(2, 4, 32, NARROW), vm(3, 2, 4, 32, NARROW), vm(2, 32, NARROW), vm(3, 2, 32, NARROW),
            vm(32, NARROW), vm(3, 32, NARROW),
        ]
        + [vm(3, 2, 32, FH), vm(2, 32, FH), vm(3, 32, FH), vm(32, FH)]
        + [vm(3, 32, FH), vm(32, FH), vm(32, FH), vm(32, FH)]
        + [vm(3, 80, D), vm(80, D)]
        + [sem((6, 3, 3)), sem((6, 3, 3)), sem((4,)), sem((4,)), sem((6, 3)), sem((6, 3)), sem((6, 4)), sem((6, 4)), sem((6,))],
        compiler_params=params(3),
    )(*args)


def adamw_update(weight, gradient, first, second, rate, decay):
    weight = weight.astype(F32)
    first_new = beta_first * first.astype(F32) + (1.0 - beta_first) * gradient
    second_new = beta_second * second.astype(F32) + (1.0 - beta_second) * gradient * gradient
    first_hat = first_new / (1.0 - beta_first**STEP)
    second_hat = second_new / (1.0 - beta_second**STEP)
    weight_new = weight - rate * (
        first_hat / (jnp.sqrt(second_hat) + adam_epsilon) + decay * weight
    )
    return (weight_new, first_new, second_new)


def update_kernel(lo, hi, narrow, gate, up, down, *refs):
    state, new = refs[:18], refs[18:]

    def update(which, index, gradient, rate=matrix_rate, decay=matrix_decay):
        weight, first, second = (state[3 * which + i][index] for i in range(3))
        for i, value in enumerate(adamw_update(weight, gradient, first, second, rate, decay)):
            new[3 * which + i][index] = value

    for m, source in ((0, gate), (1, up)):
        update(3, m, source[...].astype(F32)[:ROWS])
    update(4, slice(None), down[...].astype(F32))

    @pl.when(pl.program_id(0) == 0)
    def _():
        for which, core in ((0, 0), (2, 1)):
            update(which, (slice(None), slice(0, WIDE)), lo[core].astype(F32)[:ROWS])
            update(which, (slice(None), slice(WIDE, D)), hi[core].astype(F32)[:ROWS])
        for m in (0, 1):
            update(1, m, narrow[m].astype(F32).T[:, :ROWS])
        gains = lo[0, 112:, :128].astype(F32) + lo[1, 112:, :128].astype(F32)
        update(5, slice(None), gains[8:10, :ROWS], gain_rate, 0.0)


def update_all(lo, hi, narrow, gate, up, down, state):
    steps = 5
    fixed = lambda a: pl.BlockSpec(a.shape, lambda i: (0,) * len(a.shape))
    sums = pl.BlockSpec((PAD, FF // steps), lambda i: (0, i))
    rows = pl.BlockSpec((KW // steps, D), lambda i: (i, 0))
    wide = pl.BlockSpec((2, ROWS, FF // steps), lambda i: (0, 0, i))
    specs = []
    for i, array in enumerate(state):
        specs.append(wide if i // 3 == 3 else rows if i // 3 == 4 else fixed(array))
    return pl.pallas_call(
        update_kernel,
        name="update",
        grid=(steps,),
        out_shape=tuple(jax.ShapeDtypeStruct(a.shape, F32) for a in state),
        in_specs=[fixed(lo), fixed(hi), fixed(narrow), sums, sums, rows] + specs,
        out_specs=tuple(specs),
        compiler_params=pltpu.CompilerParams(vmem_limit_bytes=40 * 2**20),
    )(lo, hi, narrow, gate, up, down, *state)


def body(
    tokens,
    cotangent,
    query_weight,
    keyval_weight,
    output_weight,
    gateup_weight,
    down_weight,
    norm_gains,
    query_first,
    keyval_first,
    output_first,
    gateup_first,
    down_first,
    gains_first,
    query_second,
    keyval_second,
    output_second,
    gateup_second,
    down_second,
    gains_second,
):
    ctx = lax.axis_index("ctx")
    core = lax.rem(ctx, 2)
    stream_t, dy_t = tokens[0].T, cotangent[0].T
    gain_tile = jnp.pad(norm_gains.astype(F32), ((0, 6), (0, 8)))
    positions = (ctx * TOK + jnp.arange(TOK, dtype=jnp.int32)).astype(F32)
    counter = jnp.arange(HALF, dtype=F32)
    frequency = 1.0 / rotary_base ** (counter * (2.0 / HEAD_WIDTH))
    angles = frequency[:, None] * positions[None, :]
    cosine, sine = jnp.cos(angles), jnp.sin(angles)

    (
        query_low, attended_t, level, keys, one_t, middle_t, two_all, dy_all, gains,
        query_all, output_all, key_all, value_all, gate_all, up_all, dn_all,
    ) = forward(
        stream_t, cosine, sine, jnp.stack([query_weight, output_weight]), keyval_weight, gain_tile, dy_t,
        gateup_weight, down_weight,
    )
    query_full, output_full = query_all.reshape(D, D), output_all.reshape(D, D)
    key_full, value_full = key_all.reshape(D, KW), value_all.reshape(D, KW)
    gate_full, up_full = gate_all.reshape(D, FH), up_all.reshape(D, FH)
    down_full = dn_all.reshape(FH, D)

    (
        query_back, keyval_back, gate_part, up_part, down_sum, result_t, middle_grad, middle_low, gain_two_grad,
    ) = backward(
        query_low, keys, level, attended_t, cosine, sine, two_all, dy_all, middle_t, gains,
        gate_full, up_full, down_full, output_full,
    )
    low, high, narrow, gate_sum, up_sum, down, input_grad = finish(
        one_t, attended_t, middle_low, query_back, keyval_back, gate_part, up_part, down_sum,
        stream_t, middle_grad, gains, gain_two_grad, query_full, key_full, value_full,
    )
    turned = lambda a: a.transpose(0, 2, 1)
    state = (
        query_weight, query_first, query_second,
        turned(keyval_weight), turned(keyval_first), turned(keyval_second),
        output_weight, output_first, output_second,
        gateup_weight, gateup_first, gateup_second,
        down_weight, down_first, down_second,
        norm_gains, gains_first, gains_second,
    )
    new = list(update_all(low, high, narrow, gate_sum, up_sum, down, state))
    new[3:6] = [turned(a) for a in new[3:6]]
    return (result_t.T[None], input_grad.T[None], *new[0::3], *new[1::3], *new[2::3])


def solution(mesh):
    row, mid = P("fsdp", None), P(None, "fsdp", None)
    weights = (row, mid, row, mid, row, P(None, "fsdp"))
    stream = P(("rep", "fsdp"), "ctx", None)
    return jax.shard_map(
        body,
        mesh=mesh,
        in_specs=(stream, stream) + weights * 3,
        out_specs=(stream, stream) + weights * 3,
        check_vma=False,
    )
```

```python
import functools

import jax
import jax.numpy as jnp
from jax import lax
from jax.experimental import pallas as pl
from jax.experimental.pallas import tpu as pltpu
from jax.sharding import PartitionSpec as P

QUERY_HEADS = 15
KEY_VALUE_HEADS = 5
GROUP = QUERY_HEADS // KEY_VALUE_HEADS
HEAD_WIDTH = 64
HALF = HEAD_WIDTH // 2
STEP = 10
TOK = 256
D = 960
KW = 320
FF = 2560
FH = FF // 2
ROWS = 120
PAD = 128
BF = jnp.bfloat16
F32 = jnp.float32
MESH = pl.DeviceIdType.MESH

norm_epsilon = 1e-05
rotary_base = 100000.0
beta_first = 0.9
beta_second = 0.95
adam_epsilon = 1e-08
matrix_rate = 0.06
matrix_decay = 0.1
gain_rate = 0.6
score_scale = HEAD_WIDTH ** (-0.5)

ANY = pl.BlockSpec(memory_space=pl.ANY)
VM = pl.BlockSpec(memory_space=pltpu.VMEM)


def place():
    f = lax.axis_index("fsdp")
    q = lax.axis_index("ctx")
    z = lax.axis_index("rep")
    return (q // 2) * 2 + f // 4, f % 4, z, q % 2


def at(x, y, z, core):
    x, y, z = lax.rem(x, 4), lax.rem(y, 4), lax.rem(z, 4)
    return {"rep": z, "fsdp": lax.rem(x, 2) * 4 + y, "ctx": (x // 2) * 2 + core}


def greet(devices):
    barrier = pltpu.get_barrier_semaphore()
    for device in devices:
        pl.semaphore_signal(barrier, inc=1, device_id=device, device_id_type=MESH)
    pl.semaphore_wait(barrier, len(devices))


def remote(src, dst, send, recv, device):
    return pltpu.make_async_remote_copy(
        src_ref=src, dst_ref=dst, send_sem=send, recv_sem=recv, device_id=device, device_id_type=MESH
    )


def params(number, vmem=56):
    return pltpu.CompilerParams(
        collective_id=number, has_side_effects=True, vmem_limit_bytes=vmem * 2**20
    )


def columns(total):
    return [(start, min(start + 256, total)) for start in range(0, total, 256)]


ORDER = (1, 3, 2)
SIDE = (1, 3, 3, 1)


def dot(a, b, ca, cb):
    return lax.dot_general(a, b, (((ca,), (cb,)), ((), ())), preferred_element_type=F32)


def forward_kernel(
    stream, cos, sin, qw, ow, kv, gain, dy, gu, dn,
    q_low, att, lse, kv_out, one, mid, two_all, dy_all, gains_out, q_all, o_all, k_all, v_all, gate_all, up_all, dn_all,
    keys, wide, ones, two, qo_land, kv_land, gain_land,
    send, recv, send_y, send_x, recv_w, send_ay, send_ax, send_as, recv_a, recv_as, local,
):
    x, y, z, c = place()
    xl = lax.rem(x, 2)
    f = 4 * xl + y
    holds = c == xl
    me = 2 * (x // 2) + c
    sib_slot, far_slot, diag_slot = me + 1 - 2 * c, lax.rem(me + 2, 4), lax.rem(me + 2, 4) + 1 - 2 * c
    sibling, far = at(x, y, z, 1 - c), at(x + 2, y, z, c)
    greet([at(x, y + j, z, c) for j in (1, 2, 3)] + [at(x + j, y, z, c) for j in (1, 2, 3)] + [sibling])

    def column(k):
        return 4 * xl + lax.rem(y + k + 1, 4) if k < 3 else 4 * (1 - xl) + lax.rem(y + k - 3, 4)

    def own_a(item):
        return (None, kv.at[c], gain)[item]

    def by_core(item, make):
        if item:
            make(own_a(item))
        else:
            pl.when(c == 0)(lambda: make(qw))
            pl.when(c == 1)(lambda: make(ow))

    def slot_a(item, g, core):
        if item == 2:
            return gain_land.at[g]
        return (qo_land, kv_land)[item].at[core, g]

    def wait_a(item, k):
        ref = slot_a(item, column(k), c)
        remote(ref, ref, send_as.at[0, 0], recv_a.at[item, column(k)], sibling).wait_recv()

    def row_a(item, j, source=None):
        source = slot_a(item, f, c) if source is None else source
        return remote(source, slot_a(item, f, c), send_ay.at[item, j - 1], recv_a.at[item, f], at(x, y + j, z, c))

    def side_a(item, j, source=None):
        g = 4 * xl + lax.rem(y + j, 4)
        return remote(
            slot_a(item, g, c) if source is None else source,
            slot_a(item, g, c),
            send_ax.at[item, j],
            recv_a.at[item, g],
            at(x + SIDE[j], y, z, c),
        )

    def sib_a(item, k):
        ref = slot_a(item, column(k), c)
        return remote(ref, ref, send_as.at[item, k], recv_as.at[item, column(k)], sibling)

    def take(item, k):
        wait_a(item, k)
        if k < 3:
            side_a(item, k + 1).start()
        if item < 2:
            sib_a(item, k).start()

    def taken(item):
        for k in range(7):
            ref = slot_a(item, column(k), 1 - c)
            remote(ref, ref, send_as.at[0, 0], recv_as.at[item, column(k)], sibling).wait_recv()

    lanes = pl.ds(pl.multiple_of(c * FH, 128), FH)
    own = (gu.at[0, :, lanes], gu.at[1, :, lanes], dn.at[0:160], dn.at[160:320])

    def slot(item, g):
        if item < 2:
            return (gate_all, up_all)[item].at[g]
        return dn_all.at[lax.rem(g, 4), 160 * (item - 2) : 160 * (item - 1)]

    def wait_slot(item, g):
        remote(slot(item, g), slot(item, g), send_x.at[0, 0], recv_w.at[item, g], sibling).wait_recv()

    def send_row(item, j):
        return remote(own[item], slot(item, f), send_y.at[item, j - 1], recv_w.at[item, f], at(x, y + j, z, c))

    def send_side(item, j):
        g = 4 * xl + lax.rem(y + j, 4)
        return remote(
            own[item] if j == 0 else slot(item, g),
            slot(item, g),
            send_x.at[item, j],
            recv_w.at[item, g],
            at(x + (1, 3, 1, 3)[item], y, z, c),
        )

    def pass_on(items, offsets):
        for item in items:
            for j in offsets:
                wait_slot(item, 4 * xl + lax.rem(y + j, 4))
                send_side(item, j).start()

    def pass_down(offsets):
        pl.when(holds)(lambda: pass_on((2, 3), offsets))

    for item in (2, 1, 0):

        def launch(source, item=item):
            side_a(item, 0, source).start()
            for j in ORDER:
                row_a(item, j, source).start()

        by_core(item, launch)
    copies = [
        pltpu.make_async_copy(gain, gain_land.at[f], local.at[0]),
        pltpu.make_async_copy(kv, kv_land.at[:, f], local.at[1]),
        pltpu.make_async_copy(qw, qo_land.at[0, f], local.at[2]),
        pltpu.make_async_copy(ow, qo_land.at[1, f], local.at[9]),
        pltpu.make_async_copy(own[0], gate_all.at[f], local.at[3]),
        pltpu.make_async_copy(own[1], up_all.at[f], local.at[8]),
        pltpu.make_async_copy(dy, dy_all.at[0], local.at[4]),
    ]
    for copy in copies:
        copy.start()
    own_down = pltpu.make_async_copy(dn, dn_all.at[y], local.at[5])
    pl.when(holds)(own_down.start)

    co, si = cos[...], sin[...]
    wide[...] = stream[...].astype(F32)
    scale = lax.rsqrt(jnp.sum(wide[...] ** 2, axis=0, keepdims=True) / D + norm_epsilon)

    for k in (0, 2):
        take(2, k)
        take(1, k)
    take(1, 3)
    wait_a(2, 3)
    for k in (0, 2):
        take(0, k)
    for j in ORDER:
        for item in (0, 1):
            send_row(item, j).start()

        @pl.when(holds)
        def _():
            for item in (2, 3):
                send_row(item, j).start()

    take(2, 1)
    take(1, 1)
    take(0, 3)
    for k in (4, 6, 5):
        wait_a(2, k)
        take(1, k)
    take(0, 1)

    for copy in copies[:4]:
        copy.wait()
    for g in range(8):
        tile = gain_land[g].T
        gains_out[0, ROWS * g : ROWS * (g + 1), :] = tile[:ROWS, 0:1]
        gains_out[1, ROWS * g : ROWS * (g + 1), :] = tile[:ROWS, 1:2]
    ones[...] = wide[...] * scale * gains_out[0]
    one[...] = ones[...].astype(BF)
    taken(1)

    def block(ref, g):
        return ref[ROWS * g : ROWS * (g + 1), :].astype(BF)

    def project(land, which, cols, source):
        total = dot(land[which, 0, :, cols], block(source, 0), 0, 0)
        for g in range(1, 8):
            total += dot(land[which, g, :, cols], block(source, g), 0, 0)
        return total

    key = project(kv_land, 0, slice(0, KW), ones)
    for h in range(KEY_VALUE_HEADS):
        a, b = key[64 * h : 64 * h + 32, :], key[64 * h + 32 : 64 * h + 64, :]
        keys[me, 64 * h : 64 * h + 32, :] = (a * co - b * si).astype(BF)
        keys[me, 64 * h + 32 : 64 * h + 64, :] = (b * co + a * si).astype(BF)
    keys[me, KW:, :] = project(kv_land, 1, slice(0, KW), ones).astype(BF)
    to_far = remote(keys.at[me], keys.at[me], send.at[0], recv.at[0], far)
    to_sib = remote(keys.at[me], keys.at[me], send.at[1], recv.at[1], sibling)
    to_far.start()
    to_sib.start()
    for k in (4, 6, 5):
        take(0, k)
    for item in (0, 1):
        send_side(item, 0).start()

    @pl.when(holds)
    def _():
        for item in (2, 3):
            send_side(item, 0).start()

    taken(0)
    exchange = remote(dy, dy_all.at[1], send.at[4], recv.at[4], sibling)
    exchange.start()
    keep_a = [
        pltpu.make_async_copy(qo_land.at[0], q_all, local.at[0]),
        pltpu.make_async_copy(qo_land.at[1], o_all, local.at[1]),
        pltpu.make_async_copy(kv_land.at[0], k_all, local.at[2]),
        pltpu.make_async_copy(kv_land.at[1], v_all, local.at[6]),
    ]
    for copy in keep_a:
        copy.start()
    for start, stop in columns(D):
        query = project(qo_land, 0, slice(start, stop), ones)
        for h in range(0, stop - start, 64):
            a, b = query[h : h + 32, :], query[h + 32 : h + 64, :]
            rows = start + h
            q_low[rows : rows + 32, :] = ((a * co - b * si).astype(BF) * score_scale).astype(BF)
            q_low[rows + 32 : rows + 64, :] = ((b * co + a * si).astype(BF) * score_scale).astype(BF)
    pass_on((0,), (1, 3))
    remote(keys.at[far_slot], keys.at[far_slot], send.at[0], recv.at[0], far).wait_recv()
    on = remote(keys.at[far_slot], keys.at[far_slot], send.at[2], recv.at[2], sibling)
    on.start()
    remote(keys.at[sib_slot], keys.at[sib_slot], send.at[1], recv.at[1], sibling).wait_recv()
    remote(keys.at[diag_slot], keys.at[diag_slot], send.at[2], recv.at[2], sibling).wait_recv()
    gap = lax.broadcasted_iota(jnp.int32, (TOK, TOK), 0) - lax.broadcasted_iota(jnp.int32, (TOK, TOK), 1)

    def head(h, carry):
        rows = pl.ds(pl.multiple_of(h * 64, 64), 64)
        g = h // GROUP
        krows = pl.ds(pl.multiple_of(g * 64, 64), 64)
        vrows = pl.ds(pl.multiple_of(KW + g * 64, 64), 64)
        qh = q_low[rows, :]
        s = []
        for j in range(4):
            part = dot(keys[j, krows, :], qh, 0, 0)
            s.append(jnp.where(gap <= 256 * (me - j), part, -1e30))
        top = jnp.max(jnp.maximum(jnp.maximum(s[0], s[1]), jnp.maximum(s[2], s[3])), axis=0, keepdims=True)
        e = [jnp.exp(part - top) for part in s]
        total = jnp.sum(e[0] + e[1] + (e[2] + e[3]), axis=0, keepdims=True)
        acc = dot(keys[0, vrows, :], e[0].astype(BF), 1, 0)
        for j in range(1, 4):
            acc += dot(keys[j, vrows, :], e[j].astype(BF), 1, 0)
        ones[rows, :] = acc / total
        lse[pl.ds(h, 1), 0, :] = top + jnp.log(total)
        pl.when(h == 1)(lambda: pass_on((1,), (1, 3)))
        pl.when(h == 4)(lambda: pass_down((1, 3)))
        pl.when(h == 9)(lambda: pass_on((0,), (2,)))
        pl.when(h == 13)(lambda: pass_on((1,), (2,)))
        return carry

    lax.fori_loop(0, QUERY_HEADS, head, 0)
    kv_out[...] = keys[...]
    att[...] = ones[...].astype(BF)

    square = jnp.zeros((1, TOK), F32)
    for start, stop in columns(D):
        part = wide[start:stop, :] + project(qo_land, 1, slice(start, stop), ones)
        mid[start:stop, :] = part
        square += jnp.sum(part * part, axis=0, keepdims=True)
    scale = lax.rsqrt(square / D + norm_epsilon)
    two[...] = (mid[...] * scale * gains_out[1]).astype(BF)
    keep = pltpu.make_async_copy(two, two_all.at[0], local.at[7])
    keep.start()
    trade = remote(two, two_all.at[1], send.at[3], recv.at[3], sibling)
    trade.start()
    pass_down((2,))

    for k in range(4):
        g = 4 * (1 - xl) + lax.rem(y + k, 4)
        for item in (0, 1):
            wait_slot(item, g)

        @pl.when(jnp.logical_not(holds))
        def _():
            for item in (2, 3):
                wait_slot(item, g)

    for copy in copies[4:] + keep_a + [keep]:
        copy.wait()
    trade.wait()
    exchange.wait()
    to_far.wait_send()
    to_sib.wait_send()
    on.wait_send()
    for item in (0, 1, 2):
        for j in ORDER:
            row_a(item, j).wait_send()
        for j in range(4):
            side_a(item, j).wait_send()
        if item < 2:
            for k in range(7):
                sib_a(item, k).wait_send()

    def sent(items):
        for item in items:
            for j in ORDER:
                send_row(item, j).wait_send()
            for j in range(4):
                send_side(item, j).wait_send()

    sent((0, 1))

    @pl.when(holds)
    def _():
        own_down.wait()
        sent((2, 3))


def forward(*args):
    sem = pltpu.SemaphoreType.DMA
    low = lambda *shape: jax.ShapeDtypeStruct(shape, BF)
    return pl.pallas_call(
        forward_kernel,
        name="forward",
        out_shape=(
            low(D, TOK),
            low(D, TOK),
            jax.ShapeDtypeStruct((16, 1, TOK), F32),
            low(4, 2 * KW, TOK),
            low(D, TOK),
            jax.ShapeDtypeStruct((D, TOK), F32),
            low(2, D, TOK),
            low(2, D, TOK),
            jax.ShapeDtypeStruct((2, D, 1), F32),
            low(8, ROWS, D),
            low(8, ROWS, D),
            low(8, ROWS, KW),
            low(8, ROWS, KW),
            low(8, ROWS, FH),
            low(8, ROWS, FH),
            low(4, KW, D),
        ),
        in_specs=[VM] * 3 + [ANY] * 7,
        out_specs=(VM,) * 6 + (ANY,) * 2 + (VM,) + (ANY,) * 7,
        scratch_shapes=[
            pltpu.VMEM((4, 2 * KW, TOK), BF),
            pltpu.VMEM((D, TOK), F32),
            pltpu.VMEM((D, TOK), F32),
            pltpu.VMEM((D, TOK), BF),
            pltpu.VMEM((2, 8, ROWS, D), BF),
            pltpu.VMEM((2, 8, ROWS, KW), BF),
            pltpu.VMEM((8, 8, 128), F32),
            sem((5,)),
            sem((5,)),
            sem((4, 3)),
            sem((4, 4)),
            sem((4, 8)),
            sem((3, 3)),
            sem((3, 4)),
            sem((2, 7)),
            sem((3, 8)),
            sem((2, 8)),
            sem((10,)),
        ],
        compiler_params=params(1),
    )(*args)


def summed(own, got, count=3):
    total = own.astype(F32)
    for i in range(count):
        total += got[i].astype(F32)
    return total.astype(BF)


def ring(x, y, z, c):
    along_x = [at(x + j, y, z, c) for j in (1, 2, 3)]
    along_y = [at(x, y + j, z, c) for j in (1, 2, 3)]
    along_z = [at(x, y, z + j, c) for j in (1, 2, 3)]
    return along_x, along_y, along_z


def quarter(index, size):
    return pl.ds(pl.multiple_of(lax.rem(index, 4) * size, 16), size)


def planes(value, extra):
    return [
        jnp.concatenate([value[ROWS * f : ROWS * (f + 1)], extra[f]], axis=0).astype(BF)
        for f in range(8)
    ]


def backward_kernel(
    q_low, keys, lse, att, cos, sin, two_all, dy_all, mid, gains, wg, wu, wd, wo,
    q_back, kv_back, c0_out, c1_out, c1y_out, d_out, result, mid_grad, mid_low, gain_grad,
    two, dy, gate_grad, up_grad, hidden, grad, down_part, down_got, two_part, two_got, send_s, recv_s,
    mine, got, far_got, acc, c0, c0r, c1, c1r, c1s, c1t, c1u, d, dr, ds_, dt,
    send, recv, send_z, recv_z, send_x, recv_x, send_t, recv_t, send_u, recv_u, send_y, recv_y, send_d, recv_d,
):
    x, y, z, c = place()
    xl = lax.rem(x, 2)
    holds = c == xl
    me = 2 * (x // 2) + c
    far_slot = lax.rem(me + 2, 4)
    sib_slot = me + 1 - 2 * c
    diag_slot = far_slot + 1 - 2 * c
    sibling, far = at(x, y, z, 1 - c), at(x + 2, y, z, c)
    along_x, along_y, along_z = ring(x, y, z, c)
    greet(along_x + along_y + along_z + [sibling])
    co, si = cos[...], sin[...]
    nothing = {size: [jnp.zeros((8, size), F32)] * 8 for size in (128, 256)}

    halves = (slice(0, 640), slice(640, FH))

    def c0_z(i, j):
        return remote(
            c0.at[i, :, :, quarter(z + j, 32)], c0r.at[j - 1, i], send_z.at[i, j - 1], recv_z.at[i, j - 1], along_z[j - 1]
        )

    def c1_x(i):
        return remote(c1.at[i, 1 - xl], c1r.at[i], send_x.at[i], recv_x.at[i], along_x[2 * i])

    def c1_z(j):
        return remote(c1s.at[0, :, quarter(z + j, 32)], c1t.at[j - 1], send_t.at[j - 1], recv_t.at[j - 1], along_z[j - 1])

    def c1_y(j):
        return remote(c1s.at[1, lax.rem(y + j, 4)], c1u.at[j - 1], send_u.at[j - 1], recv_u.at[j - 1], along_y[j - 1])

    def d_y(j):
        return remote(d.at[lax.rem(y + j, 4)], dr.at[j - 1], send_y.at[j - 1], recv_y.at[j - 1], along_y[j - 1])

    def d_block(k):
        for j in (1, 2, 3):
            pl.when(lax.rem(y + j, 4) == k)(lambda j=j: d_y(j).start())

    def d_x(i):
        return remote(ds_.at[160 * i : 160 * (i + 1)], dt.at[i], send_d.at[i], recv_d.at[i], along_x[2 * i])

    for i in (0, 1):
        two[:, TOK * i : TOK * (i + 1)] = two_all[i]
        dy[:, TOK * i : TOK * (i + 1)] = dy_all[i]
    for i, half in enumerate(halves):
        for start, stop in ((half.start, half.start + 256), (half.start + 256, half.start + 512), (half.start + 512, half.stop)):
            gate = dot(wg[:, start:stop], two[...], 0, 0)
            up = dot(wu[:, start:stop], two[...], 0, 0)
            back = dot(wd[start:stop, :], dy[...], 1, 0)
            sigmoid = jax.nn.sigmoid(gate)
            silu = gate * sigmoid
            hidden[start:stop, :] = (silu * up).astype(BF)
            gate_grad[start:stop, :] = (back * up * sigmoid * (1.0 + gate * (1.0 - sigmoid))).astype(BF)
            up_grad[start:stop, :] = (back * silu).astype(BF)
        for start, stop in columns(D):
            part = dot(hidden[half, :], dy[start:stop, :], 1, 1).astype(BF)
            d[2 * i, :, start:stop] = part[:KW]
            d[2 * i + 1, :, start:stop] = part[KW:]
        d_block(2 * i)
        d_block(2 * i + 1)
        for source, into in ((gate_grad, c0), (up_grad, c1)):
            for start, stop in ((0, 256), (256, 512), (512, 640)):
                part = planes(dot(two[...], source[half.start + start : half.start + stop, :], 1, 1), nothing[stop - start])
                for f in range(8):
                    into[i, f // 4, f % 4, :, start:stop] = part[f]
            if into is c0:
                for j in ORDER:
                    c0_z(i, j).start()
            else:
                c1_x(i).start()
    far_half = pl.ds(TOK, TOK)
    for start, stop in columns(D):
        two_part[start:stop, :] = dot(wg[start:stop, :], gate_grad[...], 1, 0) + dot(wu[start:stop, :], up_grad[...], 1, 0)
    trade_two = remote(two_part.at[:, far_half], two_got, send_s.at[0], recv_s.at[0], sibling)
    trade_two.start()
    for start, stop in columns(D):
        down_part[start:stop, :] = dot(wd[:, start:stop], hidden[...], 0, 0)
    trade_down = remote(down_part.at[:, far_half], down_got, send_s.at[1], recv_s.at[1], sibling)
    trade_down.start()
    middle = mid[...]
    scale = lax.rsqrt(jnp.sum(middle * middle, axis=0, keepdims=True) / D + norm_epsilon)
    trade_two.wait_recv()
    normal = middle * scale
    incoming = two_part[:, :TOK] + two_got[...]
    gain_grad[...] = jnp.sum(incoming * normal, axis=1, keepdims=True)
    scaled = incoming * gains[1]
    level_two = jnp.sum(scaled * normal, axis=0, keepdims=True) / D
    mid_grad[...] = dy_all[0].astype(F32) + scale * (scaled - normal * level_two)
    mid_low[...] = mid_grad[...].astype(BF)
    for start, stop in columns(D):
        grad[start:stop, :] = dot(wo[start:stop, :], mid_low[...], 1, 0).astype(BF)
    trade_down.wait_recv()
    result[...] = (middle + down_part[:, :TOK] + down_got[...]).astype(BF)

    def step_c1():
        for i in (0, 1):
            c1_x(i).wait_recv()
            for k in range(4):
                c1s[i, k] = (c1[i, xl, k].astype(F32) + c1r[i, k].astype(F32)).astype(BF)
            for j in ORDER:
                (c1_z, c1_y)[i](j).start()

    def step_d():
        for j in (1, 2, 3):
            d_y(j).wait_recv()
        ds_[...] = summed(d[y], dr)

        @pl.when(jnp.logical_not(holds))
        def _():
            d_x(0).start()
            d_x(1).start()

    gap = lax.broadcasted_iota(jnp.int32, (TOK, TOK), 0) - lax.broadcasted_iota(jnp.int32, (TOK, TOK), 1)

    def group(g, carry):
        krows = pl.ds(pl.multiple_of(g * 64, 64), 64)
        vrows = pl.ds(pl.multiple_of(KW + g * 64, 64), 64)

        def head(t, inner):
            h = g * GROUP + t
            rows = pl.ds(pl.multiple_of(h * 64, 64), 64)
            qh, gh = q_low[rows, :], grad[rows, :]
            row_dot = jnp.sum(gh.astype(F32) * att[rows, :].astype(F32), axis=0, keepdims=True)
            level = lse[pl.ds(h, 1), 0, :]
            dq = jnp.zeros((64, TOK), F32)
            for j in range(4):
                s = dot(keys[j, krows, :], qh, 0, 0)
                s = jnp.where(gap <= 256 * (me - j), s, -1e30)
                p = jnp.exp(s - level)
                dp = dot(keys[j, vrows, :], gh, 0, 0)
                ds = (p * (dp - row_dot)).astype(BF)
                pb = p.astype(BF)
                dq += dot(keys[j, krows, :], ds, 1, 0)
                dk = dot(qh, ds, 1, 1)
                dv = dot(gh, pb, 1, 1)
                first = t == 0
                acc[j, 0] = jnp.where(first, dk, acc[j, 0] + dk)
                acc[j, 1] = jnp.where(first, dv, acc[j, 1] + dv)
            dq = dq * score_scale
            a, b = dq[:32], dq[32:]
            q_back[pl.ds(pl.multiple_of(h * 64, 32), 32), :] = (a * co + b * si).astype(BF)
            q_back[pl.ds(pl.multiple_of(h * 64 + 32, 32), 32), :] = (b * co - a * si).astype(BF)
            return inner

        lax.fori_loop(0, GROUP, head, 0)
        for j in range(4):
            mine[j, krows, :] = acc[j, 0].astype(BF)
            mine[j, vrows, :] = acc[j, 1].astype(BF)
        pl.when(g == 1)(step_c1)
        pl.when(g == 3)(step_d)
        return carry

    acc[...] = jnp.zeros_like(acc)
    lax.fori_loop(0, KEY_VALUE_HEADS, group, 0)
    to_sib_far = remote(mine.at[diag_slot], got.at[1], send.at[0], recv.at[0], sibling)
    to_sib = remote(mine.at[sib_slot], got.at[0], send.at[1], recv.at[1], sibling)
    to_sib_far.start()
    to_sib.start()
    to_sib_far.wait_recv()
    got[1] = (mine[far_slot].astype(F32) + got[1].astype(F32)).astype(BF)
    to_far = remote(got.at[1], far_got, send.at[2], recv.at[2], far)
    to_far.start()
    to_sib.wait_recv()

    @pl.when(holds)
    def _():
        for i in (0, 1):
            d_x(i).wait_recv()
            rows = slice(160 * i, 160 * (i + 1))
            d_out[rows, :] = (ds_[rows, :].astype(F32) + dt[i].astype(F32)).astype(BF)

    @pl.when(jnp.logical_not(holds))
    def _():
        d_out[...] = jnp.zeros_like(d_out)

    near = mine[me].astype(F32) + got[0].astype(F32)
    to_far.wait_recv()
    total = near + far_got[...].astype(F32)
    for h in range(KEY_VALUE_HEADS):
        a, b = total[64 * h : 64 * h + 32, :], total[64 * h + 32 : 64 * h + 64, :]
        kv_back[64 * h : 64 * h + 32, :] = (a * co + b * si).astype(BF)
        kv_back[64 * h + 32 : 64 * h + 64, :] = (b * co - a * si).astype(BF)
    kv_back[KW:, :] = total[KW:, :].astype(BF)
    for i, half in enumerate(halves):
        for j in (1, 2, 3):
            c0_z(i, j).wait_recv()
        for m in range(2):
            for k in range(4):
                c0_out[m, k, :, half] = summed(c0[i, m, k, quarter(z, 32)], [c0r[j, i, m, k] for j in range(3)])
    for j in (1, 2, 3):
        c1_z(j).wait_recv()
    for k in range(4):
        c1_out[k] = summed(c1s[0, k, quarter(z, 32)], [c1t[j, k] for j in range(3)])
    for j in (1, 2, 3):
        c1_y(j).wait_recv()
    c1y_out[...] = summed(c1s[1, y], c1u)

    trade_two.wait_send()
    trade_down.wait_send()
    to_sib_far.wait_send()
    to_sib.wait_send()
    to_far.wait_send()
    for j in (1, 2, 3):
        c0_z(0, j).wait_send()
        c0_z(1, j).wait_send()
        c1_z(j).wait_send()
        c1_y(j).wait_send()
        d_y(j).wait_send()
    for i in (0, 1):
        c1_x(i).wait_send()

    @pl.when(jnp.logical_not(holds))
    def _():
        d_x(0).wait_send()
        d_x(1).wait_send()


def backward(*args):
    sem = pltpu.SemaphoreType.DMA
    vm = lambda *shape: pltpu.VMEM(shape, BF)
    return pl.pallas_call(
        backward_kernel,
        name="backward",
        out_shape=(
            jax.ShapeDtypeStruct((D, TOK), BF),
            jax.ShapeDtypeStruct((2 * KW, TOK), BF),
            jax.ShapeDtypeStruct((2, 4, 32, FH), BF),
            jax.ShapeDtypeStruct((4, 32, 640), BF),
            jax.ShapeDtypeStruct((PAD, 640), BF),
            jax.ShapeDtypeStruct((KW, D), BF),
            jax.ShapeDtypeStruct((D, TOK), BF),
            jax.ShapeDtypeStruct((D, TOK), F32),
            jax.ShapeDtypeStruct((D, TOK), BF),
            jax.ShapeDtypeStruct((D, 1), F32),
        ),
        in_specs=[VM] * 14,
        out_specs=(VM,) * 10,
        scratch_shapes=[
            vm(D, 2 * TOK), vm(D, 2 * TOK), vm(FH, 2 * TOK), vm(FH, 2 * TOK), vm(FH, 2 * TOK), vm(D, TOK),
            pltpu.VMEM((D, 2 * TOK), F32), pltpu.VMEM((D, TOK), F32),
            pltpu.VMEM((D, 2 * TOK), F32), pltpu.VMEM((D, TOK), F32),
            sem((2,)), sem((2,)),
            vm(4, 2 * KW, TOK), vm(2, 2 * KW, TOK), vm(2 * KW, TOK), pltpu.VMEM((4, 2, 64, TOK), F32),
            vm(2, 2, 4, PAD, 640), vm(3, 2, 2, 4, 32, 640),
            vm(2, 2, 4, PAD, 640), vm(2, 4, PAD, 640), vm(2, 4, PAD, 640), vm(3, 4, 32, 640), vm(3, PAD, 640),
            vm(4, KW, D), vm(3, KW, D), vm(KW, D), vm(2, 160, D),
        ]
        + [sem((3,))] * 2
        + [sem((2, 3))] * 2
        + [sem((2,))] * 2
        + [sem((3,))] * 8,
        compiler_params=params(2, 61),
    )(*args)


WIDE, NARROW = 512, D - 512


def finish_kernel(
    one, att, mid, q_back, kv_back, c0, c1, c1y, dd, stream, mid_grad, gains, gain_two, wq, wk, wv,
    lo_sum, hi_sum, kv_sum, c0_sum, c1_sum, d_sum, in_grad,
    gain_cols,
    left, right, thin, both, lo, hi, kv,
    lo1, lo1r, lo2, lo2r, lo3, lo3r,
    kv1, kv1r, kv2, kv2r, kv3, kv3r,
    hi1, hi1r, hi2, hi2r, hi3, hi3r,
    c02r, c02, c03r, c03,
    c1r, c1zr, c1s, c1t, c1u,
    dr, dh, dx, ds_,
    send, recv, send_s, recv_s, send_g, recv_g, send_o, recv_o, local,
):
    x, y, z, c = place()
    xl = lax.rem(x, 2)
    holds = c == xl
    sibling = at(x, y, z, 1 - c)
    along_x, along_y, along_z = ring(x, y, z, c)
    greet(along_x + along_y + along_z + [sibling])
    LO, HI, KV, C0, C1, DN = range(6)

    def trade(i, src, dst):
        return remote(src, dst, send_s.at[i], recv_s.at[i], sibling)

    far = slice(TOK, 2 * TOK)

    def trades(core):
        return [
            trade(0, att if core == 0 else one, left.at[:, far]),
            trade(1, mid if core == 0 else q_back, right.at[:, far]),
            trade(2, kv_back.at[KW:] if core == 0 else kv_back.at[:KW], thin.at[:, far]),
            trade(3, one, both.at[:, far]),
        ]

    def move(item, phase, j, src, dst, along):
        return remote(src, dst.at[j - 1], send.at[item, phase, j - 1], recv.at[item, phase, j - 1], along[j - 1])

    def y1(item, j):
        return move(item, 0, j, lo.at[:, lax.rem(y + j, 4)], lo1r, along_y)

    def x2(item, j):
        return move(item, 1, j, lo1.at[xl if j == 2 else 1 - xl], lo2r, along_x)

    def z3(item, j):
        if item == DN:
            return move(item, 2, j, dd.at[quarter(z + j, 80)], dr, along_z)
        return move(item, 2, j, lo2.at[quarter(z + j, 32)], lo3r, along_z)

    def z1(item, j):
        src, dst = {HI: (hi, hi1r), KV: (kv, kv1r)}[item]
        return move(item, 0, j, src.at[:, :, quarter(z + j, 32)], dst, along_z)

    def y2(item, j):
        src, dst = {HI: (hi1, hi2r), KV: (kv1, kv2r), C0: (c0, c02r)}[item]
        return move(item, 1, j, src.at[:, lax.rem(y + j, 4)], dst, along_y)

    def x3(item, j):
        src, dst = {HI: (hi2, hi3r), KV: (kv2, kv3r), C0: (c02, c03r)}[item]
        return move(item, 2, j, src.at[xl if j == 2 else 1 - xl], dst, along_x)

    def y_up(j):
        return move(C1, 0, j, c1.at[lax.rem(y + j, 4)], c1r, along_y)

    def z_up(j):
        return move(C1, 2, j, c1y.at[quarter(z + j, 32)], c1zr, along_z)

    def x_up():
        return remote(c1s, c1t, send.at[C1, 1, 0], recv.at[C1, 1, 0], along_x[1])

    def x_down():
        return remote(dh, dx, send.at[DN, 1, 0], recv.at[DN, 1, 0], along_x[1])

    for core in (0, 1):

        @pl.when(c == core)
        def _(core=core):
            for copy in trades(core):
                copy.start()

    for j in ORDER:
        y2(C0, j).start()
        y_up(j).start()
        z_up(j).start()

    @pl.when(holds)
    def _():
        for j in ORDER:
            z3(DN, j).start()

    near = slice(0, TOK)

    @pl.when(c == 0)
    def _():
        left[:, near] = one[...]
        right[:, near] = q_back[...]
        thin[:, near] = kv_back[:KW, :]

    @pl.when(c == 1)
    def _():
        left[:, near] = att[...]
        right[:, near] = mid[...]
        thin[:, near] = kv_back[KW:, :]

    both[:, near] = one[...]

    trade(0, one, left.at[:, far]).wait_recv()
    trade(1, one, right.at[:, far]).wait_recv()

    def wide_part(start, stop, into, shift, extra):
        part = planes(dot(left[...], right[start:stop, :], 1, 1), extra)
        for f in range(8):
            into[f // 4, f % 4, :, start - shift : stop - shift] = part[f]

    nothing = [jnp.zeros((8, 256), F32)] * 8
    wide_part(0, 256, lo, 0, nothing)
    wide_part(256, 512, lo, 0, nothing)
    for j in ORDER:
        y1(LO, j).start()
    trade(3, one, both.at[:, far]).wait_recv()
    trade(2, kv_back.at[:KW], thin.at[:, far]).wait_recv()
    part = planes(dot(both[...], thin[...], 1, 1), [jnp.zeros((8, KW), F32)] * 8)
    for f in range(8):
        kv[f // 4, f % 4] = part[f]
    for j in ORDER:
        z1(KV, j).start()
    wide_part(768, D, hi, WIDE, [jnp.zeros((8, D - 768), F32)] * 8)

    source = stream[...].astype(F32)
    scale = lax.rsqrt(jnp.sum(source * source, axis=0, keepdims=True) / D + norm_epsilon)
    normal = source * scale
    for start, stop in columns(D):
        in_grad[start:stop, :] = (
            dot(wq[start:stop, :], q_back[...], 1, 0)
            + dot(wk[start:stop, :], kv_back[:KW, :], 1, 0)
            + dot(wv[start:stop, :], kv_back[KW:, :], 1, 0)
        )
    incoming = in_grad[...]
    gain_cols[...] = jnp.sum(incoming * normal, axis=1, keepdims=True)
    scaled = incoming * gains[0]
    level = jnp.sum(scaled * normal, axis=0, keepdims=True) / D
    in_grad[...] = mid_grad[...] + scale * (scaled - normal * level)
    lane = lax.broadcasted_iota(jnp.int32, (PAD, 128), 1)
    gain = []
    for f in range(8):
        rows_f = slice(ROWS * f, ROWS * (f + 1))
        zeros = jnp.zeros((PAD - ROWS, 128), F32)
        first_col = jnp.concatenate([jnp.broadcast_to(gain_cols[rows_f, :], (ROWS, 128)), zeros], axis=0)
        second_col = jnp.concatenate([jnp.broadcast_to(gain_two[rows_f, :], (ROWS, 128)), zeros], axis=0)
        tile = jnp.where(lane == 0, first_col, jnp.where(lane == 1, second_col, 0.0)).T
        gain.append(jnp.concatenate([tile[:8], jnp.zeros((8, 128), F32)], axis=1))

    wide_part(512, 768, hi, WIDE, gain)
    for j in ORDER:
        z1(HI, j).start()

    def arrived(make, *key):
        for j in (1, 2, 3):
            make(*key, j).wait_recv()

    arrived(y2, C0)
    for i in range(2):
        c02[i] = summed(c0[i, y], [c02r[j, i] for j in range(3)])
    for j in ORDER:
        x3(C0, j).start()
    arrived(y_up)
    c1s[:, 0:640] = summed(c1[y], c1r)
    arrived(z_up)
    c1s[:, 640:FH] = summed(c1y[quarter(z, 32)], c1zr)
    x_up().start()

    part_of = {LO: lo3, HI: hi3, KV: kv3, C0: c03, C1: c1u, DN: ds_}

    def place_of(item, index, core):
        if item == DN:
            return d_sum.at[quarter(index, 80)]
        if item in (C0, C1):
            lanes = pl.ds(pl.multiple_of(FH * core, 128), FH)
            return (c0_sum if item == C0 else c1_sum).at[quarter(index, 32), lanes]
        return {LO: lo_sum, HI: hi_sum, KV: kv_sum}[item].at[core, quarter(index, 32)]

    def spread(item, j):
        return remote(
            part_of[item], place_of(item, z, c), send_g.at[item, j - 1], recv_g.at[item, j - 1], along_z[j - 1]
        )

    def keep(item):
        return pltpu.make_async_copy(part_of[item], place_of(item, z, c), local.at[item])

    def across(item, k):
        index = lax.rem(z + 4 - k, 4)
        src = part_of[item] if k == 0 else place_of(item, index, c)
        return remote(src, place_of(item, index, c), send_o.at[item, k], recv_o.at[item, k], sibling)

    def publish(item):
        keep(item).start()
        for j in ORDER:
            spread(item, j).start()
        across(item, 0).start()

    def landed(item, j):
        ref = place_of(item, lax.rem(z + 4 - j, 4), c)
        remote(ref, ref, send_g.at[item, j - 1], recv_g.at[item, j - 1], sibling).wait_recv()

    def collect(item):
        for j in ORDER:
            landed(item, j)
            across(item, j).start()

    def arrive(item):
        for k in range(4):
            ref = place_of(item, lax.rem(z + 4 - k, 4), 1 - c)
            remote(ref, ref, send_o.at[item, k], recv_o.at[item, k], sibling).wait_recv()

    @pl.when(holds)
    def _():
        arrived(z3, DN)
        dh[...] = summed(dd[quarter(z, 80)], dr)
        x_down().start()

    @pl.when(holds)
    def _():
        x_down().wait_recv()
        ds_[...] = (dh[...].astype(F32) + dx[...].astype(F32)).astype(BF)
        publish(DN)

    x_up().wait_recv()
    c1u[...] = (c1s[...].astype(F32) + c1t[...].astype(F32)).astype(BF)
    publish(C1)
    arrived(x3, C0)
    c03[...] = summed(c02[xl], c03r)
    publish(C0)

    arrived(y1, LO)
    for i in range(2):
        lo1[i] = summed(lo[i, y], [lo1r[j, i] for j in range(3)])
    for j in ORDER:
        x2(LO, j).start()
    for item, first, out, got in ((KV, kv, kv1, kv1r), (HI, hi, hi1, hi1r)):
        arrived(z1, item)
        for i in range(2):
            for k in range(4):
                out[i, k] = summed(first[i, k, quarter(z, 32)], [got[j, i, k] for j in range(3)])
        for j in ORDER:
            y2(item, j).start()
    arrived(x2, LO)
    lo2[...] = summed(lo1[xl], lo2r)
    for j in ORDER:
        z3(LO, j).start()
    for item, first, out, got in ((KV, kv1, kv2, kv2r), (HI, hi1, hi2, hi2r)):
        arrived(y2, item)
        for i in range(2):
            out[i] = summed(first[i, y], [got[j, i] for j in range(3)])
        for j in ORDER:
            x3(item, j).start()
    arrived(z3, LO)
    lo3[...] = summed(lo2[quarter(z, 32)], lo3r)
    publish(LO)
    arrived(x3, KV)
    kv3[...] = summed(kv2[xl], kv3r)
    publish(KV)
    arrived(x3, HI)
    hi3[...] = summed(hi2[xl], hi3r)
    publish(HI)

    pl.when(holds)(lambda: collect(DN))
    for item in (C1, C0, KV, LO, HI):
        collect(item)
    pl.when(jnp.logical_not(holds))(lambda: arrive(DN))
    for item in (C1, C0, KV, LO, HI):
        arrive(item)

    for core in (0, 1):

        @pl.when(c == core)
        def _(core=core):
            for copy in trades(core):
                copy.wait_send()

    def settled(item):
        keep(item).wait()
        for j in (1, 2, 3):
            spread(item, j).wait_send()
        for k in range(4):
            across(item, k).wait_send()

    for j in (1, 2, 3):
        for make, key in (
            (y1, LO), (x2, LO), (z3, LO), (z1, KV), (y2, KV), (x3, KV), (z1, HI), (y2, HI), (x3, HI), (y2, C0), (x3, C0),
        ):
            make(key, j).wait_send()
        y_up(j).wait_send()
        z_up(j).wait_send()
    x_up().wait_send()
    for item in (LO, HI, KV, C0, C1):
        settled(item)

    @pl.when(holds)
    def _():
        for j in (1, 2, 3):
            z3(DN, j).wait_send()
        x_down().wait_send()
        settled(DN)


def finish(*args):
    sem = pltpu.SemaphoreType.DMA
    vm = lambda *shape: pltpu.VMEM(shape, BF)

    def yxz(width):
        return [
            vm(2, PAD, width), vm(3, 2, PAD, width), vm(PAD, width), vm(3, PAD, width),
            vm(32, width), vm(3, 32, width),
        ]

    def zyx(width):
        return [
            vm(2, 4, 32, width), vm(3, 2, 4, 32, width), vm(2, 32, width), vm(3, 2, 32, width),
            vm(32, width), vm(3, 32, width),
        ]

    return pl.pallas_call(
        finish_kernel,
        name="finish",
        out_shape=(
            jax.ShapeDtypeStruct((2, PAD, WIDE), BF),
            jax.ShapeDtypeStruct((2, PAD, NARROW), BF),
            jax.ShapeDtypeStruct((2, PAD, KW), BF),
            jax.ShapeDtypeStruct((PAD, FF), BF),
            jax.ShapeDtypeStruct((PAD, FF), BF),
            jax.ShapeDtypeStruct((KW, D), BF),
            jax.ShapeDtypeStruct((D, TOK), F32),
        ),
        in_specs=[VM] * 16,
        out_specs=(ANY,) * 6 + (VM,),
        scratch_shapes=[
            pltpu.VMEM((D, 1), F32),
            vm(D, 2 * TOK), vm(D, 2 * TOK), vm(KW, 2 * TOK), vm(D, 2 * TOK),
            vm(2, 4, PAD, WIDE), vm(2, 4, PAD, NARROW), vm(2, 4, PAD, KW),
        ]
        + yxz(WIDE)
        + zyx(KW)
        + zyx(NARROW)
        + [vm(3, 2, 32, FH), vm(2, 32, FH), vm(3, 32, FH), vm(32, FH)]
        + [vm(3, 32, 640), vm(3, 32, 640), vm(32, FH), vm(32, FH), vm(32, FH)]
        + [vm(3, 80, D), vm(80, D), vm(80, D), vm(80, D)]
        + [sem((6, 3, 3)), sem((6, 3, 3)), sem((4,)), sem((4,)), sem((6, 3)), sem((6, 3)), sem((6, 4)), sem((6, 4)), sem((6,))],
        compiler_params=params(3),
    )(*args)


def adamw_update(weight, gradient, first, second, rate, decay):
    weight = weight.astype(F32)
    first_new = beta_first * first.astype(F32) + (1.0 - beta_first) * gradient
    second_new = beta_second * second.astype(F32) + (1.0 - beta_second) * gradient * gradient
    first_hat = first_new * (rate / (1.0 - beta_first**STEP))
    second_hat = second_new * (1.0 / (1.0 - beta_second**STEP))
    weight_new = weight * (1.0 - rate * decay) - first_hat / (jnp.sqrt(second_hat) + adam_epsilon)
    return (weight_new, first_new, second_new)


def update_kernel(lo, hi, narrow, gate, up, down, *refs):
    state, new = refs[:18], refs[18:]

    def update(which, index, gradient, rate=matrix_rate, decay=matrix_decay):
        weight, first, second = (state[3 * which + i][index] for i in range(3))
        for i, value in enumerate(adamw_update(weight, gradient, first, second, rate, decay)):
            new[3 * which + i][index] = value

    for m, source in ((0, gate), (1, up)):
        update(3, m, source[...].astype(F32)[:ROWS])
    update(4, slice(None), down[...].astype(F32))

    @pl.when(pl.program_id(0) == 0)
    def _():
        for which, core in ((0, 0), (2, 1)):
            update(which, (slice(None), slice(0, WIDE)), lo[core].astype(F32)[:ROWS])
            update(which, (slice(None), slice(WIDE, D)), hi[core].astype(F32)[:ROWS])
        for m in (0, 1):
            update(1, m, narrow[m].astype(F32).T[:, :ROWS])
        gains = hi[0, 112:, :128].astype(F32) + hi[1, 112:, :128].astype(F32)
        update(5, slice(None), gains[8:10, :ROWS], gain_rate, 0.0)


def update_all(lo, hi, narrow, gate, up, down, state):
    steps = 5
    fixed = lambda a: pl.BlockSpec(a.shape, lambda i: (0,) * len(a.shape))
    sums = pl.BlockSpec((PAD, FF // steps), lambda i: (0, i))
    rows = pl.BlockSpec((KW // steps, D), lambda i: (i, 0))
    wide = pl.BlockSpec((2, ROWS, FF // steps), lambda i: (0, 0, i))
    specs = []
    for i, array in enumerate(state):
        specs.append(wide if i // 3 == 3 else rows if i // 3 == 4 else fixed(array))
    return pl.pallas_call(
        update_kernel,
        name="update",
        grid=(steps,),
        out_shape=tuple(jax.ShapeDtypeStruct(a.shape, F32) for a in state),
        in_specs=[fixed(lo), fixed(hi), fixed(narrow), sums, sums, rows] + specs,
        out_specs=tuple(specs),
        compiler_params=pltpu.CompilerParams(vmem_limit_bytes=62 * 2**20),
    )(lo, hi, narrow, gate, up, down, *state)


def body(
    tokens,
    cotangent,
    query_weight,
    keyval_weight,
    output_weight,
    gateup_weight,
    down_weight,
    norm_gains,
    query_first,
    keyval_first,
    output_first,
    gateup_first,
    down_first,
    gains_first,
    query_second,
    keyval_second,
    output_second,
    gateup_second,
    down_second,
    gains_second,
):
    ctx = lax.axis_index("ctx")
    core = lax.rem(ctx, 2)
    stream_t, dy_t = tokens[0].T, cotangent[0].T
    gain_tile = jnp.pad(norm_gains.astype(F32), ((0, 6), (0, 8)))
    positions = (ctx * TOK + jnp.arange(TOK, dtype=jnp.int32)).astype(F32)
    counter = jnp.arange(HALF, dtype=F32)
    frequency = 1.0 / rotary_base ** (counter * (2.0 / HEAD_WIDTH))
    angles = frequency[:, None] * positions[None, :]
    cosine, sine = jnp.cos(angles), jnp.sin(angles)

    (
        query_low, attended_t, level, keys, one_t, middle_t, two_all, dy_all, gains,
        query_all, output_all, key_all, value_all, gate_all, up_all, dn_all,
    ) = forward(
        stream_t, cosine, sine, query_weight, output_weight, keyval_weight, gain_tile, dy_t,
        gateup_weight, down_weight,
    )
    query_full, output_full = query_all.reshape(D, D), output_all.reshape(D, D)
    key_full, value_full = key_all.reshape(D, KW), value_all.reshape(D, KW)
    gate_full, up_full = gate_all.reshape(D, FH), up_all.reshape(D, FH)
    down_full = dn_all.reshape(FH, D)

    (
        query_back, keyval_back, gate_part, up_part, up_row, down_sum, result_t, middle_grad, middle_low, gain_two_grad,
    ) = backward(
        query_low, keys, level, attended_t, cosine, sine, two_all, dy_all, middle_t, gains,
        gate_full, up_full, down_full, output_full,
    )
    low, high, narrow, gate_sum, up_sum, down, input_grad = finish(
        one_t, attended_t, middle_low, query_back, keyval_back, gate_part, up_part, up_row, down_sum,
        stream_t, middle_grad, gains, gain_two_grad, query_full, key_full, value_full,
    )
    turned = lambda a: a.transpose(0, 2, 1)
    state = (
        query_weight, query_first, query_second,
        turned(keyval_weight), turned(keyval_first), turned(keyval_second),
        output_weight, output_first, output_second,
        gateup_weight, gateup_first, gateup_second,
        down_weight, down_first, down_second,
        norm_gains, gains_first, gains_second,
    )
    new = list(update_all(low, high, narrow, gate_sum, up_sum, down, state))
    new[3:6] = [turned(a) for a in new[3:6]]
    return (result_t.T[None], input_grad.T[None], *new[0::3], *new[1::3], *new[2::3])


def solution(mesh):
    row, mid = P("fsdp", None), P(None, "fsdp", None)
    weights = (row, mid, row, mid, row, P(None, "fsdp"))
    stream = P(("rep", "fsdp"), "ctx", None)
    return jax.shard_map(
        body,
        mesh=mesh,
        in_specs=(stream, stream) + weights * 3,
        out_specs=(stream, stream) + weights * 3,
        check_vma=False,
    )
```

```python
import functools

import jax
import jax.numpy as jnp
from jax import lax
from jax.experimental import pallas as pl
from jax.experimental.pallas import tpu as pltpu
from jax.sharding import PartitionSpec as P

QUERY_HEADS = 15
KEY_VALUE_HEADS = 5
GROUP = QUERY_HEADS // KEY_VALUE_HEADS
HEAD_WIDTH = 64
HALF = HEAD_WIDTH // 2
STEP = 10
TOK = 256
D = 960
KW = 320
FF = 2560
FH = FF // 2
ROWS = 120
PAD = 128
BF = jnp.bfloat16
F32 = jnp.float32
MESH = pl.DeviceIdType.MESH

norm_epsilon = 1e-05
rotary_base = 100000.0
beta_first = 0.9
beta_second = 0.95
adam_epsilon = 1e-08
matrix_rate = 0.06
matrix_decay = 0.1
gain_rate = 0.6
score_scale = HEAD_WIDTH ** (-0.5)

ANY = pl.BlockSpec(memory_space=pl.ANY)
VM = pl.BlockSpec(memory_space=pltpu.VMEM)


def place():
    f = lax.axis_index("fsdp")
    q = lax.axis_index("ctx")
    z = lax.axis_index("rep")
    return (q // 2) * 2 + f // 4, f % 4, z, q % 2


def at(x, y, z, core):
    x, y, z = lax.rem(x, 4), lax.rem(y, 4), lax.rem(z, 4)
    return {"rep": z, "fsdp": lax.rem(x, 2) * 4 + y, "ctx": (x // 2) * 2 + core}


def ring(x, y, z, c):
    along_x = [at(x + j, y, z, c) for j in (1, 2, 3)]
    along_y = [at(x, y + j, z, c) for j in (1, 2, 3)]
    along_z = [at(x, y, z + j, c) for j in (1, 2, 3)]
    return along_x, along_y, along_z


def greet(devices):
    barrier = pltpu.get_barrier_semaphore()
    for device in devices:
        pl.semaphore_signal(barrier, inc=1, device_id=device, device_id_type=MESH)
    pl.semaphore_wait(barrier, len(devices))


def remote(src, dst, send, recv, device):
    return pltpu.make_async_remote_copy(
        src_ref=src, dst_ref=dst, send_sem=send, recv_sem=recv, device_id=device, device_id_type=MESH
    )


def params(number, vmem=56):
    return pltpu.CompilerParams(
        collective_id=number, has_side_effects=True, vmem_limit_bytes=vmem * 2**20
    )


def columns(total):
    return [(start, min(start + 256, total)) for start in range(0, total, 256)]


ORDER = (1, 3, 2)
SIDE = (1, 3, 3, 1)


def dot(a, b, ca, cb):
    return lax.dot_general(a, b, (((ca,), (cb,)), ((), ())), preferred_element_type=F32)


def forward_kernel(
    stream, cos, sin, kv_turned, gain_row, qw, ow, dy, gu, dn,
    q_low, att, lse, kv_out, one, mid, two_all, dy_all, gains_out, q_all, o_all, k_all, v_all, gate_all, up_all, dn_all,
    keys, wide, ones, two, qo_land, kv_land, gain_land, kv, gain,
    send, recv, send_zd, recv_zd, send_y, send_x, recv_w, send_ay, send_ax, send_as, recv_a, recv_as, local,
):
    x, y, z, c = place()
    xl = lax.rem(x, 2)
    f = 4 * xl + y
    holds = c == xl
    me = 2 * (x // 2) + c
    sib_slot, far_slot, diag_slot = me + 1 - 2 * c, lax.rem(me + 2, 4), lax.rem(me + 2, 4) + 1 - 2 * c
    sibling, far = at(x, y, z, 1 - c), at(x + 2, y, z, c)
    along_x, along_y, along_z = ring(x, y, z, c)
    greet(along_x + along_y + along_z + [sibling])

    def column(k):
        return 4 * xl + lax.rem(y + k + 1, 4) if k < 3 else 4 * (1 - xl) + lax.rem(y + k - 3, 4)

    for m in (0, 1):
        kv[m] = kv_turned[m].astype(F32).T.astype(BF)
    gain[...] = jnp.zeros_like(gain)
    gain[0:2, 0:ROWS] = gain_row[...].astype(F32)

    def own_a(item):
        return (None, kv.at[c], gain)[item]

    def by_core(item, make):
        if item:
            make(own_a(item))
        else:
            pl.when(c == 0)(lambda: make(qw))
            pl.when(c == 1)(lambda: make(ow))

    def slot_a(item, g, core):
        if item == 2:
            return gain_land.at[g]
        return (qo_land, kv_land)[item].at[core, g]

    def wait_a(item, k):
        ref = slot_a(item, column(k), c)
        remote(ref, ref, send_as.at[0, 0], recv_a.at[item, column(k)], sibling).wait_recv()

    def row_a(item, j, source=None):
        source = slot_a(item, f, c) if source is None else source
        return remote(source, slot_a(item, f, c), send_ay.at[item, j - 1], recv_a.at[item, f], at(x, y + j, z, c))

    def side_a(item, j, source=None):
        g = 4 * xl + lax.rem(y + j, 4)
        return remote(
            slot_a(item, g, c) if source is None else source,
            slot_a(item, g, c),
            send_ax.at[item, j],
            recv_a.at[item, g],
            at(x + SIDE[j], y, z, c),
        )

    def sib_a(item, k):
        ref = slot_a(item, column(k), c)
        return remote(ref, ref, send_as.at[item, k], recv_as.at[item, column(k)], sibling)

    def take(item, k):
        wait_a(item, k)
        if k < 3:
            side_a(item, k + 1).start()
        if item < 2:
            sib_a(item, k).start()

    def taken(item):
        for k in range(7):
            ref = slot_a(item, column(k), 1 - c)
            remote(ref, ref, send_as.at[0, 0], recv_as.at[item, column(k)], sibling).wait_recv()

    lanes = pl.ds(pl.multiple_of(c * FH, 128), FH)
    own = (gu.at[0, :, lanes], gu.at[1, :, lanes], dn.at[0:160], dn.at[160:320])

    def slot(item, g):
        if item < 2:
            return (gate_all, up_all)[item].at[g]
        return dn_all.at[lax.rem(g, 4), 160 * (item - 2) : 160 * (item - 1)]

    def wait_slot(item, g):
        remote(slot(item, g), slot(item, g), send_x.at[0, 0], recv_w.at[item, g], sibling).wait_recv()

    def send_row(item, j):
        return remote(own[item], slot(item, f), send_y.at[item, j - 1], recv_w.at[item, f], at(x, y + j, z, c))

    def send_side(item, j):
        g = 4 * xl + lax.rem(y + j, 4)
        return remote(
            own[item] if j == 0 else slot(item, g),
            slot(item, g),
            send_x.at[item, j],
            recv_w.at[item, g],
            at(x + (1, 3, 1, 3)[item], y, z, c),
        )

    def send_ring(item):
        j = (3, 1, 3, 1)[item]
        ref = slot(item, 4 * xl + lax.rem(y + j, 4))
        return remote(ref, ref, send_y.at[item, 1], recv_w.at[item, 4 * xl + lax.rem(y + j, 4)], at(x, y + 4 - j, z, c))

    def crossing(item, j, action):
        if item < 2:
            action()
        else:
            pl.when(lax.rem(y + j, 4) == z)(action)

    def pass_on(items, offsets):
        for item in items:
            for j in offsets:
                wait_slot(item, 4 * xl + lax.rem(y + j, 4))
                if j == (3, 1, 3, 1)[item]:
                    send_ring(item).start()
                crossing(item, j, lambda: send_side(item, j).start())

    def pass_down(offsets):
        pl.when(holds)(lambda: pass_on((2, 3), offsets))

    def down_z(j):
        return remote(dn_all.at[z], dn_all.at[z], send_zd.at[j - 1], recv_zd.at[j - 1], along_z[j - 1])

    def share_down():
        @pl.when(jnp.logical_not(holds))
        def _():
            for item in (2, 3):
                wait_slot(item, 4 * (1 - xl) + z)
            for j in ORDER:
                down_z(j).start()

    for item in (2, 1, 0):

        def launch(source, item=item):
            side_a(item, 0, source).start()
            for j in ORDER:
                row_a(item, j, source).start()

        by_core(item, launch)
    copies = [
        pltpu.make_async_copy(gain, gain_land.at[f], local.at[0]),
        pltpu.make_async_copy(kv, kv_land.at[:, f], local.at[1]),
        pltpu.make_async_copy(qw, qo_land.at[0, f], local.at[2]),
        pltpu.make_async_copy(ow, qo_land.at[1, f], local.at[9]),
        pltpu.make_async_copy(own[0], gate_all.at[f], local.at[3]),
        pltpu.make_async_copy(own[1], up_all.at[f], local.at[8]),
        pltpu.make_async_copy(dy, dy_all.at[0], local.at[4]),
    ]
    for copy in copies:
        copy.start()
    own_down = pltpu.make_async_copy(dn, dn_all.at[y], local.at[5])
    pl.when(holds)(own_down.start)

    co, si = cos[...], sin[...]
    wide[...] = stream[...].astype(F32)
    scale = lax.rsqrt(jnp.sum(wide[...] ** 2, axis=0, keepdims=True) / D + norm_epsilon)

    for k in (0, 2):
        take(2, k)
        take(1, k)
    take(1, 3)
    wait_a(2, 3)
    for k in (0, 2):
        take(0, k)
    @pl.when(holds)
    def _():
        for item in (2, 3):
            for j in (1, 3):
                send_row(item, j).start()

    for item in (0, 1):
        for j in (1, 3):
            send_row(item, j).start()

    take(2, 1)
    take(1, 1)
    take(0, 3)
    for k in (4, 6, 5):
        wait_a(2, k)
        take(1, k)
    take(0, 1)

    for copy in copies[:4]:
        copy.wait()
    for g in range(8):
        tile = gain_land[g].T
        gains_out[0, ROWS * g : ROWS * (g + 1), :] = tile[:ROWS, 0:1]
        gains_out[1, ROWS * g : ROWS * (g + 1), :] = tile[:ROWS, 1:2]
    ones[...] = wide[...] * scale * gains_out[0]
    one[...] = ones[...].astype(BF)
    taken(1)

    def block(ref, g):
        return ref[ROWS * g : ROWS * (g + 1), :].astype(BF)

    def project(land, which, cols, source):
        total = dot(land[which, 0, :, cols], block(source, 0), 0, 0)
        for g in range(1, 8):
            total += dot(land[which, g, :, cols], block(source, g), 0, 0)
        return total

    key = project(kv_land, 0, slice(0, KW), ones)
    for h in range(KEY_VALUE_HEADS):
        a, b = key[64 * h : 64 * h + 32, :], key[64 * h + 32 : 64 * h + 64, :]
        keys[me, 64 * h : 64 * h + 32, :] = (a * co - b * si).astype(BF)
        keys[me, 64 * h + 32 : 64 * h + 64, :] = (b * co + a * si).astype(BF)
    keys[me, KW:, :] = project(kv_land, 1, slice(0, KW), ones).astype(BF)
    to_far = remote(keys.at[me], keys.at[me], send.at[0], recv.at[0], far)
    to_sib = remote(keys.at[me], keys.at[me], send.at[1], recv.at[1], sibling)
    to_far.start()
    to_sib.start()
    for k in (4, 6, 5):
        take(0, k)
    @pl.when(jnp.logical_and(holds, y == z))
    def _():
        for item in (2, 3):
            send_side(item, 0).start()

    for item in (0, 1):
        send_side(item, 0).start()

    taken(0)
    exchange = remote(dy, dy_all.at[1], send.at[4], recv.at[4], sibling)
    exchange.start()
    keep_a = [
        pltpu.make_async_copy(qo_land.at[0], q_all, local.at[0]),
        pltpu.make_async_copy(qo_land.at[1], o_all, local.at[1]),
        pltpu.make_async_copy(kv_land.at[0], k_all, local.at[2]),
        pltpu.make_async_copy(kv_land.at[1], v_all, local.at[6]),
    ]
    for copy in keep_a:
        copy.start()
    for start, stop in columns(D):
        query = project(qo_land, 0, slice(start, stop), ones)
        for h in range(0, stop - start, 64):
            a, b = query[h : h + 32, :], query[h + 32 : h + 64, :]
            rows = start + h
            q_low[rows : rows + 32, :] = ((a * co - b * si).astype(BF) * score_scale).astype(BF)
            q_low[rows + 32 : rows + 64, :] = ((b * co + a * si).astype(BF) * score_scale).astype(BF)
    pass_down((1, 3))
    remote(keys.at[far_slot], keys.at[far_slot], send.at[0], recv.at[0], far).wait_recv()
    on = remote(keys.at[far_slot], keys.at[far_slot], send.at[2], recv.at[2], sibling)
    on.start()
    remote(keys.at[sib_slot], keys.at[sib_slot], send.at[1], recv.at[1], sibling).wait_recv()
    remote(keys.at[diag_slot], keys.at[diag_slot], send.at[2], recv.at[2], sibling).wait_recv()
    gap = lax.broadcasted_iota(jnp.int32, (TOK, TOK), 0) - lax.broadcasted_iota(jnp.int32, (TOK, TOK), 1)

    def head(h, carry):
        rows = pl.ds(pl.multiple_of(h * 64, 64), 64)
        g = h // GROUP
        krows = pl.ds(pl.multiple_of(g * 64, 64), 64)
        vrows = pl.ds(pl.multiple_of(KW + g * 64, 64), 64)
        qh = q_low[rows, :]
        s = []
        for j in range(4):
            part = dot(keys[j, krows, :], qh, 0, 0)
            s.append(jnp.where(gap <= 256 * (me - j), part, -1e30))
        top = jnp.max(jnp.maximum(jnp.maximum(s[0], s[1]), jnp.maximum(s[2], s[3])), axis=0, keepdims=True)
        e = [jnp.exp(part - top) for part in s]
        total = jnp.sum(e[0] + e[1] + (e[2] + e[3]), axis=0, keepdims=True)
        acc = dot(keys[0, vrows, :], e[0].astype(BF), 1, 0)
        for j in range(1, 4):
            acc += dot(keys[j, vrows, :], e[j].astype(BF), 1, 0)
        ones[rows, :] = acc / total
        lse[pl.ds(h, 1), 0, :] = top + jnp.log(total)
        pl.when(h == 1)(lambda: pass_on((0,), (1, 3)))
        pl.when(h == 5)(lambda: pass_down((2,)))
        pl.when(h == 7)(lambda: pass_on((1,), (1, 3)))
        pl.when(h == 9)(share_down)
        pl.when(h == 13)(lambda: pass_on((0,), (2,)))
        return carry

    lax.fori_loop(0, QUERY_HEADS, head, 0)
    kv_out[...] = keys[...]
    att[...] = ones[...].astype(BF)

    square = jnp.zeros((1, TOK), F32)
    for start, stop in columns(D):
        part = wide[start:stop, :] + project(qo_land, 1, slice(start, stop), ones)
        mid[start:stop, :] = part
        square += jnp.sum(part * part, axis=0, keepdims=True)
    scale = lax.rsqrt(square / D + norm_epsilon)
    two[...] = (mid[...] * scale * gains_out[1]).astype(BF)
    keep = pltpu.make_async_copy(two, two_all.at[0], local.at[7])
    keep.start()
    trade = remote(two, two_all.at[1], send.at[3], recv.at[3], sibling)
    trade.start()
    pass_on((1,), (2,))

    for k in range(4):
        g = 4 * (1 - xl) + lax.rem(y + k, 4)
        for item in (0, 1):
            wait_slot(item, g)

    @pl.when(jnp.logical_not(holds))
    def _():
        for j in ORDER:
            ref = dn_all.at[lax.rem(z + 4 - j, 4)]
            remote(ref, ref, send_zd.at[j - 1], recv_zd.at[j - 1], sibling).wait_recv()
            down_z(j).wait_send()

    for copy in copies[4:] + keep_a + [keep]:
        copy.wait()
    trade.wait()
    exchange.wait()
    to_far.wait_send()
    to_sib.wait_send()
    on.wait_send()
    for item in (0, 1, 2):
        for j in ORDER:
            row_a(item, j).wait_send()
        for j in range(4):
            side_a(item, j).wait_send()
        if item < 2:
            for k in range(7):
                sib_a(item, k).wait_send()

    def sent(items):
        for item in items:
            for j in (1, 3):
                send_row(item, j).wait_send()
            send_ring(item).wait_send()
            for j in range(4):
                crossing(item, j, lambda: send_side(item, j).wait_send())

    sent((0, 1))

    @pl.when(holds)
    def _():
        own_down.wait()
        sent((2, 3))


def forward(*args):
    sem = pltpu.SemaphoreType.DMA
    low = lambda *shape: jax.ShapeDtypeStruct(shape, BF)
    return pl.pallas_call(
        forward_kernel,
        name="forward",
        out_shape=(
            low(D, TOK),
            low(D, TOK),
            jax.ShapeDtypeStruct((16, 1, TOK), F32),
            low(4, 2 * KW, TOK),
            low(D, TOK),
            jax.ShapeDtypeStruct((D, TOK), F32),
            low(2, D, TOK),
            low(2, D, TOK),
            jax.ShapeDtypeStruct((2, D, 1), F32),
            low(8, ROWS, D),
            low(8, ROWS, D),
            low(8, ROWS, KW),
            low(8, ROWS, KW),
            low(8, ROWS, FH),
            low(8, ROWS, FH),
            low(4, KW, D),
        ),
        in_specs=[VM] * 5 + [ANY] * 5,
        out_specs=(VM,) * 6 + (ANY,) * 2 + (VM,) + (ANY,) * 7,
        scratch_shapes=[
            pltpu.VMEM((4, 2 * KW, TOK), BF),
            pltpu.VMEM((D, TOK), F32),
            pltpu.VMEM((D, TOK), F32),
            pltpu.VMEM((D, TOK), BF),
            pltpu.VMEM((2, 8, ROWS, D), BF),
            pltpu.VMEM((2, 8, ROWS, KW), BF),
            pltpu.VMEM((8, 8, 128), F32),
            pltpu.VMEM((2, ROWS, KW), BF),
            pltpu.VMEM((8, 128), F32),
            sem((5,)),
            sem((5,)),
            sem((3,)),
            sem((3,)),
            sem((4, 3)),
            sem((4, 4)),
            sem((4, 8)),
            sem((3, 3)),
            sem((3, 4)),
            sem((2, 7)),
            sem((3, 8)),
            sem((2, 8)),
            sem((10,)),
        ],
        compiler_params=params(1),
    )(*args)


def summed(own, got, count=3):
    total = own.astype(F32)
    for i in range(count):
        total += got[i].astype(F32)
    return total.astype(BF)


def quarter(index, size):
    return pl.ds(pl.multiple_of(lax.rem(index, 4) * size, 16), size)


def planes(value, extra):
    return [
        jnp.concatenate([value[ROWS * f : ROWS * (f + 1)], extra[f]], axis=0).astype(BF)
        for f in range(8)
    ]


def backward_kernel(
    q_low, keys, lse, att, cos, sin, two_all, dy_all, mid, gains, wg, wu, wd, wo,
    q_back, kv_back, c0_out, c1_out, c1y_out, d_out, result, mid_grad, mid_low, gain_grad,
    two, dy, gate_grad, up_grad, hidden, grad, down_part, down_got, two_part, two_got, send_s, recv_s,
    mine, got, far_got, acc, c0, c0r, c1, c1r, c1s, c1t, c1u, d, dr, ds_, dt,
    send, recv, send_z, recv_z, send_x, recv_x, send_t, recv_t, send_u, recv_u, send_y, recv_y, send_d, recv_d,
):
    x, y, z, c = place()
    xl = lax.rem(x, 2)
    holds = c == xl
    me = 2 * (x // 2) + c
    far_slot = lax.rem(me + 2, 4)
    sib_slot = me + 1 - 2 * c
    diag_slot = far_slot + 1 - 2 * c
    sibling, far = at(x, y, z, 1 - c), at(x + 2, y, z, c)
    along_x, along_y, along_z = ring(x, y, z, c)
    greet(along_x + along_y + along_z + [sibling])
    co, si = cos[...], sin[...]
    nothing = {size: [jnp.zeros((8, size), F32)] * 8 for size in (128, 256)}

    halves = (slice(0, 640), slice(640, FH))

    def c0_z(i, j):
        return remote(
            c0.at[i, :, :, quarter(z + j, 32)], c0r.at[j - 1, i], send_z.at[i, j - 1], recv_z.at[i, j - 1], along_z[j - 1]
        )

    def c1_x(i):
        return remote(c1.at[i, 1 - xl], c1r.at[i], send_x.at[i], recv_x.at[i], along_x[2 * i])

    def c1_z(j):
        return remote(c1s.at[0, :, quarter(z + j, 32)], c1t.at[j - 1], send_t.at[j - 1], recv_t.at[j - 1], along_z[j - 1])

    def c1_y(j):
        return remote(c1s.at[1, lax.rem(y + j, 4)], c1u.at[j - 1], send_u.at[j - 1], recv_u.at[j - 1], along_y[j - 1])

    def d_y(j):
        return remote(d.at[lax.rem(y + j, 4)], dr.at[j - 1], send_y.at[j - 1], recv_y.at[j - 1], along_y[j - 1])

    def d_block(k):
        for j in (1, 2, 3):
            pl.when(lax.rem(y + j, 4) == k)(lambda j=j: d_y(j).start())

    def d_x(i):
        return remote(ds_.at[160 * i : 160 * (i + 1)], dt.at[i], send_d.at[i], recv_d.at[i], along_x[2 * i])

    for i in (0, 1):
        two[:, TOK * i : TOK * (i + 1)] = two_all[i]
        dy[:, TOK * i : TOK * (i + 1)] = dy_all[i]
    for i, half in enumerate(halves):
        for start, stop in ((half.start, half.start + 256), (half.start + 256, half.start + 512), (half.start + 512, half.stop)):
            gate = dot(wg[:, start:stop], two[...], 0, 0)
            up = dot(wu[:, start:stop], two[...], 0, 0)
            back = dot(wd[start:stop, :], dy[...], 1, 0)
            sigmoid = jax.nn.sigmoid(gate)
            silu = gate * sigmoid
            hidden[start:stop, :] = (silu * up).astype(BF)
            gate_grad[start:stop, :] = (back * up * sigmoid * (1.0 + gate * (1.0 - sigmoid))).astype(BF)
            up_grad[start:stop, :] = (back * silu).astype(BF)
        for start, stop in columns(D):
            part = dot(hidden[half, :], dy[start:stop, :], 1, 1).astype(BF)
            d[2 * i, :, start:stop] = part[:KW]
            d[2 * i + 1, :, start:stop] = part[KW:]
        d_block(2 * i)
        d_block(2 * i + 1)
        for source, into in ((gate_grad, c0), (up_grad, c1)):
            for start, stop in ((0, 256), (256, 512), (512, 640)):
                part = planes(dot(two[...], source[half.start + start : half.start + stop, :], 1, 1), nothing[stop - start])
                for f in range(8):
                    into[i, f // 4, f % 4, :, start:stop] = part[f]
            if into is c0:
                for j in ORDER:
                    c0_z(i, j).start()
            else:
                c1_x(i).start()
    far_half = pl.ds(TOK, TOK)
    for start, stop in columns(D):
        two_part[start:stop, :] = dot(wg[start:stop, :], gate_grad[...], 1, 0) + dot(wu[start:stop, :], up_grad[...], 1, 0)
    trade_two = remote(two_part.at[:, far_half], two_got, send_s.at[0], recv_s.at[0], sibling)
    trade_two.start()
    for start, stop in columns(D):
        down_part[start:stop, :] = dot(wd[:, start:stop], hidden[...], 0, 0)
    trade_down = remote(down_part.at[:, far_half], down_got, send_s.at[1], recv_s.at[1], sibling)
    trade_down.start()
    middle = mid[...]
    scale = lax.rsqrt(jnp.sum(middle * middle, axis=0, keepdims=True) / D + norm_epsilon)
    trade_two.wait_recv()
    normal = middle * scale
    incoming = two_part[:, :TOK] + two_got[...]
    gain_grad[...] = jnp.sum(incoming * normal, axis=1, keepdims=True)
    scaled = incoming * gains[1]
    level_two = jnp.sum(scaled * normal, axis=0, keepdims=True) / D
    mid_grad[...] = dy_all[0].astype(F32) + scale * (scaled - normal * level_two)
    mid_low[...] = mid_grad[...].astype(BF)
    for start, stop in columns(D):
        grad[start:stop, :] = dot(wo[start:stop, :], mid_low[...], 1, 0).astype(BF)
    trade_down.wait_recv()
    result[...] = (middle + down_part[:, :TOK] + down_got[...]).astype(BF)

    def step_c1():
        for i in (0, 1):
            c1_x(i).wait_recv()
            for k in range(4):
                c1s[i, k] = (c1[i, xl, k].astype(F32) + c1r[i, k].astype(F32)).astype(BF)
            for j in ORDER:
                (c1_z, c1_y)[i](j).start()

    def step_d():
        for j in (1, 2, 3):
            d_y(j).wait_recv()
        ds_[...] = summed(d[y], dr)

        @pl.when(jnp.logical_not(holds))
        def _():
            d_x(0).start()
            d_x(1).start()

    gap = lax.broadcasted_iota(jnp.int32, (TOK, TOK), 0) - lax.broadcasted_iota(jnp.int32, (TOK, TOK), 1)

    def group(g, carry):
        krows = pl.ds(pl.multiple_of(g * 64, 64), 64)
        vrows = pl.ds(pl.multiple_of(KW + g * 64, 64), 64)

        def head(t, inner):
            h = g * GROUP + t
            rows = pl.ds(pl.multiple_of(h * 64, 64), 64)
            qh, gh = q_low[rows, :], grad[rows, :]
            row_dot = jnp.sum(gh.astype(F32) * att[rows, :].astype(F32), axis=0, keepdims=True)
            level = lse[pl.ds(h, 1), 0, :]
            dq = jnp.zeros((64, TOK), F32)
            for j in range(4):
                s = dot(keys[j, krows, :], qh, 0, 0)
                s = jnp.where(gap <= 256 * (me - j), s, -1e30)
                p = jnp.exp(s - level)
                dp = dot(keys[j, vrows, :], gh, 0, 0)
                ds = (p * (dp - row_dot)).astype(BF)
                pb = p.astype(BF)
                dq += dot(keys[j, krows, :], ds, 1, 0)
                dk = dot(qh, ds, 1, 1)
                dv = dot(gh, pb, 1, 1)
                first = t == 0
                acc[j, 0] = jnp.where(first, dk, acc[j, 0] + dk)
                acc[j, 1] = jnp.where(first, dv, acc[j, 1] + dv)
            dq = dq * score_scale
            a, b = dq[:32], dq[32:]
            q_back[pl.ds(pl.multiple_of(h * 64, 32), 32), :] = (a * co + b * si).astype(BF)
            q_back[pl.ds(pl.multiple_of(h * 64 + 32, 32), 32), :] = (b * co - a * si).astype(BF)
            return inner

        lax.fori_loop(0, GROUP, head, 0)
        for j in range(4):
            mine[j, krows, :] = acc[j, 0].astype(BF)
            mine[j, vrows, :] = acc[j, 1].astype(BF)
        pl.when(g == 1)(step_c1)
        pl.when(g == 3)(step_d)
        return carry

    acc[...] = jnp.zeros_like(acc)
    lax.fori_loop(0, KEY_VALUE_HEADS, group, 0)
    to_sib_far = remote(mine.at[diag_slot], got.at[1], send.at[0], recv.at[0], sibling)
    to_sib = remote(mine.at[sib_slot], got.at[0], send.at[1], recv.at[1], sibling)
    to_sib_far.start()
    to_sib.start()
    to_sib_far.wait_recv()
    got[1] = (mine[far_slot].astype(F32) + got[1].astype(F32)).astype(BF)
    to_far = remote(got.at[1], far_got, send.at[2], recv.at[2], far)
    to_far.start()
    to_sib.wait_recv()

    @pl.when(holds)
    def _():
        for i in (0, 1):
            d_x(i).wait_recv()
            rows = slice(160 * i, 160 * (i + 1))
            d_out[rows, :] = (ds_[rows, :].astype(F32) + dt[i].astype(F32)).astype(BF)

    @pl.when(jnp.logical_not(holds))
    def _():
        d_out[...] = jnp.zeros_like(d_out)

    near = mine[me].astype(F32) + got[0].astype(F32)
    to_far.wait_recv()
    total = near + far_got[...].astype(F32)
    for h in range(KEY_VALUE_HEADS):
        a, b = total[64 * h : 64 * h + 32, :], total[64 * h + 32 : 64 * h + 64, :]
        kv_back[64 * h : 64 * h + 32, :] = (a * co + b * si).astype(BF)
        kv_back[64 * h + 32 : 64 * h + 64, :] = (b * co - a * si).astype(BF)
    kv_back[KW:, :] = total[KW:, :].astype(BF)
    for i, half in enumerate(halves):
        for j in (1, 2, 3):
            c0_z(i, j).wait_recv()
        for m in range(2):
            for k in range(4):
                c0_out[m, k, :, half] = summed(c0[i, m, k, quarter(z, 32)], [c0r[j, i, m, k] for j in range(3)])
    for j in (1, 2, 3):
        c1_z(j).wait_recv()
    for k in range(4):
        c1_out[k] = summed(c1s[0, k, quarter(z, 32)], [c1t[j, k] for j in range(3)])
    for j in (1, 2, 3):
        c1_y(j).wait_recv()
    c1y_out[...] = summed(c1s[1, y], c1u)

    trade_two.wait_send()
    trade_down.wait_send()
    to_sib_far.wait_send()
    to_sib.wait_send()
    to_far.wait_send()
    for j in (1, 2, 3):
        c0_z(0, j).wait_send()
        c0_z(1, j).wait_send()
        c1_z(j).wait_send()
        c1_y(j).wait_send()
        d_y(j).wait_send()
    for i in (0, 1):
        c1_x(i).wait_send()

    @pl.when(jnp.logical_not(holds))
    def _():
        d_x(0).wait_send()
        d_x(1).wait_send()


def backward(*args):
    sem = pltpu.SemaphoreType.DMA
    vm = lambda *shape: pltpu.VMEM(shape, BF)
    return pl.pallas_call(
        backward_kernel,
        name="backward",
        out_shape=(
            jax.ShapeDtypeStruct((D, TOK), BF),
            jax.ShapeDtypeStruct((2 * KW, TOK), BF),
            jax.ShapeDtypeStruct((2, 4, 32, FH), BF),
            jax.ShapeDtypeStruct((4, 32, 640), BF),
            jax.ShapeDtypeStruct((PAD, 640), BF),
            jax.ShapeDtypeStruct((KW, D), BF),
            jax.ShapeDtypeStruct((D, TOK), BF),
            jax.ShapeDtypeStruct((D, TOK), F32),
            jax.ShapeDtypeStruct((D, TOK), BF),
            jax.ShapeDtypeStruct((D, 1), F32),
        ),
        in_specs=[VM] * 14,
        out_specs=(VM,) * 10,
        scratch_shapes=[
            vm(D, 2 * TOK), vm(D, 2 * TOK), vm(FH, 2 * TOK), vm(FH, 2 * TOK), vm(FH, 2 * TOK), vm(D, TOK),
            pltpu.VMEM((D, 2 * TOK), F32), pltpu.VMEM((D, TOK), F32),
            pltpu.VMEM((D, 2 * TOK), F32), pltpu.VMEM((D, TOK), F32),
            sem((2,)), sem((2,)),
            vm(4, 2 * KW, TOK), vm(2, 2 * KW, TOK), vm(2 * KW, TOK), pltpu.VMEM((4, 2, 64, TOK), F32),
            vm(2, 2, 4, PAD, 640), vm(3, 2, 2, 4, 32, 640),
            vm(2, 2, 4, PAD, 640), vm(2, 4, PAD, 640), vm(2, 4, PAD, 640), vm(3, 4, 32, 640), vm(3, PAD, 640),
            vm(4, KW, D), vm(3, KW, D), vm(KW, D), vm(2, 160, D),
        ]
        + [sem((3,))] * 2
        + [sem((2, 3))] * 2
        + [sem((2,))] * 2
        + [sem((3,))] * 8,
        compiler_params=params(2, 61),
    )(*args)


WIDE, NARROW = 512, D - 512


def finish_kernel(
    one, att, mid, q_back, kv_back, c0, c1, c1y, dd, stream, mid_grad, gains, gain_two, wq, wk, wv,
    lo_sum, hi_sum, kv_sum, c0_sum, c1_sum, d_sum, in_grad,
    gain_cols,
    left, right, thin, both, lo, hi, kv,
    lo1, lo1r, lo2, lo2r, lo3, lo3r,
    kv1, kv1r, kv2, kv2r, kv3, kv3r,
    hi1, hi1r, hi2, hi2r, hi3, hi3r,
    c02r, c02, c03r, c03,
    c1r, c1zr, c1s, c1t, c1u,
    dr, dh, dx, ds_,
    send, recv, send_s, recv_s, send_g, recv_g, send_o, recv_o, local,
):
    x, y, z, c = place()
    xl = lax.rem(x, 2)
    holds = c == xl
    sibling = at(x, y, z, 1 - c)
    along_x, along_y, along_z = ring(x, y, z, c)
    greet(along_x + along_y + along_z + [sibling])
    LO, HI, KV, C0, C1, DN = range(6)

    def trade(i, src, dst):
        return remote(src, dst, send_s.at[i], recv_s.at[i], sibling)

    far = slice(TOK, 2 * TOK)

    def trades(core):
        return [
            trade(0, att if core == 0 else one, left.at[:, far]),
            trade(1, mid if core == 0 else q_back, right.at[:, far]),
            trade(2, kv_back.at[KW:] if core == 0 else kv_back.at[:KW], thin.at[:, far]),
            trade(3, one, both.at[:, far]),
        ]

    def move(item, phase, j, src, dst, along):
        return remote(src, dst.at[j - 1], send.at[item, phase, j - 1], recv.at[item, phase, j - 1], along[j - 1])

    def y1(item, j):
        return move(item, 0, j, lo.at[:, lax.rem(y + j, 4)], lo1r, along_y)

    def x2(item, j):
        return move(item, 1, j, lo1.at[xl if j == 2 else 1 - xl], lo2r, along_x)

    def z3(item, j):
        if item == DN:
            return move(item, 2, j, dd.at[quarter(z + j, 80)], dr, along_z)
        return move(item, 2, j, lo2.at[quarter(z + j, 32)], lo3r, along_z)

    def z1(item, j):
        src, dst = {HI: (hi, hi1r), KV: (kv, kv1r)}[item]
        return move(item, 0, j, src.at[:, :, quarter(z + j, 32)], dst, along_z)

    def y2(item, j):
        src, dst = {HI: (hi1, hi2r), KV: (kv1, kv2r), C0: (c0, c02r)}[item]
        return move(item, 1, j, src.at[:, lax.rem(y + j, 4)], dst, along_y)

    def x3(item, j):
        src, dst = {HI: (hi2, hi3r), KV: (kv2, kv3r), C0: (c02, c03r)}[item]
        return move(item, 2, j, src.at[xl if j == 2 else 1 - xl], dst, along_x)

    def y_up(j):
        return move(C1, 0, j, c1.at[lax.rem(y + j, 4)], c1r, along_y)

    def z_up(j):
        return move(C1, 2, j, c1y.at[quarter(z + j, 32)], c1zr, along_z)

    def x_up():
        return remote(c1s, c1t, send.at[C1, 1, 0], recv.at[C1, 1, 0], along_x[1])

    def x_down():
        return remote(dh, dx, send.at[DN, 1, 0], recv.at[DN, 1, 0], along_x[1])

    for core in (0, 1):

        @pl.when(c == core)
        def _(core=core):
            for copy in trades(core):
                copy.start()

    for j in ORDER:
        y2(C0, j).start()
        y_up(j).start()
        z_up(j).start()

    @pl.when(holds)
    def _():
        for j in ORDER:
            z3(DN, j).start()

    near = slice(0, TOK)

    @pl.when(c == 0)
    def _():
        left[:, near] = one[...]
        right[:, near] = q_back[...]
        thin[:, near] = kv_back[:KW, :]

    @pl.when(c == 1)
    def _():
        left[:, near] = att[...]
        right[:, near] = mid[...]
        thin[:, near] = kv_back[KW:, :]

    both[:, near] = one[...]

    trade(0, one, left.at[:, far]).wait_recv()
    trade(1, one, right.at[:, far]).wait_recv()

    def wide_part(start, stop, into, shift, extra):
        part = planes(dot(left[...], right[start:stop, :], 1, 1), extra)
        for f in range(8):
            into[f // 4, f % 4, :, start - shift : stop - shift] = part[f]

    nothing = [jnp.zeros((8, 256), F32)] * 8
    wide_part(0, 256, lo, 0, nothing)
    wide_part(256, 512, lo, 0, nothing)
    for j in ORDER:
        y1(LO, j).start()
    trade(3, one, both.at[:, far]).wait_recv()
    trade(2, kv_back.at[:KW], thin.at[:, far]).wait_recv()
    part = planes(dot(both[...], thin[...], 1, 1), [jnp.zeros((8, KW), F32)] * 8)
    for f in range(8):
        kv[f // 4, f % 4] = part[f]
    for j in ORDER:
        z1(KV, j).start()
    wide_part(768, D, hi, WIDE, [jnp.zeros((8, D - 768), F32)] * 8)

    source = stream[...].astype(F32)
    scale = lax.rsqrt(jnp.sum(source * source, axis=0, keepdims=True) / D + norm_epsilon)
    normal = source * scale
    for start, stop in columns(D):
        in_grad[start:stop, :] = (
            dot(wq[start:stop, :], q_back[...], 1, 0)
            + dot(wk[start:stop, :], kv_back[:KW, :], 1, 0)
            + dot(wv[start:stop, :], kv_back[KW:, :], 1, 0)
        )
    incoming = in_grad[...]
    gain_cols[...] = jnp.sum(incoming * normal, axis=1, keepdims=True)
    scaled = incoming * gains[0]
    level = jnp.sum(scaled * normal, axis=0, keepdims=True) / D
    in_grad[...] = mid_grad[...] + scale * (scaled - normal * level)
    lane = lax.broadcasted_iota(jnp.int32, (PAD, 128), 1)
    gain = []
    for f in range(8):
        rows_f = slice(ROWS * f, ROWS * (f + 1))
        zeros = jnp.zeros((PAD - ROWS, 128), F32)
        first_col = jnp.concatenate([jnp.broadcast_to(gain_cols[rows_f, :], (ROWS, 128)), zeros], axis=0)
        second_col = jnp.concatenate([jnp.broadcast_to(gain_two[rows_f, :], (ROWS, 128)), zeros], axis=0)
        tile = jnp.where(lane == 0, first_col, jnp.where(lane == 1, second_col, 0.0)).T
        gain.append(jnp.concatenate([tile[:8], jnp.zeros((8, 128), F32)], axis=1))

    wide_part(512, 768, hi, WIDE, gain)
    for j in ORDER:
        z1(HI, j).start()

    def arrived(make, *key):
        for j in (1, 2, 3):
            make(*key, j).wait_recv()

    arrived(y2, C0)
    for i in range(2):
        c02[i] = summed(c0[i, y], [c02r[j, i] for j in range(3)])
    for j in ORDER:
        x3(C0, j).start()
    arrived(y_up)
    c1s[:, 0:640] = summed(c1[y], c1r)
    arrived(z_up)
    c1s[:, 640:FH] = summed(c1y[quarter(z, 32)], c1zr)
    x_up().start()

    part_of = {LO: lo3, HI: hi3, KV: kv3, C0: c03, C1: c1u, DN: ds_}

    def place_of(item, index, core):
        if item == DN:
            return d_sum.at[quarter(index, 80)]
        if item in (C0, C1):
            lanes = pl.ds(pl.multiple_of(FH * core, 128), FH)
            return (c0_sum if item == C0 else c1_sum).at[quarter(index, 32), lanes]
        return {LO: lo_sum, HI: hi_sum, KV: kv_sum}[item].at[core, quarter(index, 32)]

    def spread(item, j):
        return remote(
            part_of[item], place_of(item, z, c), send_g.at[item, j - 1], recv_g.at[item, j - 1], along_z[j - 1]
        )

    def keep(item):
        return pltpu.make_async_copy(part_of[item], place_of(item, z, c), local.at[item])

    def across(item, k):
        index = lax.rem(z + 4 - k, 4)
        src = part_of[item] if k == 0 else place_of(item, index, c)
        return remote(src, place_of(item, index, c), send_o.at[item, k], recv_o.at[item, k], sibling)

    def publish(item):
        keep(item).start()
        for j in ORDER:
            spread(item, j).start()
        across(item, 0).start()

    def landed(item, j):
        ref = place_of(item, lax.rem(z + 4 - j, 4), c)
        remote(ref, ref, send_g.at[item, j - 1], recv_g.at[item, j - 1], sibling).wait_recv()

    def collect(item):
        for j in ORDER:
            landed(item, j)
            across(item, j).start()

    def arrive(item):
        for k in range(4):
            ref = place_of(item, lax.rem(z + 4 - k, 4), 1 - c)
            remote(ref, ref, send_o.at[item, k], recv_o.at[item, k], sibling).wait_recv()

    @pl.when(holds)
    def _():
        arrived(z3, DN)
        dh[...] = summed(dd[quarter(z, 80)], dr)
        x_down().start()

    @pl.when(holds)
    def _():
        x_down().wait_recv()
        ds_[...] = (dh[...].astype(F32) + dx[...].astype(F32)).astype(BF)
        publish(DN)

    x_up().wait_recv()
    c1u[...] = (c1s[...].astype(F32) + c1t[...].astype(F32)).astype(BF)
    publish(C1)
    arrived(x3, C0)
    c03[...] = summed(c02[xl], c03r)
    publish(C0)

    arrived(y1, LO)
    for i in range(2):
        lo1[i] = summed(lo[i, y], [lo1r[j, i] for j in range(3)])
    for j in ORDER:
        x2(LO, j).start()
    for item, first, out, got in ((KV, kv, kv1, kv1r), (HI, hi, hi1, hi1r)):
        arrived(z1, item)
        for i in range(2):
            for k in range(4):
                out[i, k] = summed(first[i, k, quarter(z, 32)], [got[j, i, k] for j in range(3)])
        for j in ORDER:
            y2(item, j).start()
    arrived(x2, LO)
    lo2[...] = summed(lo1[xl], lo2r)
    for j in ORDER:
        z3(LO, j).start()
    for item, first, out, got in ((KV, kv1, kv2, kv2r), (HI, hi1, hi2, hi2r)):
        arrived(y2, item)
        for i in range(2):
            out[i] = summed(first[i, y], [got[j, i] for j in range(3)])
        for j in ORDER:
            x3(item, j).start()
    arrived(z3, LO)
    lo3[...] = summed(lo2[quarter(z, 32)], lo3r)
    publish(LO)
    arrived(x3, KV)
    kv3[...] = summed(kv2[xl], kv3r)
    publish(KV)
    arrived(x3, HI)
    hi3[...] = summed(hi2[xl], hi3r)
    publish(HI)

    pl.when(holds)(lambda: collect(DN))
    for item in (C1, C0, KV, LO, HI):
        collect(item)
    pl.when(jnp.logical_not(holds))(lambda: arrive(DN))
    for item in (C1, C0, KV, LO, HI):
        arrive(item)

    for core in (0, 1):

        @pl.when(c == core)
        def _(core=core):
            for copy in trades(core):
                copy.wait_send()

    def settled(item):
        keep(item).wait()
        for j in (1, 2, 3):
            spread(item, j).wait_send()
        for k in range(4):
            across(item, k).wait_send()

    for j in (1, 2, 3):
        for make, key in (
            (y1, LO), (x2, LO), (z3, LO), (z1, KV), (y2, KV), (x3, KV), (z1, HI), (y2, HI), (x3, HI), (y2, C0), (x3, C0),
        ):
            make(key, j).wait_send()
        y_up(j).wait_send()
        z_up(j).wait_send()
    x_up().wait_send()
    for item in (LO, HI, KV, C0, C1):
        settled(item)

    @pl.when(holds)
    def _():
        for j in (1, 2, 3):
            z3(DN, j).wait_send()
        x_down().wait_send()
        settled(DN)


def finish(*args):
    sem = pltpu.SemaphoreType.DMA
    vm = lambda *shape: pltpu.VMEM(shape, BF)

    def yxz(width):
        return [
            vm(2, PAD, width), vm(3, 2, PAD, width), vm(PAD, width), vm(3, PAD, width),
            vm(32, width), vm(3, 32, width),
        ]

    def zyx(width):
        return [
            vm(2, 4, 32, width), vm(3, 2, 4, 32, width), vm(2, 32, width), vm(3, 2, 32, width),
            vm(32, width), vm(3, 32, width),
        ]

    return pl.pallas_call(
        finish_kernel,
        name="finish",
        out_shape=(
            jax.ShapeDtypeStruct((2, PAD, WIDE), BF),
            jax.ShapeDtypeStruct((2, PAD, NARROW), BF),
            jax.ShapeDtypeStruct((2, PAD, KW), BF),
            jax.ShapeDtypeStruct((PAD, FF), BF),
            jax.ShapeDtypeStruct((PAD, FF), BF),
            jax.ShapeDtypeStruct((KW, D), BF),
            jax.ShapeDtypeStruct((D, TOK), F32),
        ),
        in_specs=[VM] * 16,
        out_specs=(ANY,) * 6 + (VM,),
        scratch_shapes=[
            pltpu.VMEM((D, 1), F32),
            vm(D, 2 * TOK), vm(D, 2 * TOK), vm(KW, 2 * TOK), vm(D, 2 * TOK),
            vm(2, 4, PAD, WIDE), vm(2, 4, PAD, NARROW), vm(2, 4, PAD, KW),
        ]
        + yxz(WIDE)
        + zyx(KW)
        + zyx(NARROW)
        + [vm(3, 2, 32, FH), vm(2, 32, FH), vm(3, 32, FH), vm(32, FH)]
        + [vm(3, 32, 640), vm(3, 32, 640), vm(32, FH), vm(32, FH), vm(32, FH)]
        + [vm(3, 80, D), vm(80, D), vm(80, D), vm(80, D)]
        + [sem((6, 3, 3)), sem((6, 3, 3)), sem((4,)), sem((4,)), sem((6, 3)), sem((6, 3)), sem((6, 4)), sem((6, 4)), sem((6,))],
        compiler_params=params(3),
    )(*args)


def adamw_update(weight, gradient, first, second, rate, decay):
    weight = weight.astype(F32)
    first_new = beta_first * first.astype(F32) + (1.0 - beta_first) * gradient
    second_new = beta_second * second.astype(F32) + (1.0 - beta_second) * gradient * gradient
    first_hat = first_new * (rate / (1.0 - beta_first**STEP))
    second_hat = second_new * (1.0 / (1.0 - beta_second**STEP))
    weight_new = weight * (1.0 - rate * decay) - first_hat / (jnp.sqrt(second_hat) + adam_epsilon)
    return (weight_new, first_new, second_new)


def update_kernel(lo, hi, narrow, gate, up, down, *refs):
    state, new = refs[:18], refs[18:]

    def update(which, index, gradient, rate=matrix_rate, decay=matrix_decay):
        weight, first, second = (state[3 * which + i][index] for i in range(3))
        for i, value in enumerate(adamw_update(weight, gradient, first, second, rate, decay)):
            new[3 * which + i][index] = value

    for m, source in ((0, gate), (1, up)):
        update(3, m, source[...].astype(F32)[:ROWS])
    update(4, slice(None), down[...].astype(F32))

    @pl.when(pl.program_id(0) == 0)
    def _():
        for which, core in ((0, 0), (2, 1)):
            update(which, (slice(None), slice(0, WIDE)), lo[core].astype(F32)[:ROWS])
            update(which, (slice(None), slice(WIDE, D)), hi[core].astype(F32)[:ROWS])
        for m in (0, 1):
            update(1, m, narrow[m].astype(F32).T[:, :ROWS])
        gains = hi[0, 112:, :128].astype(F32) + hi[1, 112:, :128].astype(F32)
        update(5, slice(None), gains[8:10, :ROWS], gain_rate, 0.0)


def update_all(lo, hi, narrow, gate, up, down, state):
    steps = 5
    fixed = lambda a: pl.BlockSpec(a.shape, lambda i: (0,) * len(a.shape))
    sums = pl.BlockSpec((PAD, FF // steps), lambda i: (0, i))
    rows = pl.BlockSpec((KW // steps, D), lambda i: (i, 0))
    wide = pl.BlockSpec((2, ROWS, FF // steps), lambda i: (0, 0, i))
    specs = []
    for i, array in enumerate(state):
        specs.append(wide if i // 3 == 3 else rows if i // 3 == 4 else fixed(array))
    return pl.pallas_call(
        update_kernel,
        name="update",
        grid=(steps,),
        out_shape=tuple(jax.ShapeDtypeStruct(a.shape, F32) for a in state),
        in_specs=[fixed(lo), fixed(hi), fixed(narrow), sums, sums, rows] + specs,
        out_specs=tuple(specs),
        compiler_params=pltpu.CompilerParams(vmem_limit_bytes=62 * 2**20),
    )(lo, hi, narrow, gate, up, down, *state)


def body(
    tokens,
    cotangent,
    query_weight,
    keyval_weight,
    output_weight,
    gateup_weight,
    down_weight,
    norm_gains,
    query_first,
    keyval_first,
    output_first,
    gateup_first,
    down_first,
    gains_first,
    query_second,
    keyval_second,
    output_second,
    gateup_second,
    down_second,
    gains_second,
):
    ctx = lax.axis_index("ctx")
    core = lax.rem(ctx, 2)
    stream_t, dy_t = tokens[0].T, cotangent[0].T
    positions = (ctx * TOK + jnp.arange(TOK, dtype=jnp.int32)).astype(F32)
    counter = jnp.arange(HALF, dtype=F32)
    frequency = 1.0 / rotary_base ** (counter * (2.0 / HEAD_WIDTH))
    angles = frequency[:, None] * positions[None, :]
    cosine, sine = jnp.cos(angles), jnp.sin(angles)

    (
        query_low, attended_t, level, keys, one_t, middle_t, two_all, dy_all, gains,
        query_all, output_all, key_all, value_all, gate_all, up_all, dn_all,
    ) = forward(
        stream_t, cosine, sine, keyval_weight.transpose(0, 2, 1), norm_gains, query_weight, output_weight, dy_t,
        gateup_weight, down_weight,
    )
    query_full, output_full = query_all.reshape(D, D), output_all.reshape(D, D)
    key_full, value_full = key_all.reshape(D, KW), value_all.reshape(D, KW)
    gate_full, up_full = gate_all.reshape(D, FH), up_all.reshape(D, FH)
    down_full = dn_all.reshape(FH, D)

    (
        query_back, keyval_back, gate_part, up_part, up_row, down_sum, result_t, middle_grad, middle_low, gain_two_grad,
    ) = backward(
        query_low, keys, level, attended_t, cosine, sine, two_all, dy_all, middle_t, gains,
        gate_full, up_full, down_full, output_full,
    )
    low, high, narrow, gate_sum, up_sum, down, input_grad = finish(
        one_t, attended_t, middle_low, query_back, keyval_back, gate_part, up_part, up_row, down_sum,
        stream_t, middle_grad, gains, gain_two_grad, query_full, key_full, value_full,
    )
    turned = lambda a: a.transpose(0, 2, 1)
    state = (
        query_weight, query_first, query_second,
        turned(keyval_weight), turned(keyval_first), turned(keyval_second),
        output_weight, output_first, output_second,
        gateup_weight, gateup_first, gateup_second,
        down_weight, down_first, down_second,
        norm_gains, gains_first, gains_second,
    )
    new = list(update_all(low, high, narrow, gate_sum, up_sum, down, state))
    new[3:6] = [turned(a) for a in new[3:6]]
    return (result_t.T[None], input_grad.T[None], *new[0::3], *new[1::3], *new[2::3])


def solution(mesh):
    row, mid = P("fsdp", None), P(None, "fsdp", None)
    weights = (row, mid, row, mid, row, P(None, "fsdp"))
    stream = P(("rep", "fsdp"), "ctx", None)
    return jax.shard_map(
        body,
        mesh=mesh,
        in_specs=(stream, stream) + weights * 3,
        out_specs=(stream, stream) + weights * 3,
        check_vma=False,
    )
```
